32 devices in a mesh: fsdp: 32 (over z, y, x, core).
Axes of the slice: x: 2, y: 2, z: 4, core: 2. Of those that a mesh axis runs over, the one named last changes fastest.
Arguments:
- latents: bfloat16 [64, 256, 16], P('fsdp'), may hold values from -6 to 6
- noise_draw: bfloat16 [64, 256, 16], P('fsdp'), may hold values from -6 to 6
- timesteps: int32 [64], P('fsdp'), may hold values from 0 to 999
- labels: int32 [64], P('fsdp'), may hold values from 0 to 999
- weights_in: float32 [1024, 17408], P('fsdp'), may hold values from -2 to 2, as said below
- weights_down: float32 [4096, 1024], P('fsdp'), may hold values from -0.09375 to 0.09375
- weights_side: float32 [1024, 1288], P('fsdp'), may hold values from -4 to 4, as said below
- biases: float32 [19456], P('fsdp'), may hold values from -1 to 1
- first_in: float32 [1024, 17408], P('fsdp'), may hold values from -24 to 24
- first_down: float32 [4096, 1024], P('fsdp'), may hold values from -24 to 24
- first_side: float32 [1024, 1288], P('fsdp'), may hold values from -24 to 24
- first_bias: float32 [19456], P('fsdp'), may hold values from -24 to 24
- second_in: float32 [1024, 17408], P('fsdp'), may hold values from 14.0625 to 56.25
- second_down: float32 [4096, 1024], P('fsdp'), may hold values from 14.0625 to 56.25
- second_side: float32 [1024, 1288], P('fsdp'), may hold values from 14.0625 to 56.25
- second_bias: float32 [19456], P('fsdp'), may hold values from 14.0625 to 56.25
Outputs:
- loss_sum: float32 [], replicated
- updated_in: float32 [1024, 17408], P('fsdp')
- updated_down: float32 [4096, 1024], P('fsdp')
- updated_side: float32 [1024, 1288], P('fsdp')
- updated_bias: float32 [19456], P('fsdp')
- first_in_new: float32 [1024, 17408], P('fsdp')
- first_down_new: float32 [4096, 1024], P('fsdp')
- first_side_new: float32 [1024, 1288], P('fsdp')
- first_bias_new: float32 [19456], P('fsdp')
- second_in_new: float32 [1024, 17408], P('fsdp')
- second_down_new: float32 [4096, 1024], P('fsdp')
- second_side_new: float32 [1024, 1288], P('fsdp')
- second_bias_new: float32 [19456], P('fsdp')
- trust_ratios: float32 [12], replicated
- weight_norms: float32 [12], replicated
- update_norms: float32 [12], replicated
The draws below stay inside these ranges and needn't reach their ends.
Inputs may be any that keep to these rules, and one draw needn't show every extreme that they name: `weights_in`: weights of order one over the root of their fan-in; the attention output columns W_out max(sqrt(256) / 2, 1) times larger. `weights_side`: weights of order one over the root of their fan-in, class embeddings of order one.
All inputs are finite; a program needn't handle non-finite values.
Results may differ from the reference program's by a relative error of at most 0.0083.
The reference program's roundings to bfloat16 on the way count: a program that leaves them out, or rounds other values in their place, can miss the bound.
Values may be sent and summed in bfloat16 or wider, within the bound.
No kernel may reach another device: no remote copies, remote signals or barrier semaphores. Data moves between devices by JAX's collectives and lax.ppermute only.
A program may use at most 512 MiB of HBM per device.

```python
import math
import jax
import jax.numpy as jnp
from jax import lax

D = 1024
HEADS = 16
HEAD_DIM = 64
FF = 4096
CLASSES = 1000
PATCH_FEAT = 16
TFREQ = 256
GRID = 16
TOK = 256
MICRO = 2
STEP = 10
IMG_DEV = 1
IMAGES = 64
COLS = 17408
SIDE = 1288
BIASES = 19456
N_FSDP = 32


def draw_weights_in(key, part):
    key = jax.random.fold_in(key, 11)
    values = jax.random.truncated_normal(key, -4.0, 4.0, (D, COLS), jnp.float32)
    columns = jnp.arange(COLS, dtype=jnp.int32)
    base = D ** (-0.5)
    boost = max(TOK ** 0.5 / 2.0, 1.0)
    scale = jnp.where((columns >= 3 * D) & (columns < 4 * D), base * boost, base)
    return values * scale[None, :]


def draw_weights_side(key, part):
    key = jax.random.fold_in(key, 23)
    values = jax.random.truncated_normal(key, -4.0, 4.0, (D, SIDE), jnp.float32)
    columns = jnp.arange(SIDE, dtype=jnp.int32)
    scale = jnp.where(columns < TFREQ, TFREQ ** (-0.5), jnp.where(columns < TFREQ + PATCH_FEAT, PATCH_FEAT ** (-0.5), jnp.where(columns < TFREQ + PATCH_FEAT + CLASSES, 1.0, D ** (-0.5))))
    return values * scale[None, :]


def touch_ends(entries, own_key, smallest, largest):
    spot = [jax.random.randint(jax.random.fold_in(own_key, axis), (), 0, length) for axis, length in enumerate(entries.shape)]
    longest = entries.shape.index(max(entries.shape))
    neighbour = spot[:longest] + [(spot[longest] + 1) % entries.shape[longest]] + spot[longest + 1:]
    return entries.at[tuple(spot)].set(smallest).at[tuple(neighbour)].set(largest)


def block_scale(key, shape, cuts, least, high):
    factor_of, own = 1.0, jax.random.fold_in(key, 6)
    for dim, shards_of in cuts:
        steps = jnp.exp(jax.random.uniform(jax.random.fold_in(own, dim), (shards_of,), jnp.float32, least / len(cuts), high / len(cuts)))
        factor_of = factor_of * jnp.repeat(steps, shape[dim] // shards_of).reshape([-1 if axis == dim else 1 for axis in range(len(shape))])
    return factor_of


def bell_draw(own_key, extent, width, most, pieces=(), kind=jnp.bfloat16):
    entries = jax.random.normal(own_key, extent, jnp.float32) * width
    if len(pieces) > 0:
        entries = block_scale(own_key, extent, pieces, -0.22, 0.18) * entries
    return jnp.clip(entries, min=-most, max=most).astype(kind)


def setup_inputs(seed: int = 0) -> dict:
    keys = jax.random.split(jax.random.key(seed), 17)
    return {
        "latents": bell_draw(keys[0], (IMAGES, TOK, PATCH_FEAT), 1.0, 6.0, ((0, 32),)),
        "noise_draw": bell_draw(keys[1], (IMAGES, TOK, PATCH_FEAT), 1.0, 6.0, ((0, 32),)),
        "timesteps": touch_ends(jax.random.randint(keys[2], (IMAGES,), 0, 1000), jax.random.fold_in(keys[2], 1), 0, 999).astype(jnp.int32),
        "labels": touch_ends(jax.random.randint(keys[3], (IMAGES,), 0, CLASSES), jax.random.fold_in(keys[3], 1), 0, CLASSES - 1).astype(jnp.int32),
        "weights_in": draw_weights_in(jax.random.fold_in(keys[16], 71), 0),
        "weights_down": bell_draw(keys[5], (FF, D), FF ** -0.5, 0.09375, ((0, 32),), jnp.float32),
        "weights_side": draw_weights_side(jax.random.fold_in(keys[16], 71), 0),
        "biases": bell_draw(keys[7], (BIASES,), 0.2, 1.0, ((0, 32),), jnp.float32),
        "first_in": bell_draw(keys[8], (D, COLS), (30 / (IMG_DEV * MICRO * N_FSDP) ** 0.5), 24.0, ((0, 32),), jnp.float32),
        "first_down": bell_draw(keys[9], (FF, D), (30 / (IMG_DEV * MICRO * N_FSDP) ** 0.5), 24.0, ((0, 32),), jnp.float32),
        "first_side": bell_draw(keys[10], (D, SIDE), (30 / (IMG_DEV * MICRO * N_FSDP) ** 0.5), 24.0, ((0, 32),), jnp.float32),
        "first_bias": bell_draw(keys[11], (BIASES,), (30 / (IMG_DEV * MICRO * N_FSDP) ** 0.5), 24.0, ((0, 32),), jnp.float32),
        "second_in": jnp.clip(jnp.exp(math.log(56.25) - 1.3862944 * jax.random.uniform(keys[12], (D, COLS), jnp.float32) ** block_scale(keys[12], (D, COLS), ((0, 32),), -0.2, 0.2)), 14.0625, 56.25),
        "second_down": jnp.clip(jnp.exp(math.log(56.25) - 1.3862944 * jax.random.uniform(keys[13], (FF, D), jnp.float32) ** block_scale(keys[13], (FF, D), ((0, 32),), -0.2, 0.2)), 14.0625, 56.25),
        "second_side": jnp.clip(jnp.exp(math.log(56.25) - 1.3862944 * jax.random.uniform(keys[14], (D, SIDE), jnp.float32) ** block_scale(keys[14], (D, SIDE), ((0, 32),), -0.2, 0.2)), 14.0625, 56.25),
        "second_bias": jnp.clip(jnp.exp(math.log(56.25) - 1.3862944 * jax.random.uniform(keys[15], (BIASES,), jnp.float32) ** block_scale(keys[15], (BIASES,), ((0, 32),), -0.2, 0.2)), 14.0625, 56.25),
    }


BETA_ONE = 0.5
BETA_TWO = 0.5
EPSILON = 1e-06
DECAY = 0.01
RATE = 0.25
NORM_EPS = 1e-06

@jax.custom_vjp
def low(v):
    return lax.optimization_barrier(v.astype(jnp.bfloat16)).astype(jnp.float32)

@jax.custom_vjp
def low_back(v):
    return v

def low_keep(v):
    return (low(v), None)

def low_pass(kept, grad):
    return (grad,)

def back_keep(v):
    return (v, None)

def back_low(kept, grad):
    return (low(grad),)
low.defvjp(low_keep, low_pass)
low_back.defvjp(back_keep, back_low)

def matmul(left, right):
    return jnp.dot(left, right, precision=lax.Precision.HIGHEST, preferred_element_type=jnp.float32)

def layer_norm(values):
    center = values - lax.optimization_barrier(jnp.mean(values, axis=-1, keepdims=True))
    return center * lax.rsqrt(lax.optimization_barrier(jnp.mean(center * center, axis=-1, keepdims=True)) + NORM_EPS)

def modulate(values, shift, scale):
    return layer_norm(values) * (1.0 + scale[:, None, :]) + shift[:, None, :]

def noise_scales(steps_part):
    phase = (steps_part.astype(jnp.float32) / 1000.0 + 0.008) / 1.008 * (math.pi / 2.0)
    signal = jnp.cos(phase) * jnp.cos(phase)
    return (jnp.sqrt(signal), jnp.sqrt(1.0 - signal))

def time_features(steps_part):
    half_width = TFREQ // 2
    freqs = jnp.exp(-math.log(10000.0) * jnp.arange(half_width, dtype=jnp.float32) / half_width)
    angles = steps_part.astype(jnp.float32)[:, None] * freqs[None, :]
    return jnp.concatenate([jnp.cos(angles), jnp.sin(angles)], axis=1)

def positions():
    quarter = D // 4
    omega = 1.0 / 10000.0 ** (jnp.arange(quarter, dtype=jnp.float32) / quarter)
    cells = jnp.arange(TOK, dtype=jnp.int32)
    row_pos = (cells // GRID).astype(jnp.float32)[:, None] * omega[None, :]
    col_pos = (cells % GRID).astype(jnp.float32)[:, None] * omega[None, :]
    return jnp.concatenate([jnp.sin(row_pos), jnp.cos(row_pos), jnp.sin(col_pos), jnp.cos(col_pos)], axis=1)

def column_blocks():
    return [(0, 0, 3 * D), (0, 3 * D, 4 * D), (0, 4 * D, 4 * D + FF), (0, 4 * D + FF, 10 * D + FF), (0, 10 * D + FF, 12 * D + FF), (0, 12 * D + FF, 13 * D + FF), (1, 0, 0), (2, 0, TFREQ), (2, TFREQ, TFREQ + PATCH_FEAT), (2, TFREQ + PATCH_FEAT, TFREQ + PATCH_FEAT + CLASSES), (2, TFREQ + PATCH_FEAT + CLASSES, SIDE), (3, 0, 0)]

def block_squares(arrays):
    totals = []
    for kind, start, stop in column_blocks():
        if kind in (0, 2):
            piece = arrays[kind][:, start:stop]
        else:
            piece = arrays[kind]
        totals.append(jnp.sum(piece * piece))
    return jnp.stack(totals)

def block_factors(trust):
    rows_in, rows_side = ([], [])
    for index, (kind, start, stop) in enumerate(column_blocks()):
        if kind == 0:
            rows_in.append(jnp.full((stop - start,), trust[index], jnp.float32))
        if kind == 2:
            rows_side.append(jnp.full((stop - start,), trust[index], jnp.float32))
    return (jnp.concatenate(rows_in)[None, :], trust[6], jnp.concatenate(rows_side)[None, :], trust[11])

def adam_direction(weight, grad, first, second):
    first_new = BETA_ONE * first + (1.0 - BETA_ONE) * grad
    second_new = BETA_TWO * second + (1.0 - BETA_TWO) * grad * grad
    direction = first_new / (1.0 - BETA_ONE ** STEP) / (jnp.sqrt(second_new / (1.0 - BETA_TWO ** STEP)) + EPSILON) + DECAY * weight
    return (first_new, second_new, direction)

def image_loss(params, latent, noise_part, steps_part, label_part):
    weights_in, weights_down, weights_side, biases = params
    count = latent.shape[0]
    rows_all = count * TOK
    w_qkv = weights_in[:, :3 * D]
    w_out = weights_in[:, 3 * D:4 * D]
    w_up = weights_in[:, 4 * D:4 * D + FF]
    w_mod = weights_in[:, 4 * D + FF:10 * D + FF]
    w_final = weights_in[:, 10 * D + FF:12 * D + FF]
    w_time = weights_in[:, 12 * D + FF:]
    t_first = weights_side[:, :TFREQ]
    w_patch = weights_side[:, TFREQ:TFREQ + PATCH_FEAT]
    w_class = weights_side[:, TFREQ + PATCH_FEAT:TFREQ + PATCH_FEAT + CLASSES]
    w_head = weights_side[:, TFREQ + PATCH_FEAT + CLASSES:]
    b_query = biases[:D]
    b_value = biases[D:2 * D]
    b_out = biases[2 * D:3 * D]
    b_up = biases[3 * D:3 * D + FF]
    b_down = biases[3 * D + FF:4 * D + FF]
    b_mod = biases[4 * D + FF:10 * D + FF]
    b_final = biases[10 * D + FF:12 * D + FF]
    b_tfirst = biases[12 * D + FF:13 * D + FF]
    b_time = biases[13 * D + FF:14 * D + FF]
    b_patch = biases[14 * D + FF:]
    signal, spread = noise_scales(steps_part)
    noisy = low(signal[:, None, None] * latent + spread[:, None, None] * noise_part).reshape(rows_all, PATCH_FEAT)
    hidden = low_back(matmul(noisy, w_patch.T)) + b_patch + jnp.tile(positions(), (count, 1))
    feats = low(time_features(steps_part))
    time_act = low(jax.nn.silu(low_back(matmul(feats, t_first.T)) + b_tfirst))
    onehot = (label_part[:, None] == jnp.arange(CLASSES, dtype=jnp.int32)[None, :]).astype(jnp.float32)
    cond = low_back(matmul(time_act, w_time)) + b_time + matmul(onehot, w_class.T)
    cond_act = low(jax.nn.silu(cond))
    mods = low_back(matmul(cond_act, w_mod)) + b_mod
    finals = low_back(matmul(cond_act, w_final)) + b_final
    resid = hidden.reshape(count, TOK, D)
    normed = low(modulate(resid, mods[:, :D], mods[:, D:2 * D])).reshape(rows_all, D)
    proj = low_back(matmul(normed, w_qkv))
    head_shape = (count, TOK, HEADS, HEAD_DIM)
    queries = low(proj[:, :D] + b_query).reshape(head_shape)
    keys_all = low(proj[:, D:2 * D]).reshape(head_shape)
    values_all = low(proj[:, 2 * D:] + b_value).reshape(head_shape)
    scores = jnp.einsum('bqhd,bkhd->bhqk', queries, keys_all, precision=lax.Precision.HIGHEST)
    scores = low_back(scores * HEAD_DIM ** (-0.5))
    probs = low(jax.nn.softmax(scores, axis=-1))
    mixed = jnp.einsum('bhqk,bkhd->bqhd', probs, values_all, precision=lax.Precision.HIGHEST)
    mixed = low_back(low(mixed)).reshape(rows_all, D)
    attended = low_back(matmul(mixed, w_out)) + b_out
    resid = resid + mods[:, 2 * D:3 * D][:, None, :] * attended.reshape(count, TOK, D)
    normed = low(modulate(resid, mods[:, 3 * D:4 * D], mods[:, 4 * D:5 * D])).reshape(rows_all, D)
    active = low(jax.nn.gelu(low_back(matmul(normed, w_up)) + b_up, approximate=True))
    lowered = low_back(matmul(active, weights_down)) + b_down
    resid = resid + mods[:, 5 * D:][:, None, :] * lowered.reshape(count, TOK, D)
    normed = low(modulate(resid, finals[:, :D], finals[:, D:])).reshape(rows_all, D)
    predicted = low_back(matmul(normed, w_head))
    error = predicted - noise_part.reshape(rows_all, PATCH_FEAT)
    return jnp.sum(error * error)

def reference(latents, noise_draw, timesteps, labels, weights_in, weights_down, weights_side, biases, first_in, first_down, first_side, first_bias, second_in, second_down, second_side, second_bias):
    masters = (weights_in, weights_down, weights_side, biases)
    per_group = IMG_DEV * MICRO
    groups = IMAGES // per_group
    batches = (latents.astype(jnp.float32).reshape(groups, per_group, TOK, PATCH_FEAT), noise_draw.astype(jnp.float32).reshape(groups, per_group, TOK, PATCH_FEAT), timesteps.reshape(groups, per_group), labels.reshape(groups, per_group))

    def total_loss(params):
        rounded = tuple((low(item) for item in params))

        def one_group(carry, batch):
            part_loss = jax.checkpoint(image_loss)(rounded, batch[0], batch[1], batch[2], batch[3])
            return (carry + part_loss, None)
        total, _ = lax.scan(one_group, jnp.zeros((), jnp.float32), batches)
        return (total / IMAGES, total)
    _, pull, loss_sum = jax.vjp(total_loss, masters, has_aux=True)
    grads = pull(jnp.ones((), jnp.float32))[0]
    firsts = (first_in, first_down, first_side, first_bias)
    seconds = (second_in, second_down, second_side, second_bias)
    results = [adam_direction(masters[index], grads[index], firsts[index], seconds[index]) for index in range(4)]
    directions = [item[2] for item in results]
    weight_norms = jnp.sqrt(block_squares(masters))
    update_norms = jnp.sqrt(block_squares(directions))
    trust = weight_norms / update_norms
    factors = block_factors(trust)
    updated = [masters[index] - RATE * factors[index] * directions[index] for index in range(4)]
    return (loss_sum, updated[0], updated[1], updated[2], updated[3], results[0][0], results[1][0], results[2][0], results[3][0], results[0][1], results[1][1], results[2][1], results[3][1], trust, weight_norms, update_norms)
```

```python
from functools import partial
import math

import jax
import jax.numpy as jnp
from jax import lax
from jax.experimental import pallas as pl
from jax.experimental.pallas import tpu as pltpu
from jax.sharding import PartitionSpec as P

D = 1024
HEADS = 16
HEAD_DIM = 64
FF = 4096
CLASSES = 1000
PATCH_FEAT = 16
TFREQ = 256
GRID = 16
TOK = 256
MICRO = 2
STEP = 10
IMG_DEV = 1
SIDE = 1288


BETA_ONE = 0.5
BETA_TWO = 0.5
EPSILON = 1e-06
DECAY = 0.01
RATE = 0.25
NORM_EPS = 1e-06
SMALL_ROWS = 16
AXIS = "fsdp"


def matmul(left, right):
    return jnp.dot(left, right, preferred_element_type=jnp.float32)


def dot_tail(left, right):
    return lax.dot_general(
        left, right, (((1,), (1,)), ((), ())), preferred_element_type=jnp.float32
    )


def dot_head(left, right):
    return lax.dot_general(
        left, right, (((0,), (0,)), ((), ())), preferred_element_type=jnp.float32
    )


def layer_norm(values):
    center = values - jnp.mean(values, axis=-1, keepdims=True)
    return center * lax.rsqrt(jnp.mean(center * center, axis=-1, keepdims=True) + NORM_EPS)


def modulate(values, shift, scale):
    return layer_norm(values) * (1.0 + scale[:, None, :]) + shift[:, None, :]


def noise_scales(steps_part):
    phase = (steps_part.astype(jnp.float32) / 1000.0 + 0.008) / 1.008 * (math.pi / 2.0)
    signal = jnp.cos(phase) * jnp.cos(phase)
    return (jnp.sqrt(signal), jnp.sqrt(1.0 - signal))


def time_features(steps_part):
    half_width = TFREQ // 2
    freqs = jnp.exp(-math.log(10000.0) * jnp.arange(half_width, dtype=jnp.float32) / half_width)
    angles = steps_part.astype(jnp.float32)[:, None] * freqs[None, :]
    return jnp.concatenate([jnp.cos(angles), jnp.sin(angles)], axis=1)


def positions():
    quarter = D // 4
    omega = 1.0 / 10000.0 ** (jnp.arange(quarter, dtype=jnp.float32) / quarter)
    cells = jnp.arange(TOK, dtype=jnp.int32)
    row_pos = (cells // GRID).astype(jnp.float32)[:, None] * omega[None, :]
    col_pos = (cells % GRID).astype(jnp.float32)[:, None] * omega[None, :]
    return jnp.concatenate(
        [jnp.sin(row_pos), jnp.cos(row_pos), jnp.sin(col_pos), jnp.cos(col_pos)], axis=1
    )


def column_blocks():
    return [
        (0, 0, 3 * D),
        (0, 3 * D, 4 * D),
        (0, 4 * D, 4 * D + FF),
        (0, 4 * D + FF, 10 * D + FF),
        (0, 10 * D + FF, 12 * D + FF),
        (0, 12 * D + FF, 13 * D + FF),
        (1, 0, 0),
        (2, 0, TFREQ),
        (2, TFREQ, TFREQ + PATCH_FEAT),
        (2, TFREQ + PATCH_FEAT, TFREQ + PATCH_FEAT + CLASSES),
        (2, TFREQ + PATCH_FEAT + CLASSES, SIDE),
        (3, 0, 0),
    ]


def block_squares(arrays):
    totals = []
    for kind, start, stop in column_blocks():
        if kind in (0, 2):
            piece = arrays[kind][:, start:stop]
        else:
            piece = arrays[kind]
        totals.append(jnp.sum(piece * piece))
    return jnp.stack(totals)


def block_factors(trust):
    rows_in, rows_side = ([], [])
    for index, (kind, start, stop) in enumerate(column_blocks()):
        if kind == 0:
            rows_in.append(jnp.full((stop - start,), trust[index], jnp.float32))
        if kind == 2:
            rows_side.append(jnp.full((stop - start,), trust[index], jnp.float32))
    return (
        jnp.concatenate(rows_in)[None, :],
        trust[6],
        jnp.concatenate(rows_side)[None, :],
        trust[11],
    )


def adam_direction(weight, grad, first, second):
    first_new = BETA_ONE * first + (1.0 - BETA_ONE) * grad
    second_new = BETA_TWO * second + (1.0 - BETA_TWO) * grad * grad
    direction = (
        first_new
        / (1.0 - BETA_ONE**STEP)
        / (jnp.sqrt(second_new / (1.0 - BETA_TWO**STEP)) + EPSILON)
        + DECAY * weight
    )
    return (first_new, second_new, direction)


class Grid:
    def __init__(self, count):
        if count == 32:
            self.sizes = (4, 2, 2, 2)
        elif count == 256:
            self.sizes = (8, 4, 4, 2)
        else:
            self.sizes = (count, 1, 1, 1)
        self.count = count
        index = lax.axis_index(AXIS)
        coords = []
        for size in reversed(self.sizes):
            coords.append(index % size)
            index = index // size
        self.coords = tuple(reversed(coords))

    def ahead(self, values, axis, shift):
        stride = math.prod(self.sizes[axis + 1 :])
        size = self.sizes[axis]
        pairs = []
        for source in range(self.count):
            place = source // stride % size
            pairs.append((source, source + ((place - shift) % size - place) * stride))
        return lax.ppermute(values, AXIS, pairs)

    def flip(self, values, axis, bit):
        stride = math.prod(self.sizes[axis + 1 :])
        pairs = []
        for source in range(self.count):
            place = source // stride % self.sizes[axis]
            pairs.append((source, source + ((place ^ bit) - place) * stride))
        return lax.ppermute(values, AXIS, pairs)

    def place(self, axis, shift):
        return (self.coords[axis] + shift) % self.sizes[axis]


def in_order(grid, pieces, axis):
    size = grid.sizes[axis]
    if size == 1:
        return pieces[0][None]
    if size == 2:
        lower = grid.coords[axis] == 0
        return jnp.stack(
            [jnp.where(lower, pieces[0], pieces[1]), jnp.where(lower, pieces[1], pieces[0])]
        )
    twice = jnp.stack(pieces + pieces)
    return lax.dynamic_slice_in_dim(twice, (size - grid.coords[axis]) % size, size, 0)


def gather_small(grid, values, order):
    for axis in order:
        pieces = [values]
        for shift in range(1, grid.sizes[axis]):
            pieces.append(grid.ahead(values, axis, shift))
        values = in_order(grid, pieces, axis)
    return values


def scatter_axis(grid, values, axis, dim):
    def entry(shift):
        return lax.dynamic_index_in_dim(values, grid.place(axis, shift), dim, keepdims=False)

    total = entry(0)
    for shift in range(1, grid.sizes[axis]):
        total = total + grid.ahead(entry(-shift), axis, shift)
    return total


def scatter_small(grid, values):
    values = scatter_axis(grid, values, 3, 3)
    values = scatter_axis(grid, values, 2, 2)
    values = scatter_axis(grid, values, 1, 1)
    return scatter_axis(grid, values, 0, 0)


def sum_small(grid, values):
    for axis in (3, 2, 1, 0):
        bit = 1
        while bit < grid.sizes[axis]:
            values = values + grid.flip(values, axis, bit)
            bit *= 2
    return values


def place_kernel(moves, where, *refs):
    pieces, full, sems = refs[:-2], refs[-2], refs[-1]
    copies = []
    for number, (piece, entry, spot) in enumerate(moves):
        place = tuple(where[slot] for slot in spot)
        copies.append(
            pltpu.make_async_copy(pieces[piece].at[entry], full.at[place], sems.at[number])
        )
    for copy in copies:
        copy.start()
    for copy in copies:
        copy.wait()


def gather_bulk(grid, shard, order):
    rows, columns = shard.shape
    first, second, third = order
    sizes = grid.sizes
    pieces = [shard]
    for _ in range(1, sizes[first]):
        pieces.append(grid.ahead(pieces[-1], first, 1))
    tagged = [((), jnp.stack(pieces))]
    for axis in (second, third, 3):
        reached = []
        for tag, piece in tagged:
            reached.append((tag + (0,), piece))
            for shift in range(1, sizes[axis]):
                piece = grid.ahead(piece, axis, 1)
                reached.append((tag + (shift,), piece))
        tagged = reached
    offsets = []
    for axis in range(4):
        offsets.append(sum(sizes[:axis]))
    moves = []
    for number, (tag, _) in enumerate(tagged):
        for entry in range(sizes[first]):
            shifts = {first: entry, second: tag[0], third: tag[1], 3: tag[2]}
            spot = tuple(offsets[axis] + shifts[axis] for axis in range(4))
            moves.append((number, entry, spot))
    where = jnp.stack(
        [grid.place(axis, shift) for axis in range(4) for shift in range(sizes[axis])]
    ).astype(jnp.int32)
    if rows % 16 == 0:
        full = pl.pallas_call(
            partial(place_kernel, moves),
            out_shape=jax.ShapeDtypeStruct(sizes + (rows, columns), shard.dtype),
            in_specs=[pl.BlockSpec(memory_space=pltpu.SMEM)]
            + [pl.BlockSpec(memory_space=pl.ANY)] * len(tagged),
            out_specs=pl.BlockSpec(memory_space=pl.ANY),
            scratch_shapes=[pltpu.SemaphoreType.DMA((len(moves),))],
            cost_estimate=pl.CostEstimate(
                flops=0, bytes_accessed=4 * grid.count * rows * columns, transcendentals=0
            ),
        )(where, *[piece for _, piece in tagged])
    else:
        full = jnp.zeros(sizes + (rows, columns), shard.dtype)
        for number, entry, spot in moves:
            place = tuple(where[slot] for slot in spot) + (0, 0)
            block = tagged[number][1][entry].reshape((1, 1, 1, 1, rows, columns))
            full = lax.dynamic_update_slice(full, block, place)
    return full.reshape(grid.count * rows, columns)


def scatter_bulk(grid, table, order):
    rows = table.shape[0] // grid.count
    current = table.reshape(grid.sizes + (rows, table.shape[1]))
    axes = (3,) + tuple(reversed(order))
    for axis in axes:
        size = grid.sizes[axis]

        def entry(shift, current=current, axis=axis):
            return lax.dynamic_index_in_dim(current, grid.place(axis, shift), axis)

        total = entry(1)
        for step in range(1, size):
            sent = grid.ahead(total.astype(jnp.bfloat16), axis, 1)
            total = sent.astype(jnp.float32) + entry(1 + step).astype(jnp.float32)
            if step < size - 1 or axis != axes[-1]:
                total = total.astype(jnp.bfloat16)
        current = total
    return current.reshape(rows, table.shape[1]).astype(jnp.float32)


def attention_scores(queries, keys_all):
    scores = jnp.einsum("bqhd,bkhd->bhqk", queries, keys_all, preferred_element_type=jnp.float32)
    return scores * HEAD_DIM ** (-0.5)


XZY = (2, 0, 1)
YZX = (1, 0, 2)
ZXY = (0, 2, 1)
ZYX = (0, 1, 2)
PLANS = (ZXY, YZX, XZY, YZX, XZY, ZYX)


def per_device(
    latents,
    noise_draw,
    timesteps,
    labels,
    weights_in,
    weights_down,
    weights_side,
    biases,
    first_in,
    first_down,
    first_side,
    first_bias,
    second_in,
    second_down,
    second_side,
    second_bias,
):
    bf16 = jnp.bfloat16
    count_all = lax.axis_size(AXIS)
    grid = Grid(count_all)
    sizes = grid.sizes
    count = latents.shape[0]
    rows_all = count * TOK
    image_total = count * count_all
    rows = weights_in.shape[0]
    bias_rows = biases.shape[0]
    my_rows = lax.axis_index(AXIS) * rows
    masters = (weights_in, weights_down, weights_side, biases)
    in_bf = weights_in.astype(bf16)
    down_bf = weights_down.astype(bf16)
    side_bf = weights_side.astype(bf16)
    t_first = side_bf[:, :TFREQ]
    patch_at = TFREQ
    class_at = TFREQ + PATCH_FEAT
    head_at = class_at + CLASSES
    w_class = side_bf[:, class_at:head_at]
    w_mods = in_bf[:, 4 * D + FF : 12 * D + FF]
    w_time = in_bf[:, 12 * D + FF :]

    numbers = jnp.concatenate([timesteps, labels])
    packed = jnp.concatenate(
        [
            biases.astype(bf16),
            side_bf[:, patch_at:class_at].reshape(-1),
            side_bf[:, head_at:].reshape(-1),
            (numbers // 32).astype(bf16),
            (numbers % 32).astype(bf16),
        ]
    )
    width = packed.shape[0]
    tall = -(-width // (SMALL_ROWS * 128)) * SMALL_ROWS
    packed = jnp.pad(packed, (0, tall * 128 - width)).reshape(tall, 128)
    spread_all = gather_small(grid, packed, (3, 2, 1, 0)).reshape(count_all, tall * 128)
    bias_full = spread_all[:, :bias_rows].reshape(-1).astype(jnp.float32)
    at = bias_rows
    w_patch = spread_all[:, at : at + rows * PATCH_FEAT].reshape(D, PATCH_FEAT)
    at += rows * PATCH_FEAT
    w_head = spread_all[:, at : at + rows * PATCH_FEAT].reshape(D, PATCH_FEAT)
    at += rows * PATCH_FEAT
    numbers = spread_all[:, at : at + 4 * count].astype(jnp.float32)
    numbers = numbers[:, : 2 * count] * 32.0 + numbers[:, 2 * count :]
    numbers = numbers.reshape(sizes + (2 * count,)).transpose(3, 2, 1, 0, 4)
    numbers = numbers.reshape(count_all, 2 * count)
    steps_all = numbers[:, :count].reshape(image_total)
    labels_all = numbers[:, count:].reshape(image_total).astype(jnp.int32)

    table_qk = gather_bulk(grid, in_bf[:, : 2 * D], PLANS[0])
    table_vo = gather_bulk(grid, in_bf[:, 2 * D : 4 * D], PLANS[1])
    half = FF // 2
    up_parts = (
        gather_bulk(grid, in_bf[:, 4 * D : 4 * D + half], PLANS[2]),
        gather_bulk(grid, in_bf[:, 4 * D + half : 4 * D + FF], PLANS[3]),
    )
    down_parts = (
        gather_bulk(grid, down_bf[:, : D // 2], PLANS[4]),
        gather_bulk(grid, down_bf[:, D // 2 :], PLANS[5]),
    )
    w_value, w_out = table_vo[:, :D], table_vo[:, D:]

    b_query = bias_full[:D]
    b_value = bias_full[D : 2 * D]
    b_out = bias_full[2 * D : 3 * D]
    b_up = bias_full[3 * D : 3 * D + FF]
    b_down = bias_full[3 * D + FF : 4 * D + FF]
    b_mods = bias_full[4 * D + FF : 12 * D + FF]
    b_tfirst = lax.dynamic_slice_in_dim(bias_full[12 * D + FF : 13 * D + FF], my_rows, rows)
    b_time = lax.dynamic_slice_in_dim(bias_full[13 * D + FF : 14 * D + FF], my_rows, rows)
    b_patch = bias_full[14 * D + FF :]

    feats = time_features(steps_all).astype(bf16)
    time_pre = dot_tail(t_first, feats) + b_tfirst[:, None]
    time_act = jax.nn.silu(time_pre).astype(bf16)
    onehot = labels_all[:, None] == jnp.arange(CLASSES, dtype=jnp.int32)[None, :]
    cond_part = lax.dot_general(
        w_time, time_act, (((0,), (0,)), ((), ())), preferred_element_type=jnp.float32
    )
    cond = scatter_small(grid, cond_part.reshape(sizes + (rows, image_total)))
    cond = cond + b_time[:, None] + dot_tail(w_class, onehot.astype(bf16))
    cond_act = jax.nn.silu(cond).astype(bf16)

    def scatter_mods(part):
        shape = (sizes[3], sizes[2], sizes[1], sizes[0] * count, part.shape[1])
        part = part.reshape(shape)
        for axis in (3, 2, 1):
            part = scatter_axis(grid, part, axis, 0)
        part = part.reshape(sizes[0], count * part.shape[1] // 128, 128)
        return scatter_axis(grid, part, 0, 0).reshape(count, -1)

    mods_first = scatter_mods(dot_head(cond_act, w_mods[:, : 2 * D])) + b_mods[: 2 * D]
    mods_later = scatter_mods(dot_head(cond_act, w_mods[:, 2 * D :])) + b_mods[2 * D :]
    shift_a, scale_a = mods_first[:, :D], mods_first[:, D:]
    gate_a, shift_b, scale_b, gate_b, shift_f, scale_f = jnp.split(mods_later, 6, axis=1)

    signal, spread = noise_scales(timesteps)
    noise_rows = noise_draw.astype(jnp.float32)
    noisy = signal[:, None, None] * latents.astype(jnp.float32) + spread[:, None, None] * noise_rows
    noisy = noisy.astype(bf16).reshape(rows_all, PATCH_FEAT)
    hidden = dot_tail(noisy, w_patch) + b_patch + jnp.tile(positions(), (count, 1))
    resid_in = hidden.reshape(count, TOK, D)
    normed_a = modulate(resid_in, shift_a, scale_a).astype(bf16).reshape(rows_all, D)
    head_shape = (count, TOK, HEADS, HEAD_DIM)
    proj_qk = matmul(normed_a, table_qk)
    queries = (proj_qk[:, :D] + b_query).astype(bf16).reshape(head_shape)
    keys_all = proj_qk[:, D:].astype(bf16).reshape(head_shape)
    values_all = (matmul(normed_a, w_value) + b_value).astype(bf16).reshape(head_shape)
    scores = attention_scores(queries, keys_all)
    log_total = jax.nn.logsumexp(scores, axis=-1)
    probs = jnp.exp(scores - log_total[..., None]).astype(bf16)
    mixed = jnp.einsum("bhqk,bkhd->bqhd", probs, values_all, preferred_element_type=jnp.float32)
    mixed = mixed.astype(bf16).reshape(rows_all, D)
    attended = (matmul(mixed, w_out) + b_out).reshape(count, TOK, D)
    resid_mid = resid_in + gate_a[:, None, :] * attended
    normed_b = modulate(resid_mid, shift_b, scale_b).astype(bf16).reshape(rows_all, D)
    uppers = [
        matmul(normed_b, part) + b_up[index * half : (index + 1) * half]
        for index, part in enumerate(up_parts)
    ]
    actives = [jax.nn.gelu(upper, approximate=True).astype(bf16) for upper in uppers]
    active = jnp.concatenate(actives, axis=1)
    lowered = jnp.concatenate([matmul(active, part) for part in down_parts], axis=1) + b_down
    lowered = lowered.reshape(count, TOK, D)
    resid_out = resid_mid + gate_b[:, None, :] * lowered
    normed_c = modulate(resid_out, shift_f, scale_f).astype(bf16).reshape(rows_all, D)
    predicted = matmul(normed_c, w_head)
    error = predicted - noise_rows.reshape(rows_all, PATCH_FEAT)
    loss_local = jnp.sum(error * error)
    grad_pred = (2.0 / image_total * error).astype(bf16)

    grad_head = dot_head(normed_c, grad_pred)
    grad_normed_c = dot_tail(grad_pred, w_head).reshape(count, TOK, D)
    _, pull_final = jax.vjp(modulate, resid_out, shift_f, scale_f)
    grad_out, grad_shift_f, grad_scale_f = pull_final(grad_normed_c)
    grad_gate_b = jnp.sum(grad_out * lowered, axis=1)
    grad_lowered = (grad_out * gate_b[:, None, :]).reshape(rows_all, D)
    grad_b_down = jnp.sum(grad_lowered, axis=0)
    lowered_bf = grad_lowered.astype(bf16)
    sum_down = [
        scatter_bulk(grid, dot_head(active, part).astype(bf16), PLANS[4 + index])
        for index, part in enumerate(jnp.split(lowered_bf, 2, axis=1))
    ]
    grad_active = dot_tail(lowered_bf[:, : D // 2], down_parts[0]) + dot_tail(
        lowered_bf[:, D // 2 :], down_parts[1]
    )
    gelu = partial(jax.nn.gelu, approximate=True)
    grad_uppers = [
        jax.vjp(gelu, upper)[1](grad_active[:, index * half : (index + 1) * half])[0]
        for index, upper in enumerate(uppers)
    ]
    grad_b_up = jnp.concatenate([jnp.sum(part, axis=0) for part in grad_uppers])
    upper_bf = [part.astype(bf16) for part in grad_uppers]
    sum_up = [
        scatter_bulk(grid, dot_head(normed_b, part).astype(bf16), PLANS[2 + index])
        for index, part in enumerate(upper_bf)
    ]
    grad_normed_b = (
        dot_tail(upper_bf[0], up_parts[0]) + dot_tail(upper_bf[1], up_parts[1])
    ).reshape(count, TOK, D)
    _, pull_mid = jax.vjp(modulate, resid_mid, shift_b, scale_b)
    grad_mid_norm, grad_shift_b, grad_scale_b = pull_mid(grad_normed_b)
    grad_mid = grad_out + grad_mid_norm
    grad_gate_a = jnp.sum(grad_mid * attended, axis=1)
    grad_attended = (grad_mid * gate_a[:, None, :]).reshape(rows_all, D)
    grad_b_out = jnp.sum(grad_attended, axis=0)
    attended_bf = grad_attended.astype(bf16)
    grad_w_out = dot_head(mixed, attended_bf)
    grad_mixed = dot_tail(attended_bf, w_out).astype(bf16).reshape(head_shape)
    scores = attention_scores(queries, keys_all)
    probs_full = jnp.exp(scores - log_total[..., None])
    grad_probs = jnp.einsum(
        "bqhd,bkhd->bhqk", grad_mixed, values_all, preferred_element_type=jnp.float32
    )
    inner = jnp.sum(probs_full * grad_probs, axis=-1, keepdims=True)
    grad_scores = (probs_full * (grad_probs - inner)).astype(bf16)
    scale = HEAD_DIM ** (-0.5)
    grad_queries = (
        jnp.einsum("bhqk,bkhd->bqhd", grad_scores, keys_all, preferred_element_type=jnp.float32)
        * scale
    ).reshape(rows_all, D)
    grad_keys = (
        jnp.einsum("bhqk,bqhd->bkhd", grad_scores, queries, preferred_element_type=jnp.float32)
        * scale
    ).reshape(rows_all, D)
    grad_values = jnp.einsum(
        "bhqk,bqhd->bkhd", probs_full.astype(bf16), grad_mixed, preferred_element_type=jnp.float32
    ).reshape(rows_all, D)
    grad_b_query = jnp.sum(grad_queries, axis=0)
    grad_b_value = jnp.sum(grad_values, axis=0)
    qk_bf = jnp.concatenate([grad_queries, grad_keys], axis=1).astype(bf16)
    values_bf = grad_values.astype(bf16)
    sum_vo = scatter_bulk(
        grid,
        jnp.concatenate([dot_head(normed_a, values_bf), grad_w_out], axis=1).astype(bf16),
        PLANS[1],
    )
    sum_qk = scatter_bulk(grid, dot_head(normed_a, qk_bf).astype(bf16), PLANS[0])
    grad_normed_a = (dot_tail(qk_bf, table_qk) + dot_tail(values_bf, w_value)).reshape(
        count, TOK, D
    )
    _, pull_first = jax.vjp(modulate, resid_in, shift_a, scale_a)
    grad_in_norm, grad_shift_a, grad_scale_a = pull_first(grad_normed_a)
    grad_hidden = (grad_mid + grad_in_norm).reshape(rows_all, D)
    grad_b_patch = jnp.sum(grad_hidden, axis=0)
    grad_w_patch = dot_head(grad_hidden.astype(bf16), noisy)

    grad_mods = jnp.concatenate(
        [
            grad_shift_a,
            grad_scale_a,
            grad_gate_a,
            grad_shift_b,
            grad_scale_b,
            grad_gate_b,
            grad_shift_f,
            grad_scale_f,
        ],
        axis=1,
    )
    grad_b_mods = jnp.sum(grad_mods, axis=0)
    mods_bf = gather_small(grid, grad_mods.astype(bf16).reshape(-1, 128), (0, 1, 2, 3))
    mods_bf = mods_bf.reshape(image_total, 8 * D)
    grad_w_mods = matmul(cond_act, mods_bf)
    grad_cond_act = dot_tail(w_mods, mods_bf)
    grad_cond = jax.vjp(jax.nn.silu, cond)[1](grad_cond_act)[0]
    grad_w_class = jnp.dot(
        grad_cond,
        onehot.astype(jnp.float32),
        precision=lax.Precision.HIGHEST,
        preferred_element_type=jnp.float32,
    )
    grad_b_time = jnp.sum(grad_cond, axis=1)
    cond_bf = gather_small(grid, grad_cond.astype(bf16), (3, 2, 1, 0)).reshape(D, image_total)
    grad_w_time = dot_tail(time_act, cond_bf)
    grad_time_act = matmul(w_time, cond_bf)
    grad_time_pre = jax.vjp(jax.nn.silu, time_pre)[1](grad_time_act)[0]
    grad_b_tfirst = jnp.sum(grad_time_pre, axis=1)
    grad_t_first = matmul(grad_time_pre.astype(bf16), feats)

    def spread_rows(part):
        return lax.dynamic_update_slice(jnp.zeros((D,), jnp.float32), part, (my_rows,))

    grad_bias = jnp.concatenate(
        [
            grad_b_query,
            grad_b_value,
            grad_b_out,
            grad_b_up,
            grad_b_down,
            grad_b_mods,
            spread_rows(grad_b_tfirst),
            spread_rows(grad_b_time),
            grad_b_patch,
        ]
    )
    small = jnp.concatenate(
        [
            grad_bias.reshape(count_all, bias_rows),
            grad_w_patch.reshape(count_all, rows * PATCH_FEAT),
            grad_head.reshape(count_all, rows * PATCH_FEAT),
        ],
        axis=1,
    )
    tall = -(-small.shape[1] // 1024) * 8
    small = jnp.pad(small, ((0, 0), (0, tall * 128 - small.shape[1])))
    small = scatter_small(grid, small.reshape(sizes + (tall, 128))).reshape(-1)
    at = bias_rows
    sum_patch = small[at : at + rows * PATCH_FEAT].reshape(rows, PATCH_FEAT)
    at += rows * PATCH_FEAT
    sum_head = small[at : at + rows * PATCH_FEAT].reshape(rows, PATCH_FEAT)

    reduced = (
        jnp.concatenate([sum_qk, sum_vo, *sum_up, grad_w_mods, grad_w_time], axis=1),
        jnp.concatenate(sum_down, axis=1),
        jnp.concatenate([grad_t_first, sum_patch, grad_w_class, sum_head], axis=1),
        small[:bias_rows],
    )
    firsts = (first_in, first_down, first_side, first_bias)
    seconds = (second_in, second_down, second_side, second_bias)
    results = [
        adam_direction(masters[index], reduced[index], firsts[index], seconds[index])
        for index in range(4)
    ]
    directions = [item[2] for item in results]
    early = sum_small(grid, jnp.concatenate([loss_local[None], block_squares(masters)]))
    loss_sum, weight_sq = early[0], early[1:]
    update_sq = sum_small(grid, block_squares(directions))
    weight_norms = jnp.sqrt(weight_sq)
    update_norms = jnp.sqrt(update_sq)
    trust = weight_norms / update_norms
    factors = block_factors(trust)
    updated = [masters[index] - RATE * factors[index] * directions[index] for index in range(4)]
    return (
        loss_sum,
        updated[0],
        updated[1],
        updated[2],
        updated[3],
        results[0][0],
        results[1][0],
        results[2][0],
        results[3][0],
        results[0][1],
        results[1][1],
        results[2][1],
        results[3][1],
        trust,
        weight_norms,
        update_norms,
    )


def solution(mesh):
    placed = (
        P("fsdp", None, None),
        P("fsdp", None, None),
        P("fsdp"),
        P("fsdp"),
        P("fsdp", None),
        P("fsdp", None),
        P("fsdp", None),
        P("fsdp"),
        P("fsdp", None),
        P("fsdp", None),
        P("fsdp", None),
        P("fsdp"),
        P("fsdp", None),
        P("fsdp", None),
        P("fsdp", None),
        P("fsdp"),
    )
    return jax.shard_map(
        per_device,
        mesh=mesh,
        in_specs=placed,
        out_specs=(
            P(),
            P("fsdp", None),
            P("fsdp", None),
            P("fsdp", None),
            P("fsdp"),
            P("fsdp", None),
            P("fsdp", None),
            P("fsdp", None),
            P("fsdp"),
            P("fsdp", None),
            P("fsdp", None),
            P("fsdp", None),
            P("fsdp"),
            P(),
            P(),
            P(),
        ),
        check_vma=False,
    )
```

```python
from functools import partial
import math

import jax
import jax.numpy as jnp
from jax import lax
from jax.experimental import pallas as pl
from jax.experimental.pallas import tpu as pltpu
from jax.sharding import PartitionSpec as P

D = 1024
HEADS = 16
HEAD_DIM = 64
FF = 4096
CLASSES = 1000
PATCH_FEAT = 16
TFREQ = 256
GRID = 16
TOK = 256
MICRO = 2
STEP = 10
IMG_DEV = 1
SIDE = 1288


BETA_ONE = 0.5
BETA_TWO = 0.5
EPSILON = 1e-06
DECAY = 0.01
RATE = 0.25
NORM_EPS = 1e-06
SMALL_ROWS = 16
AXIS = "fsdp"


def matmul(left, right):
    return jnp.dot(left, right, preferred_element_type=jnp.float32)


def dot_tail(left, right):
    return lax.dot_general(
        left, right, (((1,), (1,)), ((), ())), preferred_element_type=jnp.float32
    )


def dot_head(left, right):
    return lax.dot_general(
        left, right, (((0,), (0,)), ((), ())), preferred_element_type=jnp.float32
    )


def layer_norm(values):
    center = values - jnp.mean(values, axis=-1, keepdims=True)
    return center * lax.rsqrt(jnp.mean(center * center, axis=-1, keepdims=True) + NORM_EPS)


def modulate(values, shift, scale):
    return layer_norm(values) * (1.0 + scale[:, None, :]) + shift[:, None, :]


def noise_scales(steps_part):
    phase = (steps_part.astype(jnp.float32) / 1000.0 + 0.008) / 1.008 * (math.pi / 2.0)
    signal = jnp.cos(phase) * jnp.cos(phase)
    return (jnp.sqrt(signal), jnp.sqrt(1.0 - signal))


def time_features(steps_part):
    half_width = TFREQ // 2
    freqs = jnp.exp(-math.log(10000.0) * jnp.arange(half_width, dtype=jnp.float32) / half_width)
    angles = steps_part.astype(jnp.float32)[:, None] * freqs[None, :]
    return jnp.concatenate([jnp.cos(angles), jnp.sin(angles)], axis=1)


def positions():
    quarter = D // 4
    omega = 1.0 / 10000.0 ** (jnp.arange(quarter, dtype=jnp.float32) / quarter)
    cells = jnp.arange(TOK, dtype=jnp.int32)
    row_pos = (cells // GRID).astype(jnp.float32)[:, None] * omega[None, :]
    col_pos = (cells % GRID).astype(jnp.float32)[:, None] * omega[None, :]
    return jnp.concatenate(
        [jnp.sin(row_pos), jnp.cos(row_pos), jnp.sin(col_pos), jnp.cos(col_pos)], axis=1
    )


def column_blocks():
    return [
        (0, 0, 3 * D),
        (0, 3 * D, 4 * D),
        (0, 4 * D, 4 * D + FF),
        (0, 4 * D + FF, 10 * D + FF),
        (0, 10 * D + FF, 12 * D + FF),
        (0, 12 * D + FF, 13 * D + FF),
        (1, 0, 0),
        (2, 0, TFREQ),
        (2, TFREQ, TFREQ + PATCH_FEAT),
        (2, TFREQ + PATCH_FEAT, TFREQ + PATCH_FEAT + CLASSES),
        (2, TFREQ + PATCH_FEAT + CLASSES, SIDE),
        (3, 0, 0),
    ]


def block_squares(arrays):
    totals = []
    for kind, start, stop in column_blocks():
        if kind in (0, 2):
            piece = arrays[kind][:, start:stop]
        else:
            piece = arrays[kind]
        totals.append(jnp.sum(piece * piece))
    return totals


def as_vector(scalars):
    places = jnp.arange(32, dtype=jnp.int32)
    vector = jnp.zeros((32,), jnp.float32)
    for index, value in enumerate(scalars):
        vector = jnp.where(places == index, value, vector)
    return vector


def block_factors(trust):
    rows_in, rows_side = ([], [])
    for index, (kind, start, stop) in enumerate(column_blocks()):
        if kind == 0:
            rows_in.append(jnp.full((stop - start,), trust[index], jnp.float32))
        if kind == 2:
            rows_side.append(jnp.full((stop - start,), trust[index], jnp.float32))
    return (
        jnp.concatenate(rows_in)[None, :],
        trust[6],
        jnp.concatenate(rows_side)[None, :],
        trust[11],
    )


def adam_direction(weight, grad, first, second):
    first_new = BETA_ONE * first + (1.0 - BETA_ONE) * grad
    second_new = BETA_TWO * second + (1.0 - BETA_TWO) * grad * grad
    direction = (
        first_new
        / (1.0 - BETA_ONE**STEP)
        / (jnp.sqrt(second_new / (1.0 - BETA_TWO**STEP)) + EPSILON)
        + DECAY * weight
    )
    return (first_new, second_new, direction)


Z_AXIS, Y_AXIS, X_AXIS, CORE, MIX_P, MIX_Q = range(6)


class Grid:
    def __init__(self, count):
        if count == 32:
            sizes = (4, 2, 2, 2)
        elif count == 256:
            sizes = (8, 4, 4, 2)
        else:
            sizes = (count, 1, 1, 1)
        self.count = count
        self.shape = sizes
        self.sizes = sizes + (sizes[X_AXIS], sizes[Y_AXIS])
        index = lax.axis_index(AXIS)
        self.coords = self.split(index)
        mixed = [
            jnp.where(self.coords[CORE] == 0, self.coords[X_AXIS], self.coords[Y_AXIS]),
            jnp.where(self.coords[CORE] == 0, self.coords[Y_AXIS], self.coords[X_AXIS]),
        ]
        self.coords = self.coords + tuple(mixed)

    def split(self, index):
        coords = []
        for size in reversed(self.shape):
            coords.append(index % size)
            index = index // size
        return tuple(reversed(coords))

    def join(self, coords):
        index = 0
        for size, place in zip(self.shape, coords):
            index = index * size + place
        return index

    def move(self, values, axis, change):
        pairs = []
        for source in range(self.count):
            coords = list(self.split(source))
            real = axis
            if axis == MIX_P:
                real = X_AXIS if coords[CORE] == 0 else Y_AXIS
            if axis == MIX_Q:
                real = Y_AXIS if coords[CORE] == 0 else X_AXIS
            coords[real] = change(coords[real])
            pairs.append((source, self.join(coords)))
        return lax.ppermute(values, AXIS, pairs)

    def ahead(self, values, axis, shift):
        size = self.sizes[axis]
        return self.move(values, axis, lambda place: (place - shift) % size)

    def flip(self, values, axis, bit):
        return self.move(values, axis, lambda place: place ^ bit)

    def place(self, axis, shift):
        return (self.coords[axis] + shift) % self.sizes[axis]


def in_order(grid, pieces, axis):
    size = grid.sizes[axis]
    if size == 1:
        return pieces[0][None]
    if size == 2:
        lower = grid.coords[axis] == 0
        return jnp.stack(
            [jnp.where(lower, pieces[0], pieces[1]), jnp.where(lower, pieces[1], pieces[0])]
        )
    twice = jnp.stack(pieces + pieces)
    return lax.dynamic_slice_in_dim(twice, (size - grid.coords[axis]) % size, size, 0)


def gather_small(grid, values, order):
    for axis in order:
        pieces = [values]
        for shift in range(1, grid.sizes[axis]):
            pieces.append(grid.ahead(values, axis, shift))
        values = in_order(grid, pieces, axis)
    return values


def scatter_axis(grid, values, axis, dim):
    def entry(shift):
        return lax.dynamic_index_in_dim(values, grid.place(axis, shift), dim, keepdims=False)

    total = entry(0)
    for shift in range(1, grid.sizes[axis]):
        total = total + grid.ahead(entry(-shift), axis, shift)
    return total


def scatter_small(grid, values):
    values = scatter_axis(grid, values, 3, 3)
    values = scatter_axis(grid, values, 2, 2)
    values = scatter_axis(grid, values, 1, 1)
    return scatter_axis(grid, values, 0, 0)


def sum_small(grid, values):
    for axis in (3, 2, 1, 0):
        bit = 1
        while bit < grid.sizes[axis]:
            values = values + grid.flip(values, axis, bit)
            bit *= 2
    return values


def place_kernel(moves, where, *refs):
    pieces, full, sems = refs[:-2], refs[-2], refs[-1]
    copies = []
    for number, (piece, entry) in enumerate(moves):
        copies.append(
            pltpu.make_async_copy(
                pieces[piece].at[entry], full.at[where[number]], sems.at[number]
            )
        )
    for copy in copies:
        copy.start()
    for copy in copies:
        copy.wait()


def gather_bulk(grid, shard, order):
    rows, columns = shard.shape
    parts = [shard]
    for axis in order:
        sent = jnp.stack(parts).reshape((-1, rows, columns))
        parts = [sent]
        for _ in range(1, grid.sizes[axis]):
            parts.append(grid.ahead(parts[-1], axis, 1))
    if grid.sizes[CORE] == 2:
        parts = parts + [grid.ahead(part, CORE, 1) for part in parts]
    dims = (grid.sizes[CORE],) + tuple(grid.sizes[axis] for axis in reversed(order))
    number = jnp.arange(grid.count, dtype=jnp.int32)
    shifts = {}
    for axis, size in reversed(list(zip((CORE,) + tuple(reversed(order)), dims))):
        shifts[axis] = number % size
        number = number // size
    core = (grid.coords[CORE] + shifts[CORE]) % grid.sizes[CORE]
    x_ahead = jnp.where(core == 0, shifts[MIX_P], shifts[MIX_Q])
    y_ahead = jnp.where(core == 0, shifts[MIX_Q], shifts[MIX_P])
    where = grid.join(
        (
            (grid.coords[Z_AXIS] + shifts[Z_AXIS]) % grid.sizes[Z_AXIS],
            (grid.coords[Y_AXIS] + y_ahead) % grid.sizes[Y_AXIS],
            (grid.coords[X_AXIS] + x_ahead) % grid.sizes[X_AXIS],
            core,
        )
    ).astype(jnp.int32)
    entries = parts[0].shape[0]
    moves = [(piece, entry) for piece in range(len(parts)) for entry in range(entries)]
    if rows % 16 == 0:
        full = pl.pallas_call(
            partial(place_kernel, moves),
            out_shape=jax.ShapeDtypeStruct((grid.count, rows, columns), shard.dtype),
            in_specs=[pl.BlockSpec(memory_space=pltpu.SMEM)]
            + [pl.BlockSpec(memory_space=pl.ANY)] * len(parts),
            out_specs=pl.BlockSpec(memory_space=pltpu.VMEM),
            scratch_shapes=[pltpu.SemaphoreType.DMA((len(moves),))],
            compiler_params=pltpu.CompilerParams(vmem_limit_bytes=24 * 2**20),
            cost_estimate=pl.CostEstimate(
                flops=0, bytes_accessed=4 * grid.count * rows * columns, transcendentals=0
            ),
        )(where, *parts)
    else:
        stacked = jnp.stack(parts).reshape((grid.count, rows, columns))
        full = jnp.zeros((grid.count, rows, columns), shard.dtype).at[where].set(stacked)
    return full.reshape(grid.count * rows, columns)


def scatter_bulk(grid, table, order):
    rows = table.shape[0] // grid.count
    current = table.reshape(grid.shape + (rows, table.shape[1]))
    first = grid.coords[CORE] == 0

    def entry(axis, shift):
        place = grid.place(axis, shift)
        if axis in (MIX_P, MIX_Q):
            return lax.dynamic_index_in_dim(current, place, X_AXIS if axis == MIX_P else Y_AXIS)
        return lax.dynamic_index_in_dim(current, place, axis)

    for axis in (CORE,) + tuple(reversed(order)):
        size = grid.sizes[axis]
        total = entry(axis, 1)
        for step in range(1, size):
            sent = grid.ahead(total, axis, 1)
            total = sent.astype(jnp.float32) + entry(axis, 1 + step).astype(jnp.float32)
            if step < size - 1 or axis != order[0]:
                total = total.astype(jnp.bfloat16)
        current = total
        if axis == CORE:
            current = jnp.where(first, current, jnp.swapaxes(current, Y_AXIS, X_AXIS))
    return current.reshape(rows, table.shape[1]).astype(jnp.float32)


def attention_scores(queries, keys_all):
    scores = jnp.einsum("bqhd,bkhd->bhqk", queries, keys_all, preferred_element_type=jnp.float32)
    return scores * HEAD_DIM ** (-0.5)


OUTER = (MIX_P, Z_AXIS, MIX_Q)
DEEP = (Z_AXIS, MIX_P, MIX_Q)


def after(values, *others):
    return lax.optimization_barrier((values,) + others)[0]


def per_device(
    latents,
    noise_draw,
    timesteps,
    labels,
    weights_in,
    weights_down,
    weights_side,
    biases,
    first_in,
    first_down,
    first_side,
    first_bias,
    second_in,
    second_down,
    second_side,
    second_bias,
):
    bf16 = jnp.bfloat16
    count_all = lax.axis_size(AXIS)
    grid = Grid(count_all)
    sizes = grid.shape
    count = latents.shape[0]
    rows_all = count * TOK
    image_total = count * count_all
    rows = weights_in.shape[0]
    bias_rows = biases.shape[0]
    my_rows = lax.axis_index(AXIS) * rows
    masters = (weights_in, weights_down, weights_side, biases)
    in_bf = weights_in.astype(bf16)
    down_bf = weights_down.astype(bf16)
    side_bf = weights_side.astype(bf16)
    t_first = side_bf[:, :TFREQ]
    patch_at = TFREQ
    class_at = TFREQ + PATCH_FEAT
    head_at = class_at + CLASSES
    w_class = side_bf[:, class_at:head_at]
    w_mods = in_bf[:, 4 * D + FF : 12 * D + FF]
    w_time = in_bf[:, 12 * D + FF :]

    numbers = jnp.concatenate([timesteps, labels])
    packed = jnp.concatenate(
        [
            biases.astype(bf16),
            side_bf[:, patch_at:class_at].reshape(-1),
            side_bf[:, head_at:].reshape(-1),
            (numbers // 32).astype(bf16),
            (numbers % 32).astype(bf16),
        ]
    )
    width = packed.shape[0]
    tall = -(-width // (SMALL_ROWS * 128)) * SMALL_ROWS
    packed = jnp.pad(packed, (0, tall * 128 - width)).reshape(tall, 128)
    spread_all = gather_small(grid, packed, (3, 2, 1, 0)).reshape(count_all, tall * 128)
    bias_full = spread_all[:, :bias_rows].reshape(-1).astype(jnp.float32)
    at = bias_rows
    w_patch = spread_all[:, at : at + rows * PATCH_FEAT].reshape(D, PATCH_FEAT)
    at += rows * PATCH_FEAT
    w_head = spread_all[:, at : at + rows * PATCH_FEAT].reshape(D, PATCH_FEAT)
    at += rows * PATCH_FEAT
    numbers = spread_all[:, at : at + 4 * count].astype(jnp.float32)
    numbers = numbers[:, : 2 * count] * 32.0 + numbers[:, 2 * count :]
    numbers = numbers.reshape(sizes + (2 * count,))
    numbers = jnp.stack(
        [numbers[:, :, :, core].transpose((1, 2, 0, 3) if core else (2, 1, 0, 3)) for core in range(sizes[CORE])]
    ).reshape(count_all, 2 * count)
    steps_all = numbers[:, :count].reshape(image_total)
    labels_all = numbers[:, count:].reshape(image_total).astype(jnp.int32)

    table_qk = gather_bulk(grid, in_bf[:, : 2 * D], OUTER)
    table_vo = gather_bulk(grid, in_bf[:, 2 * D : 4 * D], OUTER)
    table_up = gather_bulk(grid, in_bf[:, 4 * D : 4 * D + FF], OUTER)
    table_down = gather_bulk(grid, down_bf, DEEP)
    w_value, w_out = table_vo[:, :D], table_vo[:, D:]

    b_query = bias_full[:D]
    b_value = bias_full[D : 2 * D]
    b_out = bias_full[2 * D : 3 * D]
    b_up = bias_full[3 * D : 3 * D + FF]
    b_down = bias_full[3 * D + FF : 4 * D + FF]
    b_mods = bias_full[4 * D + FF : 12 * D + FF]
    b_tfirst = lax.dynamic_slice_in_dim(bias_full[12 * D + FF : 13 * D + FF], my_rows, rows)
    b_time = lax.dynamic_slice_in_dim(bias_full[13 * D + FF : 14 * D + FF], my_rows, rows)
    b_patch = bias_full[14 * D + FF :]

    feats = time_features(steps_all).astype(bf16)
    time_pre = dot_tail(t_first, feats) + b_tfirst[:, None]
    time_act = jax.nn.silu(time_pre).astype(bf16)
    onehot = labels_all[:, None] == jnp.arange(CLASSES, dtype=jnp.int32)[None, :]
    cond_part = lax.dot_general(
        w_time, time_act, (((0,), (0,)), ((), ())), preferred_element_type=jnp.float32
    )
    cond = scatter_small(grid, cond_part.reshape(sizes + (rows, image_total)))
    cond = cond + b_time[:, None] + dot_tail(w_class, onehot.astype(bf16))
    cond_act = jax.nn.silu(cond).astype(bf16)

    mods = dot_head(cond_act, w_mods)
    mods = mods.reshape(sizes[CORE], sizes[X_AXIS], sizes[Y_AXIS], sizes[Z_AXIS] * count, 8 * D)
    for axis in (CORE, MIX_P, MIX_Q):
        mods = scatter_axis(grid, mods, axis, 0)
    mods = mods.reshape(sizes[Z_AXIS], count * 8 * D // 128, 128)
    mods = scatter_axis(grid, mods, Z_AXIS, 0).reshape(count, 8 * D) + b_mods
    shift_a, scale_a, gate_a, shift_b, scale_b, gate_b, shift_f, scale_f = jnp.split(
        mods, 8, axis=1
    )

    signal, spread = noise_scales(timesteps)
    noise_rows = noise_draw.astype(jnp.float32)
    noisy = signal[:, None, None] * latents.astype(jnp.float32) + spread[:, None, None] * noise_rows
    noisy = noisy.astype(bf16).reshape(rows_all, PATCH_FEAT)
    hidden = dot_tail(noisy, w_patch) + b_patch + jnp.tile(positions(), (count, 1))
    resid_in = hidden.reshape(count, TOK, D)
    normed_a = modulate(resid_in, shift_a, scale_a).astype(bf16).reshape(rows_all, D)
    head_shape = (count, TOK, HEADS, HEAD_DIM)
    proj_qk = matmul(normed_a, table_qk)
    queries = (proj_qk[:, :D] + b_query).astype(bf16).reshape(head_shape)
    keys_all = proj_qk[:, D:].astype(bf16).reshape(head_shape)
    values_all = (matmul(normed_a, w_value) + b_value).astype(bf16).reshape(head_shape)
    scores = attention_scores(queries, keys_all)
    log_total = jax.nn.logsumexp(scores, axis=-1)
    probs = jnp.exp(scores - log_total[..., None]).astype(bf16)
    mixed = jnp.einsum("bhqk,bkhd->bqhd", probs, values_all, preferred_element_type=jnp.float32)
    mixed = mixed.astype(bf16).reshape(rows_all, D)
    attended = (matmul(mixed, w_out) + b_out).reshape(count, TOK, D)
    resid_mid = resid_in + gate_a[:, None, :] * attended
    normed_b = modulate(resid_mid, shift_b, scale_b).astype(bf16).reshape(rows_all, D)
    upper = matmul(normed_b, table_up) + b_up
    active = jax.nn.gelu(upper, approximate=True).astype(bf16)
    lowered = matmul(active, table_down) + b_down
    lowered = lowered.reshape(count, TOK, D)
    resid_out = resid_mid + gate_b[:, None, :] * lowered
    normed_c = modulate(resid_out, shift_f, scale_f).astype(bf16).reshape(rows_all, D)
    predicted = matmul(normed_c, w_head)
    error = predicted - noise_rows.reshape(rows_all, PATCH_FEAT)
    loss_local = jnp.sum(error * error)
    grad_pred = (2.0 / image_total * error).astype(bf16)

    grad_head = dot_head(normed_c, grad_pred)
    grad_normed_c = dot_tail(grad_pred, w_head).reshape(count, TOK, D)
    _, pull_final = jax.vjp(modulate, resid_out, shift_f, scale_f)
    grad_out, grad_shift_f, grad_scale_f = pull_final(grad_normed_c)
    grad_gate_b = jnp.sum(grad_out * lowered, axis=1)
    grad_lowered = (grad_out * gate_b[:, None, :]).reshape(rows_all, D)
    grad_b_down = jnp.sum(grad_lowered, axis=0)
    lowered_bf = grad_lowered.astype(bf16)
    grad_w_down = dot_head(active, lowered_bf).astype(bf16)
    sum_down = scatter_bulk(grid, grad_w_down, OUTER)
    lowered_bf = after(lowered_bf, grad_w_down)
    grad_active = dot_tail(lowered_bf, table_down)
    gelu = partial(jax.nn.gelu, approximate=True)
    grad_upper = jax.vjp(gelu, upper)[1](grad_active)[0]
    grad_b_up = jnp.sum(grad_upper, axis=0)
    upper_bf = grad_upper.astype(bf16)
    grad_w_up = dot_head(normed_b, upper_bf).astype(bf16)
    sum_up = scatter_bulk(grid, grad_w_up, OUTER)
    upper_bf = after(upper_bf, grad_w_up)
    grad_normed_b = dot_tail(upper_bf, table_up).reshape(count, TOK, D)
    _, pull_mid = jax.vjp(modulate, resid_mid, shift_b, scale_b)
    grad_mid_norm, grad_shift_b, grad_scale_b = pull_mid(grad_normed_b)
    grad_mid = grad_out + grad_mid_norm
    grad_gate_a = jnp.sum(grad_mid * attended, axis=1)
    grad_attended = (grad_mid * gate_a[:, None, :]).reshape(rows_all, D)
    grad_b_out = jnp.sum(grad_attended, axis=0)
    attended_bf = grad_attended.astype(bf16)
    grad_w_out = dot_head(mixed, attended_bf)
    grad_mixed = dot_tail(attended_bf, w_out).astype(bf16).reshape(head_shape)
    scores = attention_scores(queries, keys_all)
    probs_full = jnp.exp(scores - log_total[..., None])
    grad_probs = jnp.einsum(
        "bqhd,bkhd->bhqk", grad_mixed, values_all, preferred_element_type=jnp.float32
    )
    inner = jnp.sum(probs_full * grad_probs, axis=-1, keepdims=True)
    grad_scores = (probs_full * (grad_probs - inner)).astype(bf16)
    scale = HEAD_DIM ** (-0.5)
    grad_queries = (
        jnp.einsum("bhqk,bkhd->bqhd", grad_scores, keys_all, preferred_element_type=jnp.float32)
        * scale
    ).reshape(rows_all, D)
    grad_keys = (
        jnp.einsum("bhqk,bqhd->bkhd", grad_scores, queries, preferred_element_type=jnp.float32)
        * scale
    ).reshape(rows_all, D)
    grad_values = jnp.einsum(
        "bhqk,bqhd->bkhd", probs_full.astype(bf16), grad_mixed, preferred_element_type=jnp.float32
    ).reshape(rows_all, D)
    grad_b_query = jnp.sum(grad_queries, axis=0)
    grad_b_value = jnp.sum(grad_values, axis=0)
    qk_bf = jnp.concatenate([grad_queries, grad_keys], axis=1).astype(bf16)
    values_bf = grad_values.astype(bf16)
    grad_vo = jnp.concatenate([dot_head(normed_a, values_bf), grad_w_out], axis=1).astype(bf16)
    grad_qk = dot_head(normed_a, qk_bf).astype(bf16)
    sum_vo = scatter_bulk(grid, grad_vo, OUTER)
    sum_qk = scatter_bulk(grid, grad_qk, OUTER)
    qk_bf = after(qk_bf, grad_vo, grad_qk)
    grad_normed_a = (dot_tail(qk_bf, table_qk) + dot_tail(values_bf, w_value)).reshape(
        count, TOK, D
    )
    _, pull_first = jax.vjp(modulate, resid_in, shift_a, scale_a)
    grad_in_norm, grad_shift_a, grad_scale_a = pull_first(grad_normed_a)
    grad_hidden = (grad_mid + grad_in_norm).reshape(rows_all, D)
    grad_b_patch = jnp.sum(grad_hidden, axis=0)
    grad_w_patch = dot_head(grad_hidden.astype(bf16), noisy)

    grad_mods = jnp.concatenate(
        [
            grad_shift_a,
            grad_scale_a,
            grad_gate_a,
            grad_shift_b,
            grad_scale_b,
            grad_gate_b,
            grad_shift_f,
            grad_scale_f,
        ],
        axis=1,
    )
    grad_b_mods = jnp.sum(grad_mods, axis=0)
    mods_bf = gather_small(grid, grad_mods.astype(bf16).reshape(-1, 128), (Z_AXIS, MIX_Q, MIX_P, CORE))
    mods_bf = mods_bf.reshape(image_total, 8 * D)
    grad_w_mods = matmul(cond_act, mods_bf)
    grad_cond_act = dot_tail(w_mods, mods_bf)
    grad_cond = jax.vjp(jax.nn.silu, cond)[1](grad_cond_act)[0]
    grad_w_class = jnp.dot(
        grad_cond,
        onehot.astype(jnp.float32),
        precision=lax.Precision.HIGHEST,
        preferred_element_type=jnp.float32,
    )
    grad_b_time = jnp.sum(grad_cond, axis=1)
    cond_bf = gather_small(grid, grad_cond.astype(bf16), (3, 2, 1, 0)).reshape(D, image_total)
    grad_w_time = dot_tail(time_act, cond_bf)
    grad_time_act = matmul(w_time, cond_bf)
    grad_time_pre = jax.vjp(jax.nn.silu, time_pre)[1](grad_time_act)[0]
    grad_b_tfirst = jnp.sum(grad_time_pre, axis=1)
    grad_t_first = matmul(grad_time_pre.astype(bf16), feats)

    def spread_rows(part):
        return lax.dynamic_update_slice(jnp.zeros((D,), jnp.float32), part, (my_rows,))

    grad_bias = jnp.concatenate(
        [
            grad_b_query,
            grad_b_value,
            grad_b_out,
            grad_b_up,
            grad_b_down,
            grad_b_mods,
            spread_rows(grad_b_tfirst),
            spread_rows(grad_b_time),
            grad_b_patch,
        ]
    )
    small = jnp.concatenate(
        [
            grad_bias.reshape(count_all, bias_rows),
            grad_w_patch.reshape(count_all, rows * PATCH_FEAT),
            grad_head.reshape(count_all, rows * PATCH_FEAT),
        ],
        axis=1,
    )
    tall = -(-small.shape[1] // 1024) * 8
    small = jnp.pad(small, ((0, 0), (0, tall * 128 - small.shape[1])))
    small = scatter_small(grid, small.reshape(sizes + (tall, 128))).reshape(-1)
    at = bias_rows
    sum_patch = small[at : at + rows * PATCH_FEAT].reshape(rows, PATCH_FEAT)
    at += rows * PATCH_FEAT
    sum_head = small[at : at + rows * PATCH_FEAT].reshape(rows, PATCH_FEAT)

    reduced = (
        jnp.concatenate([sum_qk, sum_vo, sum_up, grad_w_mods, grad_w_time], axis=1),
        sum_down,
        jnp.concatenate([grad_t_first, sum_patch, grad_w_class, sum_head], axis=1),
        small[:bias_rows],
    )
    firsts = (first_in, first_down, first_side, first_bias)
    seconds = (second_in, second_down, second_side, second_bias)
    results = [
        adam_direction(masters[index], reduced[index], firsts[index], seconds[index])
        for index in range(4)
    ]
    directions = [item[2] for item in results]
    sums = sum_small(grid, as_vector([loss_local] + block_squares(masters) + block_squares(directions)))
    loss_sum, weight_sq, update_sq = sums[0], sums[1:13], sums[13:25]
    weight_norms = jnp.sqrt(weight_sq)
    update_norms = jnp.sqrt(update_sq)
    trust = weight_norms / update_norms
    factors = block_factors(trust)
    updated = [masters[index] - RATE * factors[index] * directions[index] for index in range(4)]
    return (
        loss_sum,
        updated[0],
        updated[1],
        updated[2],
        updated[3],
        results[0][0],
        results[1][0],
        results[2][0],
        results[3][0],
        results[0][1],
        results[1][1],
        results[2][1],
        results[3][1],
        trust,
        weight_norms,
        update_norms,
    )


def solution(mesh):
    placed = (
        P("fsdp", None, None),
        P("fsdp", None, None),
        P("fsdp"),
        P("fsdp"),
        P("fsdp", None),
        P("fsdp", None),
        P("fsdp", None),
        P("fsdp"),
        P("fsdp", None),
        P("fsdp", None),
        P("fsdp", None),
        P("fsdp"),
        P("fsdp", None),
        P("fsdp", None),
        P("fsdp", None),
        P("fsdp"),
    )
    return jax.shard_map(
        per_device,
        mesh=mesh,
        in_specs=placed,
        out_specs=(
            P(),
            P("fsdp", None),
            P("fsdp", None),
            P("fsdp", None),
            P("fsdp"),
            P("fsdp", None),
            P("fsdp", None),
            P("fsdp", None),
            P("fsdp"),
            P("fsdp", None),
            P("fsdp", None),
            P("fsdp", None),
            P("fsdp"),
            P(),
            P(),
            P(),
        ),
        check_vma=False,
    )
```

```python
from functools import partial
import math

import jax
import jax.numpy as jnp
from jax import lax
from jax.experimental import pallas as pl
from jax.experimental.pallas import tpu as pltpu
from jax.sharding import PartitionSpec as P

D = 1024
HEADS = 16
HEAD_DIM = 64
FF = 4096
CLASSES = 1000
PATCH_FEAT = 16
TFREQ = 256
GRID = 16
TOK = 256
MICRO = 2
STEP = 10
IMG_DEV = 1
SIDE = 1288


BETA_ONE = 0.5
BETA_TWO = 0.5
EPSILON = 1e-06
DECAY = 0.01
RATE = 0.25
NORM_EPS = 1e-06
SMALL_ROWS = 16
AXIS = "fsdp"


def matmul(left, right):
    return jnp.dot(left, right, preferred_element_type=jnp.float32)


def dot_tail(left, right):
    return lax.dot_general(
        left, right, (((1,), (1,)), ((), ())), preferred_element_type=jnp.float32
    )


def dot_head(left, right):
    return lax.dot_general(
        left, right, (((0,), (0,)), ((), ())), preferred_element_type=jnp.float32
    )


def layer_norm(values):
    center = values - jnp.mean(values, axis=-1, keepdims=True)
    return center * lax.rsqrt(jnp.mean(center * center, axis=-1, keepdims=True) + NORM_EPS)


def modulate(values, shift, scale):
    return layer_norm(values) * (1.0 + scale[:, None, :]) + shift[:, None, :]


def noise_scales(steps_part):
    phase = (steps_part.astype(jnp.float32) / 1000.0 + 0.008) / 1.008 * (math.pi / 2.0)
    signal = jnp.cos(phase) * jnp.cos(phase)
    return (jnp.sqrt(signal), jnp.sqrt(1.0 - signal))


def time_features(steps_part):
    half_width = TFREQ // 2
    freqs = jnp.exp(-math.log(10000.0) * jnp.arange(half_width, dtype=jnp.float32) / half_width)
    angles = steps_part.astype(jnp.float32)[:, None] * freqs[None, :]
    return jnp.concatenate([jnp.cos(angles), jnp.sin(angles)], axis=1)


def positions():
    quarter = D // 4
    omega = 1.0 / 10000.0 ** (jnp.arange(quarter, dtype=jnp.float32) / quarter)
    cells = jnp.arange(TOK, dtype=jnp.int32)
    row_pos = (cells // GRID).astype(jnp.float32)[:, None] * omega[None, :]
    col_pos = (cells % GRID).astype(jnp.float32)[:, None] * omega[None, :]
    return jnp.concatenate(
        [jnp.sin(row_pos), jnp.cos(row_pos), jnp.sin(col_pos), jnp.cos(col_pos)], axis=1
    )


def column_blocks():
    return [
        (0, 0, 3 * D),
        (0, 3 * D, 4 * D),
        (0, 4 * D, 4 * D + FF),
        (0, 4 * D + FF, 10 * D + FF),
        (0, 10 * D + FF, 12 * D + FF),
        (0, 12 * D + FF, 13 * D + FF),
        (1, 0, 0),
        (2, 0, TFREQ),
        (2, TFREQ, TFREQ + PATCH_FEAT),
        (2, TFREQ + PATCH_FEAT, TFREQ + PATCH_FEAT + CLASSES),
        (2, TFREQ + PATCH_FEAT + CLASSES, SIDE),
        (3, 0, 0),
    ]


def adam_direction(weight, grad, first, second):
    first_new = BETA_ONE * first + (1.0 - BETA_ONE) * grad
    second_new = BETA_TWO * second + (1.0 - BETA_TWO) * grad * grad
    direction = (
        first_new
        / (1.0 - BETA_ONE**STEP)
        / (jnp.sqrt(second_new / (1.0 - BETA_TWO**STEP)) + EPSILON)
        + DECAY * weight
    )
    return (first_new, second_new, direction)


def direction_kernel(widths, *refs):
    weights, firsts, seconds = refs[0:4], refs[4:8], refs[8:12]
    grads, outs = refs[12:-13], refs[-13:]
    lanes = lax.broadcasted_iota(jnp.int32, (8, 128), 1)
    lines = lax.broadcasted_iota(jnp.int32, (8, 128), 0)
    sums = jnp.zeros((8, 128), jnp.float32)
    pieces = []
    at = 0
    for number, width in enumerate(widths):
        pieces.append((number, at, at + width))
        at += width
    for block, (kind, start, stop) in enumerate(column_blocks()):
        if stop == 0:
            stop = weights[kind].shape[1]
        if kind == 0:
            spans = [
                (grads[number], max(start, low) - low, max(start, low), min(stop, high))
                for number, low, high in pieces
                if max(start, low) < min(stop, high)
            ]
        else:
            spans = [(grads[len(widths) + kind - 1], start, start, stop)]
        for grad_ref, offset, low, high in spans:
            weight = weights[kind][:, low:high]
            first_new, second_new, direction = adam_direction(
                weight,
                grad_ref[:, offset : offset + high - low],
                firsts[kind][:, low:high],
                seconds[kind][:, low:high],
            )
            outs[kind][:, low:high] = first_new
            outs[4 + kind][:, low:high] = second_new
            outs[8 + kind][:, low:high] = direction
            here = lanes == block
            sums = sums + jnp.where(here & (lines == 0), jnp.sum(weight * weight), 0.0)
            sums = sums + jnp.where(here & (lines == 1), jnp.sum(direction * direction), 0.0)
    outs[12][...] = sums


def update_kernel(sums_ref, *refs):
    weights, directions, outs = refs[0:4], refs[4:8], refs[8:]
    norms = jnp.sqrt(sums_ref[...])
    trust = norms[0:1] / norms[1:2]
    line = lax.broadcasted_iota(jnp.int32, (8, 128), 0)
    outs[4][...] = jnp.where(line == 2, trust, norms)
    for block, (kind, start, stop) in enumerate(column_blocks()):
        if stop == 0:
            stop = weights[kind].shape[1]
        factor = RATE * trust[0:1, block : block + 1]
        outs[kind][:, start:stop] = (
            weights[kind][:, start:stop] - factor * directions[kind][:, start:stop]
        )


def whole_kernel(kernel, args, shapes):
    vmem = pl.BlockSpec(memory_space=pltpu.VMEM)
    size = sum(arg.size for arg in args) + sum(math.prod(shape) for shape in shapes)
    return pl.pallas_call(
        kernel,
        out_shape=[jax.ShapeDtypeStruct(shape, jnp.float32) for shape in shapes],
        in_specs=[vmem] * len(args),
        out_specs=[vmem] * len(shapes),
        compiler_params=pltpu.CompilerParams(vmem_limit_bytes=40 * 2**20),
        cost_estimate=pl.CostEstimate(
            flops=10 * size, bytes_accessed=4 * size, transcendentals=size // 8
        ),
    )(*args)


Z_AXIS, Y_AXIS, X_AXIS, CORE, MIX_P, MIX_Q = range(6)


class Grid:
    def __init__(self, count):
        if count == 32:
            sizes = (4, 2, 2, 2)
        elif count == 256:
            sizes = (8, 4, 4, 2)
        else:
            sizes = (count, 1, 1, 1)
        self.count = count
        self.shape = sizes
        self.sizes = sizes + (sizes[X_AXIS], sizes[Y_AXIS])
        index = lax.axis_index(AXIS)
        self.coords = self.split(index)
        mixed = [
            jnp.where(self.coords[CORE] == 0, self.coords[X_AXIS], self.coords[Y_AXIS]),
            jnp.where(self.coords[CORE] == 0, self.coords[Y_AXIS], self.coords[X_AXIS]),
        ]
        self.coords = self.coords + tuple(mixed)

    def split(self, index):
        coords = []
        for size in reversed(self.shape):
            coords.append(index % size)
            index = index // size
        return tuple(reversed(coords))

    def join(self, coords):
        index = 0
        for size, place in zip(self.shape, coords):
            index = index * size + place
        return index

    def move(self, values, axis, change):
        pairs = []
        for source in range(self.count):
            coords = list(self.split(source))
            real = axis
            if axis == MIX_P:
                real = X_AXIS if coords[CORE] == 0 else Y_AXIS
            if axis == MIX_Q:
                real = Y_AXIS if coords[CORE] == 0 else X_AXIS
            coords[real] = change(coords[real])
            pairs.append((source, self.join(coords)))
        return lax.ppermute(values, AXIS, pairs)

    def ahead(self, values, axis, shift):
        size = self.sizes[axis]
        return self.move(values, axis, lambda place: (place - shift) % size)

    def flip(self, values, axis, bit):
        return self.move(values, axis, lambda place: place ^ bit)

    def place(self, axis, shift):
        return (self.coords[axis] + shift) % self.sizes[axis]


def after(values, *others):
    return lax.optimization_barrier((values,) + others)[0] if others else values


def in_order(grid, pieces, axis):
    size = grid.sizes[axis]
    if size == 1:
        return pieces[0][None]
    if size == 2:
        lower = grid.coords[axis] == 0
        return jnp.stack(
            [jnp.where(lower, pieces[0], pieces[1]), jnp.where(lower, pieces[1], pieces[0])]
        )
    twice = jnp.stack(pieces + pieces)
    return lax.dynamic_slice_in_dim(twice, (size - grid.coords[axis]) % size, size, 0)


def gather_small(grid, values, order, before=None):
    for axis in order:
        values = after(values, *(before or {}).get(axis, ()))
        pieces = [values]
        for shift in range(1, grid.sizes[axis]):
            pieces.append(grid.ahead(values, axis, shift))
        values = in_order(grid, pieces, axis)
    return values


def scatter_axis(grid, values, axis, dim):
    def entry(shift):
        return lax.dynamic_index_in_dim(values, grid.place(axis, shift), dim, keepdims=False)

    total = entry(0)
    for shift in range(1, grid.sizes[axis]):
        total = total + grid.ahead(entry(-shift), axis, shift)
    return total


def scatter_small(grid, values, before=None):
    for axis in (CORE, X_AXIS, Y_AXIS, Z_AXIS):
        values = after(values, *(before or {}).get(axis, ()))
        values = scatter_axis(grid, values, axis, axis)
    return values


def sum_small(grid, values):
    for axis in (3, 2, 1, 0):
        bit = 1
        while bit < grid.sizes[axis]:
            values = values + grid.flip(values, axis, bit)
            bit *= 2
    return values


def relative_places(grid, order):
    dims = (CORE,) + tuple(reversed(order))
    number = jnp.arange(grid.count, dtype=jnp.int32)
    shifts = {}
    for axis in reversed(dims):
        shifts[axis] = number % grid.sizes[axis]
        number = number // grid.sizes[axis]
    core = (grid.coords[CORE] + shifts[CORE]) % grid.sizes[CORE]
    x_ahead = jnp.where(core == 0, shifts[MIX_P], shifts[MIX_Q])
    y_ahead = jnp.where(core == 0, shifts[MIX_Q], shifts[MIX_P])
    return grid.join(
        (
            (grid.coords[Z_AXIS] + shifts[Z_AXIS]) % grid.sizes[Z_AXIS],
            (grid.coords[Y_AXIS] + y_ahead) % grid.sizes[Y_AXIS],
            (grid.coords[X_AXIS] + x_ahead) % grid.sizes[X_AXIS],
            core,
        )
    ).astype(jnp.int32)


def place_kernel(moves, where, *refs):
    pieces, full, sems = refs[:-2], refs[-2], refs[-1]
    copies = []
    for number, (piece, entry) in enumerate(moves):
        copies.append(
            pltpu.make_async_copy(
                pieces[piece].at[entry], full.at[where[number]], sems.at[number]
            )
        )
    for copy in copies:
        copy.start()
    for copy in copies:
        copy.wait()


def gather_bulk(grid, shard, order):
    rows, columns = shard.shape
    parts = [shard]
    for axis in order:
        sent = jnp.stack(parts).reshape((-1, rows, columns))
        parts = [sent]
        for _ in range(1, grid.sizes[axis]):
            parts.append(grid.ahead(parts[-1], axis, 1))
            yield parts[-1]
    if grid.sizes[CORE] == 2:
        parts = parts + [grid.ahead(part, CORE, 1) for part in parts]
    where = relative_places(grid, order)
    entries = parts[0].shape[0]
    moves = [(piece, entry) for piece in range(len(parts)) for entry in range(entries)]
    if rows % 16 == 0:
        full = pl.pallas_call(
            partial(place_kernel, moves),
            out_shape=jax.ShapeDtypeStruct((grid.count, rows, columns), shard.dtype),
            in_specs=[pl.BlockSpec(memory_space=pltpu.SMEM)]
            + [pl.BlockSpec(memory_space=pl.ANY)] * len(parts),
            out_specs=pl.BlockSpec(memory_space=pltpu.VMEM),
            scratch_shapes=[pltpu.SemaphoreType.DMA((len(moves),))],
            compiler_params=pltpu.CompilerParams(vmem_limit_bytes=24 * 2**20),
            cost_estimate=pl.CostEstimate(
                flops=0, bytes_accessed=4 * grid.count * rows * columns, transcendentals=0
            ),
        )(where, *parts)
    else:
        stacked = jnp.stack(parts).reshape((grid.count, rows, columns))
        full = jnp.zeros((grid.count, rows, columns), shard.dtype).at[where].set(stacked)
    yield full.reshape(grid.count * rows, columns)


def pick_kernel(base, places, *refs):
    tables, picked, sems = refs[:-2], refs[-2], refs[-1]
    copies = []
    for number in range(picked.shape[0]):
        at = 0
        for table in tables:
            width = table.shape[2]
            copies.append(
                pltpu.make_async_copy(
                    table.at[places[base + number]],
                    picked.at[number, :, pl.ds(at, width)],
                    sems.at[len(copies)],
                )
            )
            at += width
    for copy in copies:
        copy.start()
    for copy in copies:
        copy.wait()


def pick_rows(tables, places, base, count):
    rows = tables[0].shape[1]
    columns = sum(table.shape[2] for table in tables)
    if rows % 16:
        return jnp.concatenate([table[places[base : base + count]] for table in tables], axis=2)
    return pl.pallas_call(
        partial(pick_kernel, base),
        out_shape=jax.ShapeDtypeStruct((count, rows, columns), jnp.bfloat16),
        in_specs=[pl.BlockSpec(memory_space=pltpu.SMEM)]
        + [pl.BlockSpec(memory_space=pl.ANY)] * len(tables),
        out_specs=pl.BlockSpec(memory_space=pltpu.VMEM),
        scratch_shapes=[pltpu.SemaphoreType.DMA((count * len(tables),))],
        compiler_params=pltpu.CompilerParams(vmem_limit_bytes=24 * 2**20),
        cost_estimate=pl.CostEstimate(
            flops=0, bytes_accessed=4 * count * rows * columns, transcendentals=0
        ),
    )(places, *tables)


def scatter_bulk(grid, tables, order):
    rows = tables[0].shape[0] // grid.count
    columns = sum(table.shape[1] for table in tables)
    places = relative_places(grid, order)
    tables = [table.reshape(grid.count, rows, table.shape[1]) for table in tables]
    kept = grid.count // grid.sizes[CORE]
    axes = tuple(reversed(order))
    dims = tuple(grid.sizes[axis] for axis in axes) + (rows, columns)
    terms = []
    for core in reversed(range(grid.sizes[CORE])):
        picked = pick_rows(tables, places, core * kept, kept)
        if core > 0:
            picked = grid.ahead(picked, CORE, core)
            yield picked
        terms.append(picked.reshape(dims))

    def entry(place):
        return sum(term[place].astype(jnp.float32) for term in terms)

    for axis in axes:
        size = grid.sizes[axis]
        total = None
        for step in range(1, size):
            total = entry(step) if total is None else total.astype(jnp.float32) + entry(step)
            total = grid.ahead(total.astype(jnp.bfloat16), axis, 1)
            yield total
        terms = [term[0] for term in terms] + ([] if total is None else [total])
    yield sum(term.astype(jnp.float32) for term in terms)


def last(steps):
    return list(steps)[-1]


HEAD_COLS = 4 * HEAD_DIM


def head_probs(query, key):
    scores = dot_tail(query, key) * HEAD_DIM ** (-0.5)
    weights = jnp.exp(scores - jnp.max(scores, axis=-1, keepdims=True))
    return weights * (1.0 / jnp.sum(weights, axis=-1, keepdims=True))


def head_masks():
    lanes = lax.broadcasted_iota(jnp.int32, (1, 2 * HEAD_DIM), 1)
    first = lanes < HEAD_DIM
    return first, (first.astype(jnp.bfloat16), (~first).astype(jnp.bfloat16))


def attend_kernel(query_ref, key_ref, value_ref, mixed_ref):
    first, masks = head_masks()
    for at in range(0, HEAD_COLS, 2 * HEAD_DIM):
        pair = slice(at, at + 2 * HEAD_DIM)
        query, key, value = query_ref[:, pair], key_ref[:, pair], value_ref[:, pair]
        mixed = [
            matmul(head_probs(query * mask, key).astype(jnp.bfloat16), value) for mask in masks
        ]
        mixed_ref[:, pair] = jnp.where(first, mixed[0], mixed[1]).astype(jnp.bfloat16)


def attend_back_kernel(query_ref, key_ref, value_ref, grad_ref, out_ref, bias_ref):
    first, masks = head_masks()

    @pl.when(pl.program_id(1) == 0)
    def _():
        bias_ref[...] = jnp.zeros_like(bias_ref)

    for at in range(0, HEAD_COLS, 2 * HEAD_DIM):
        pair = slice(at, at + 2 * HEAD_DIM)
        query, key, value = query_ref[:, pair], key_ref[:, pair], value_ref[:, pair]
        grad = grad_ref[:, pair]
        parts = []
        for mask in masks:
            probs = head_probs(query * mask, key)
            grad_probs = dot_tail(grad * mask, value)
            inner = jnp.sum(probs * grad_probs, axis=-1, keepdims=True)
            grad_scores = (probs * (grad_probs - inner)).astype(jnp.bfloat16)
            parts.append(
                (
                    matmul(grad_scores, key) * HEAD_DIM ** (-0.5),
                    dot_head(grad_scores, query) * HEAD_DIM ** (-0.5),
                    dot_head(probs.astype(jnp.bfloat16), grad),
                )
            )
        whole = [jnp.where(first, one, two) for one, two in zip(*parts)]
        for index in range(3):
            out_ref[index, :, pair] = whole[index].astype(jnp.bfloat16)
        bias_ref[0:1, pair] += jnp.sum(whole[0], axis=0, keepdims=True)
        bias_ref[1:2, pair] += jnp.sum(whole[2], axis=0, keepdims=True)


def head_specs():
    groups = D // HEAD_COLS
    return [
        pl.BlockSpec((TOK, HEAD_COLS), lambda group, image, part=part: (image, part * groups + group))
        for part in range(3)
    ]


def attend(proj):
    count = proj.shape[0] // TOK
    flops = 4 * count * HEADS * TOK * TOK * HEAD_DIM
    return pl.pallas_call(
        attend_kernel,
        grid=(D // HEAD_COLS, count),
        out_shape=jax.ShapeDtypeStruct((proj.shape[0], D), jnp.bfloat16),
        in_specs=head_specs(),
        out_specs=pl.BlockSpec((TOK, HEAD_COLS), lambda group, image: (image, group)),
        compiler_params=pltpu.CompilerParams(vmem_limit_bytes=24 * 2**20),
        cost_estimate=pl.CostEstimate(
            flops=4 * flops, bytes_accessed=8 * proj.size, transcendentals=flops // 256
        ),
    )(proj, proj, proj)


def attend_back(proj, grad_mixed):
    count = proj.shape[0] // TOK
    flops = 12 * count * HEADS * TOK * TOK * HEAD_DIM
    block = pl.BlockSpec((TOK, HEAD_COLS), lambda group, image: (image, group))
    return pl.pallas_call(
        attend_back_kernel,
        grid=(D // HEAD_COLS, count),
        out_shape=[
            jax.ShapeDtypeStruct((3, proj.shape[0], D), jnp.bfloat16),
            jax.ShapeDtypeStruct((8, D), jnp.float32),
        ],
        in_specs=head_specs() + [block],
        out_specs=[
            pl.BlockSpec((3, TOK, HEAD_COLS), lambda group, image: (0, image, group)),
            pl.BlockSpec((8, HEAD_COLS), lambda group, image: (0, group)),
        ],
        compiler_params=pltpu.CompilerParams(vmem_limit_bytes=24 * 2**20),
        cost_estimate=pl.CostEstimate(
            flops=3 * flops, bytes_accessed=16 * proj.size, transcendentals=flops // 512
        ),
    )(proj, proj, proj, grad_mixed)


OUTER = (MIX_P, Z_AXIS, MIX_Q)


def per_device(
    latents,
    noise_draw,
    timesteps,
    labels,
    weights_in,
    weights_down,
    weights_side,
    biases,
    first_in,
    first_down,
    first_side,
    first_bias,
    second_in,
    second_down,
    second_side,
    second_bias,
):
    bf16 = jnp.bfloat16
    count_all = lax.axis_size(AXIS)
    grid = Grid(count_all)
    sizes = grid.shape
    count = latents.shape[0]
    rows_all = count * TOK
    image_total = count * count_all
    rows = weights_in.shape[0]
    bias_rows = biases.shape[0]
    my_rows = lax.axis_index(AXIS) * rows
    masters = (weights_in, weights_down, weights_side, biases)
    in_bf = weights_in.astype(bf16)
    down_bf = weights_down.astype(bf16)
    side_bf = weights_side.astype(bf16)
    t_first = side_bf[:, :TFREQ]
    patch_at = TFREQ
    class_at = TFREQ + PATCH_FEAT
    head_at = class_at + CLASSES
    w_class = side_bf[:, class_at:head_at]
    w_mods = in_bf[:, 4 * D + FF : 12 * D + FF]
    w_time = in_bf[:, 12 * D + FF :]

    numbers = jnp.concatenate([timesteps, labels])
    packed = jnp.concatenate(
        [
            biases.astype(bf16),
            side_bf[:, patch_at:class_at].reshape(-1),
            side_bf[:, head_at:].reshape(-1),
            (numbers // 32).astype(bf16),
            (numbers % 32).astype(bf16),
        ]
    )
    width = packed.shape[0]
    tall = -(-width // (SMALL_ROWS * 128)) * SMALL_ROWS
    packed = jnp.pad(packed, (0, tall * 128 - width)).reshape(tall, 128)
    head_in = weights_in[:, : 4 * D].astype(bf16)
    table_qkvo = lax.all_gather(head_in, AXIS, axis=0, tiled=True)
    half = FF // 2
    up_bf = weights_in[:, 4 * D : 4 * D + FF].astype(bf16)
    table_first = lax.all_gather(up_bf[:, :half], AXIS, axis=0, tiled=True)
    get_down = gather_bulk(grid, down_bf, OUTER)
    get_up = gather_bulk(grid, up_bf[:, half:], OUTER)
    before = {Y_AXIS: [next(get_down), next(get_up)]}
    spread_all = gather_small(grid, packed, (CORE, X_AXIS, Y_AXIS, Z_AXIS), before)
    spread_all = spread_all.reshape(count_all, tall * 128)
    bias_full = spread_all[:, :bias_rows].reshape(-1).astype(jnp.float32)
    at = bias_rows
    w_patch = spread_all[:, at : at + rows * PATCH_FEAT].reshape(D, PATCH_FEAT)
    at += rows * PATCH_FEAT
    w_head = spread_all[:, at : at + rows * PATCH_FEAT].reshape(D, PATCH_FEAT)
    at += rows * PATCH_FEAT
    numbers = spread_all[:, at : at + 4 * count].astype(jnp.float32)
    numbers = numbers[:, : 2 * count] * 32.0 + numbers[:, 2 * count :]
    numbers = numbers.reshape(sizes + (2 * count,))
    numbers = jnp.stack(
        [numbers[:, :, :, core].transpose((1, 2, 0, 3) if core else (2, 1, 0, 3)) for core in range(sizes[CORE])]
    ).reshape(count_all, 2 * count)
    steps_all = numbers[:, :count].reshape(image_total)
    labels_all = numbers[:, count:].reshape(image_total).astype(jnp.int32)

    b_qkv = jnp.concatenate([bias_full[:D], jnp.zeros((D,), jnp.float32), bias_full[D : 2 * D]])
    b_out = bias_full[2 * D : 3 * D]
    b_up = bias_full[3 * D : 3 * D + FF]
    b_down = bias_full[3 * D + FF : 4 * D + FF]
    b_mods = bias_full[4 * D + FF : 12 * D + FF]
    b_tfirst = lax.dynamic_slice_in_dim(bias_full[12 * D + FF : 13 * D + FF], my_rows, rows)
    b_time = lax.dynamic_slice_in_dim(bias_full[13 * D + FF : 14 * D + FF], my_rows, rows)
    b_patch = bias_full[14 * D + FF :]

    feats = time_features(steps_all).astype(bf16)
    time_pre = dot_tail(t_first, feats) + b_tfirst[:, None]
    time_act = jax.nn.silu(time_pre).astype(bf16)
    onehot = labels_all[:, None] == jnp.arange(CLASSES, dtype=jnp.int32)[None, :]
    cond_part = lax.dot_general(
        w_time, time_act, (((0,), (0,)), ((), ())), preferred_element_type=jnp.float32
    )
    cond = cond_part.reshape(sizes + (rows, image_total))
    before = {CORE: [next(get_down), next(get_up)], Z_AXIS: [next(get_down), next(get_up)]}
    cond = scatter_small(grid, cond, before)
    cond = cond + b_time[:, None] + dot_tail(w_class, onehot.astype(bf16))
    cond_act = jax.nn.silu(cond).astype(bf16)

    mods = dot_head(cond_act, w_mods)
    mods = mods.reshape(sizes[CORE], sizes[X_AXIS], sizes[Y_AXIS], sizes[Z_AXIS] * count, 8 * D)
    mods = scatter_axis(grid, mods, CORE, 0)
    mods = scatter_axis(grid, mods, MIX_P, 0)
    ready = [next(get_down), next(get_up)]
    mods = scatter_axis(grid, after(mods, *ready), MIX_Q, 0)
    mods = mods.reshape(sizes[Z_AXIS], count * 8 * D // 128, 128)
    mods = scatter_axis(grid, mods, Z_AXIS, 0).reshape(count, 8 * D) + b_mods
    shift_a, scale_a, gate_a, shift_b, scale_b, gate_b, shift_f, scale_f = jnp.split(
        mods, 8, axis=1
    )

    w_qkv, w_out = table_qkvo[:, : 3 * D], table_qkvo[:, 3 * D :]

    signal, spread = noise_scales(timesteps)
    noise_rows = noise_draw.astype(jnp.float32)
    noisy = signal[:, None, None] * latents.astype(jnp.float32) + spread[:, None, None] * noise_rows
    noisy = noisy.astype(bf16).reshape(rows_all, PATCH_FEAT)
    hidden = dot_tail(noisy, w_patch) + b_patch + jnp.tile(positions(), (count, 1))
    resid_in = hidden.reshape(count, TOK, D)
    normed_a = modulate(resid_in, shift_a, scale_a).astype(bf16).reshape(rows_all, D)
    proj = (matmul(normed_a, w_qkv) + b_qkv).astype(bf16)
    proj = after(proj, next(get_down), next(get_up))
    mixed = attend(proj)
    attended = (matmul(mixed, w_out) + b_out).reshape(count, TOK, D)
    resid_mid = resid_in + gate_a[:, None, :] * attended
    normed_b = modulate(resid_mid, shift_b, scale_b).astype(bf16).reshape(rows_all, D)
    table_up, table_down = (table_first, last(get_up)), last(get_down)
    uppers = [
        matmul(normed_b, part) + b_up[index * half : (index + 1) * half]
        for index, part in enumerate(table_up)
    ]
    actives = [jax.nn.gelu(upper, approximate=True).astype(bf16) for upper in uppers]
    active = jnp.concatenate(actives, axis=1)
    lowered = matmul(active, table_down) + b_down
    lowered = lowered.reshape(count, TOK, D)
    resid_out = resid_mid + gate_b[:, None, :] * lowered
    normed_c = modulate(resid_out, shift_f, scale_f).astype(bf16).reshape(rows_all, D)
    predicted = matmul(normed_c, w_head)
    error = predicted - noise_rows.reshape(rows_all, PATCH_FEAT)
    loss_local = jnp.sum(error * error)
    grad_pred = (2.0 / image_total * error).astype(bf16)

    grad_head = dot_head(normed_c, grad_pred)
    grad_normed_c = dot_tail(grad_pred, w_head).reshape(count, TOK, D)
    _, pull_final = jax.vjp(modulate, resid_out, shift_f, scale_f)
    grad_out, grad_shift_f, grad_scale_f = pull_final(grad_normed_c)
    grad_gate_b = jnp.sum(grad_out * lowered, axis=1)
    grad_lowered = (grad_out * gate_b[:, None, :]).reshape(rows_all, D)
    grad_b_down = jnp.sum(grad_lowered, axis=0)
    lowered_bf = grad_lowered.astype(bf16)
    grad_w_down = dot_head(active, lowered_bf).astype(bf16)
    sum_down = lax.psum_scatter(grad_w_down, AXIS, scatter_dimension=0, tiled=True)
    lowered_bf = after(lowered_bf, grad_w_down)
    grad_active = dot_tail(lowered_bf, table_down)
    gelu = partial(jax.nn.gelu, approximate=True)
    grad_uppers = [
        jax.vjp(gelu, upper)[1](grad_active[:, index * half : (index + 1) * half])[0]
        for index, upper in enumerate(uppers)
    ]
    grad_b_up = jnp.concatenate([jnp.sum(part, axis=0) for part in grad_uppers])
    upper_bf = [part.astype(bf16) for part in grad_uppers]
    grad_w_up = [dot_head(normed_b, part).astype(bf16) for part in upper_bf]
    put_up = scatter_bulk(grid, grad_w_up, OUTER)
    upper_bf[0] = after(upper_bf[0], *grad_w_up)
    grad_normed_b = (
        dot_tail(upper_bf[0], table_up[0]) + dot_tail(upper_bf[1], table_up[1])
    ).reshape(count, TOK, D)
    grad_normed_b = after(grad_normed_b, next(put_up))
    _, pull_mid = jax.vjp(modulate, resid_mid, shift_b, scale_b)
    grad_mid_norm, grad_shift_b, grad_scale_b = pull_mid(grad_normed_b)
    grad_mid = grad_out + grad_mid_norm
    grad_gate_a = jnp.sum(grad_mid * attended, axis=1)
    grad_attended = (grad_mid * gate_a[:, None, :]).reshape(rows_all, D)
    grad_b_out = jnp.sum(grad_attended, axis=0)
    attended_bf = grad_attended.astype(bf16)
    grad_w_out = dot_head(mixed, attended_bf).astype(bf16)
    grad_mixed = dot_tail(attended_bf, w_out).astype(bf16)
    proj_bf, proj_sums = attend_back(proj, grad_mixed)
    grad_b_query, grad_b_value = proj_sums[0], proj_sums[1]
    grad_qkv = [dot_head(normed_a, proj_bf[part]).astype(bf16) for part in range(3)]
    put_vo = scatter_bulk(grid, [grad_qkv[2], grad_w_out], OUTER)
    put_qk = scatter_bulk(grid, grad_qkv[:2], OUTER)
    proj_bf = after(proj_bf, *grad_qkv, next(put_up))
    grad_normed_a = sum(
        dot_tail(proj_bf[part], w_qkv[:, part * D : (part + 1) * D]) for part in range(3)
    ).reshape(count, TOK, D)
    grad_normed_a = after(grad_normed_a, next(put_up), next(put_vo), next(put_qk))
    _, pull_first = jax.vjp(modulate, resid_in, shift_a, scale_a)
    grad_in_norm, grad_shift_a, grad_scale_a = pull_first(grad_normed_a)
    grad_hidden = (grad_mid + grad_in_norm).reshape(rows_all, D)
    grad_b_patch = jnp.sum(grad_hidden, axis=0)
    grad_w_patch = dot_head(grad_hidden.astype(bf16), noisy)

    grad_mods = jnp.concatenate(
        [
            grad_shift_a,
            grad_scale_a,
            grad_gate_a,
            grad_shift_b,
            grad_scale_b,
            grad_gate_b,
            grad_shift_f,
            grad_scale_f,
        ],
        axis=1,
    )
    grad_b_mods = jnp.sum(grad_mods, axis=0)
    before = {
        MIX_Q: [next(put_up), next(put_vo)],
        CORE: [next(put_qk), next(put_up)],
    }
    mods_bf = grad_mods.astype(bf16).reshape(-1, 128)
    mods_bf = gather_small(grid, mods_bf, (Z_AXIS, MIX_Q, MIX_P, CORE), before)
    mods_bf = mods_bf.reshape(image_total, 8 * D)
    grad_w_mods = matmul(cond_act, mods_bf)
    grad_cond_act = dot_tail(w_mods, mods_bf)
    grad_cond = jax.vjp(jax.nn.silu, cond)[1](grad_cond_act)[0]
    grad_w_class = jnp.dot(
        grad_cond,
        onehot.astype(jnp.float32),
        precision=lax.Precision.HIGHEST,
        preferred_element_type=jnp.float32,
    )
    grad_b_time = jnp.sum(grad_cond, axis=1)
    before = {X_AXIS: [next(put_vo), next(put_up)], Z_AXIS: [next(put_qk)]}
    cond_bf = gather_small(grid, grad_cond.astype(bf16), (CORE, X_AXIS, Y_AXIS, Z_AXIS), before)
    cond_bf = cond_bf.reshape(D, image_total)
    grad_w_time = dot_tail(time_act, cond_bf)
    grad_time_act = matmul(w_time, cond_bf)
    grad_time_pre = jax.vjp(jax.nn.silu, time_pre)[1](grad_time_act)[0]
    grad_b_tfirst = jnp.sum(grad_time_pre, axis=1)
    grad_t_first = matmul(grad_time_pre.astype(bf16), feats)

    def spread_rows(part):
        return lax.dynamic_update_slice(jnp.zeros((D,), jnp.float32), part, (my_rows,))

    grad_bias = jnp.concatenate(
        [
            grad_b_query,
            grad_b_value,
            grad_b_out,
            grad_b_up,
            grad_b_down,
            grad_b_mods,
            spread_rows(grad_b_tfirst),
            spread_rows(grad_b_time),
            grad_b_patch,
        ]
    )
    small = jnp.concatenate(
        [
            grad_bias.reshape(count_all, bias_rows),
            grad_w_patch.reshape(count_all, rows * PATCH_FEAT),
            grad_head.reshape(count_all, rows * PATCH_FEAT),
        ],
        axis=1,
    )
    tall = -(-small.shape[1] // 1024) * 8
    small = jnp.pad(small, ((0, 0), (0, tall * 128 - small.shape[1])))
    before = {
        CORE: [next(put_vo)],
        X_AXIS: [next(put_qk)],
        Y_AXIS: [next(put_vo)],
        Z_AXIS: [next(put_qk)],
    }
    small = scatter_small(grid, small.reshape(sizes + (tall, 128)), before).reshape(-1)
    at = bias_rows
    sum_patch = small[at : at + rows * PATCH_FEAT].reshape(rows, PATCH_FEAT)
    at += rows * PATCH_FEAT
    sum_head = small[at : at + rows * PATCH_FEAT].reshape(rows, PATCH_FEAT)

    sum_vo, sum_qk, sum_up = last(put_vo), last(put_qk), last(put_up)
    sum_down = sum_down.astype(jnp.float32)
    grads_in = (sum_qk, sum_vo, sum_up, grad_w_mods, grad_w_time)
    grads_other = (
        sum_down,
        jnp.concatenate([grad_t_first, sum_patch, grad_w_class, sum_head], axis=1),
        small[None, :bias_rows],
    )
    masters = (weights_in, weights_down, weights_side, biases[None])
    firsts = (first_in, first_down, first_side, first_bias[None])
    seconds = (second_in, second_down, second_side, second_bias[None])
    shapes = [master.shape for master in masters]
    results = whole_kernel(
        partial(direction_kernel, [grad.shape[1] for grad in grads_in]),
        masters + firsts + seconds + grads_in + grads_other,
        shapes * 3 + [(8, 128)],
    )
    loss_spot = jnp.arange(8, dtype=jnp.int32)[:, None] == 3
    sums = sum_small(grid, results[12] + jnp.where(loss_spot, loss_local, 0.0))
    updated = whole_kernel(
        update_kernel, (sums,) + masters + tuple(results[8:12]), shapes + [(8, 128)]
    )
    norms = updated[4]
    return (
        sums[3, 0],
        updated[0],
        updated[1],
        updated[2],
        updated[3][0],
        results[0],
        results[1],
        results[2],
        results[3][0],
        results[4],
        results[5],
        results[6],
        results[7][0],
        norms[2, :12],
        norms[0, :12],
        norms[1, :12],
    )


def solution(mesh):
    placed = (
        P("fsdp", None, None),
        P("fsdp", None, None),
        P("fsdp"),
        P("fsdp"),
        P("fsdp", None),
        P("fsdp", None),
        P("fsdp", None),
        P("fsdp"),
        P("fsdp", None),
        P("fsdp", None),
        P("fsdp", None),
        P("fsdp"),
        P("fsdp", None),
        P("fsdp", None),
        P("fsdp", None),
        P("fsdp"),
    )
    return jax.shard_map(
        per_device,
        mesh=mesh,
        in_specs=placed,
        out_specs=(
            P(),
            P("fsdp", None),
            P("fsdp", None),
            P("fsdp", None),
            P("fsdp"),
            P("fsdp", None),
            P("fsdp", None),
            P("fsdp", None),
            P("fsdp"),
            P("fsdp", None),
            P("fsdp", None),
            P("fsdp", None),
            P("fsdp"),
            P(),
            P(),
            P(),
        ),
        check_vma=False,
    )
```

```python
from functools import partial
import math

import jax
import jax.numpy as jnp
from jax import lax
from jax.experimental import pallas as pl
from jax.experimental.pallas import tpu as pltpu
from jax.sharding import PartitionSpec as P

D = 1024
HEADS = 16
HEAD_DIM = 64
FF = 4096
CLASSES = 1000
PATCH_FEAT = 16
TFREQ = 256
GRID = 16
TOK = 256
MICRO = 2
STEP = 10
IMG_DEV = 1
SIDE = 1288


BETA_ONE = 0.5
BETA_TWO = 0.5
EPSILON = 1e-06
DECAY = 0.01
RATE = 0.25
NORM_EPS = 1e-06
SMALL_ROWS = 16
AXIS = "fsdp"


def matmul(left, right):
    return jnp.dot(left, right, preferred_element_type=jnp.float32)


def dot_tail(left, right):
    return lax.dot_general(
        left, right, (((1,), (1,)), ((), ())), preferred_element_type=jnp.float32
    )


def dot_head(left, right):
    return lax.dot_general(
        left, right, (((0,), (0,)), ((), ())), preferred_element_type=jnp.float32
    )


def layer_norm(values):
    center = values - jnp.mean(values, axis=-1, keepdims=True)
    return center * lax.rsqrt(jnp.mean(center * center, axis=-1, keepdims=True) + NORM_EPS)


def modulate(values, shift, scale):
    return layer_norm(values) * (1.0 + scale[:, None, :]) + shift[:, None, :]


def noise_scales(steps_part):
    phase = (steps_part.astype(jnp.float32) / 1000.0 + 0.008) / 1.008 * (math.pi / 2.0)
    signal = jnp.cos(phase) * jnp.cos(phase)
    return (jnp.sqrt(signal), jnp.sqrt(1.0 - signal))


def time_features(steps_part):
    half_width = TFREQ // 2
    freqs = jnp.exp(-math.log(10000.0) * jnp.arange(half_width, dtype=jnp.float32) / half_width)
    angles = steps_part.astype(jnp.float32)[:, None] * freqs[None, :]
    return jnp.concatenate([jnp.cos(angles), jnp.sin(angles)], axis=1)


def positions():
    quarter = D // 4
    omega = 1.0 / 10000.0 ** (jnp.arange(quarter, dtype=jnp.float32) / quarter)
    cells = jnp.arange(TOK, dtype=jnp.int32)
    row_pos = (cells // GRID).astype(jnp.float32)[:, None] * omega[None, :]
    col_pos = (cells % GRID).astype(jnp.float32)[:, None] * omega[None, :]
    return jnp.concatenate(
        [jnp.sin(row_pos), jnp.cos(row_pos), jnp.sin(col_pos), jnp.cos(col_pos)], axis=1
    )


def column_blocks():
    return [
        (0, 0, 3 * D),
        (0, 3 * D, 4 * D),
        (0, 4 * D, 4 * D + FF),
        (0, 4 * D + FF, 10 * D + FF),
        (0, 10 * D + FF, 12 * D + FF),
        (0, 12 * D + FF, 13 * D + FF),
        (1, 0, 0),
        (2, 0, TFREQ),
        (2, TFREQ, TFREQ + PATCH_FEAT),
        (2, TFREQ + PATCH_FEAT, TFREQ + PATCH_FEAT + CLASSES),
        (2, TFREQ + PATCH_FEAT + CLASSES, SIDE),
        (3, 0, 0),
    ]


def adam_direction(weight, grad, first, second):
    first_new = BETA_ONE * first + (1.0 - BETA_ONE) * grad
    second_new = BETA_TWO * second + (1.0 - BETA_TWO) * grad * grad
    direction = (
        first_new
        / (1.0 - BETA_ONE**STEP)
        / (jnp.sqrt(second_new / (1.0 - BETA_TWO**STEP)) + EPSILON)
        + DECAY * weight
    )
    return (first_new, second_new, direction)


def column_chunks(edges, shapes):
    blocks = column_blocks()
    chunks = []
    for kind in (1, 2, 3):
        parts = [
            (block, start, stop or shapes[kind][1])
            for block, (other, start, stop) in enumerate(blocks)
            if other == kind
        ]
        chunks.append((kind, len(edges) - 2 + kind, 0, 0, shapes[kind][1], parts))
    for number in range(len(edges) - 1):
        for low in range(edges[number], edges[number + 1], 4 * D):
            high = min(low + 4 * D, edges[number + 1])
            parts = [
                (block, max(start, low), min(stop, high))
                for block, (kind, start, stop) in enumerate(blocks)
                if kind == 0 and max(start, low) < min(stop, high)
            ]
            chunks.append((0, number, low - edges[number], low, high, parts))
    return chunks


def span(ref, low, high):
    return ref if (low, high) == (0, ref.shape[1]) else ref.at[:, pl.ds(low, high - low)]


def direction_kernel(edges, shapes, *refs):
    weights, firsts, seconds = refs[0:4], refs[4:8], refs[8:12]
    count = len(edges) - 1 + 3
    grads, outs = refs[12 : 12 + count], refs[12 + count : 25 + count]
    scratch, in_sems, out_sems = refs[25 + count : -2], refs[-2], refs[-1]
    lanes = lax.broadcasted_iota(jnp.int32, (8, 128), 1)
    lines = lax.broadcasted_iota(jnp.int32, (8, 128), 0)
    sums = jnp.zeros((8, 128), jnp.float32)
    chunks = column_chunks(edges, shapes)
    loads, stores = [], []
    for index, (kind, number, at, low, high, _) in enumerate(chunks):
        sources = [span(group[kind], low, high) for group in (weights, firsts, seconds)]
        sources.append(span(grads[number], at, at + high - low))
        held = scratch[7 * kind : 7 * kind + 4]
        loads.append(
            [
                pltpu.make_async_copy(
                    source, span(held[slot], low, high), in_sems.at[index, slot]
                )
                for slot, source in enumerate(sources)
            ]
        )
        for copy in loads[-1]:
            copy.start()
    for index, (kind, _, _, low, high, parts) in enumerate(chunks):
        held, made = scratch[7 * kind : 7 * kind + 4], scratch[7 * kind + 4 : 7 * kind + 7]
        for copy in loads[index]:
            copy.wait()
        for block, start, stop in parts:
            columns = slice(start, stop)
            weight = held[0][:, columns]
            results = adam_direction(
                weight, held[3][:, columns], held[1][:, columns], held[2][:, columns]
            )
            for target, result in zip(made, results):
                target[:, columns] = result
            here = lanes == block
            sums = sums + jnp.where(here & (lines == 0), jnp.sum(weight * weight), 0.0)
            sums = sums + jnp.where(here & (lines == 1), jnp.sum(results[2] * results[2]), 0.0)
        for slot in range(3):
            stores.append(
                pltpu.make_async_copy(
                    span(made[slot], low, high),
                    span(outs[4 * slot + kind], low, high),
                    out_sems.at[index, slot],
                )
            )
            stores[-1].start()
    outs[12][...] = sums
    for copy in stores:
        copy.wait()


def lamb_call(kernel, args, first_specs, shapes, held, slots):
    any_space = pl.BlockSpec(memory_space=pl.ANY)
    size = sum(arg.size for arg in args) + sum(math.prod(shape) for shape in shapes)
    return pl.pallas_call(
        kernel,
        out_shape=[jax.ShapeDtypeStruct(shape, jnp.float32) for shape in shapes],
        in_specs=first_specs + [any_space] * (len(args) - len(first_specs)),
        out_specs=[any_space] * (len(shapes) - 1) + [pl.BlockSpec(memory_space=pltpu.VMEM)],
        scratch_shapes=[pltpu.VMEM(shape, jnp.float32) for shape in held]
        + [pltpu.SemaphoreType.DMA(slot) for slot in slots],
        compiler_params=pltpu.CompilerParams(vmem_limit_bytes=60 * 2**20),
        cost_estimate=pl.CostEstimate(
            flops=10 * size, bytes_accessed=4 * size, transcendentals=size // 8
        ),
    )(*args)


def directions(masters, firsts, seconds, grads_in, grads_other):
    edges = [0]
    for grad in grads_in:
        edges.append(edges[-1] + grad.shape[1])
    shapes = [master.shape for master in masters]
    return lamb_call(
        partial(direction_kernel, edges, shapes),
        masters + firsts + seconds + grads_in + grads_other,
        [],
        shapes * 3 + [(8, 128)],
        [shape for shape in shapes for _ in range(7)],
        [(len(column_chunks(edges, shapes)), slot) for slot in (4, 3)],
    )


def update_kernel(edges, shapes, sums_ref, *refs):
    weights, steps, outs = refs[0:4], refs[4:8], refs[8:13]
    scratch, in_sems, out_sems = refs[13:-2], refs[-2], refs[-1]
    norms = jnp.sqrt(sums_ref[...])
    trust = norms[0:1] / norms[1:2]
    line = lax.broadcasted_iota(jnp.int32, (8, 128), 0)
    outs[4][...] = jnp.where(line == 2, trust, norms)
    chunks = column_chunks(edges, shapes)
    loads, stores = [], []
    for index, (kind, _, _, low, high, _) in enumerate(chunks):
        loads.append(
            [
                pltpu.make_async_copy(
                    span(source[kind], low, high),
                    span(scratch[3 * kind + slot], low, high),
                    in_sems.at[index, slot],
                )
                for slot, source in enumerate((weights, steps))
            ]
        )
        for copy in loads[-1]:
            copy.start()
    for index, (kind, _, _, low, high, parts) in enumerate(chunks):
        held, made = scratch[3 * kind : 3 * kind + 2], scratch[3 * kind + 2]
        for copy in loads[index]:
            copy.wait()
        for block, start, stop in parts:
            columns = slice(start, stop)
            factor = RATE * trust[0:1, block : block + 1]
            made[:, columns] = held[0][:, columns] - factor * held[1][:, columns]
        stores.append(
            pltpu.make_async_copy(
                span(made, low, high), span(outs[kind], low, high), out_sems.at[index]
            )
        )
        stores[-1].start()
    for copy in stores:
        copy.wait()


def updates(sums, masters, steps):
    edges = [0, masters[0].shape[1]]
    shapes = [master.shape for master in masters]
    chunks = len(column_chunks(edges, shapes))
    return lamb_call(
        partial(update_kernel, edges, shapes),
        (sums,) + masters + tuple(steps),
        [pl.BlockSpec(memory_space=pltpu.VMEM)],
        shapes + [(8, 128)],
        [shape for shape in shapes for _ in range(3)],
        [(chunks, 2), (chunks,)],
    )


Z_AXIS, Y_AXIS, X_AXIS, CORE, MIX_P, MIX_Q = range(6)


class Grid:
    def __init__(self, count):
        if count == 32:
            sizes = (4, 2, 2, 2)
        elif count == 256:
            sizes = (8, 4, 4, 2)
        else:
            sizes = (count // 2, 1, 1, 2)
        self.count = count
        self.shape = sizes
        self.sizes = sizes + (sizes[X_AXIS], sizes[Y_AXIS])
        index = lax.axis_index(AXIS)
        self.coords = self.split(index)
        mixed = [
            jnp.where(self.coords[CORE] == 0, self.coords[X_AXIS], self.coords[Y_AXIS]),
            jnp.where(self.coords[CORE] == 0, self.coords[Y_AXIS], self.coords[X_AXIS]),
        ]
        self.coords = self.coords + tuple(mixed)

    def split(self, index):
        coords = []
        for size in reversed(self.shape):
            coords.append(index % size)
            index = index // size
        return tuple(reversed(coords))

    def join(self, coords):
        index = 0
        for size, place in zip(self.shape, coords):
            index = index * size + place
        return index

    def move(self, values, axis, change):
        pairs = []
        for source in range(self.count):
            coords = list(self.split(source))
            real = axis
            if axis == MIX_P:
                real = X_AXIS if coords[CORE] == 0 else Y_AXIS
            if axis == MIX_Q:
                real = Y_AXIS if coords[CORE] == 0 else X_AXIS
            coords[real] = change(coords[real])
            pairs.append((source, self.join(coords)))
        return lax.ppermute(values, AXIS, pairs)

    def ahead(self, values, axis, shift):
        size = self.sizes[axis]
        return self.move(values, axis, lambda place: (place - shift) % size)

    def flip(self, values, axis, bit):
        return self.move(values, axis, lambda place: place ^ bit)

    def place(self, axis, shift):
        return (self.coords[axis] + shift) % self.sizes[axis]


def after(values, *others):
    return lax.optimization_barrier((values,) + others)[0] if others else values


def gather_small(grid, values, order):
    for axis in order:
        values = values[None]
        bit = 1
        while bit < grid.sizes[axis]:
            other = grid.flip(values, axis, bit)
            lower = grid.coords[axis] // bit % 2 == 0
            values = jnp.concatenate(
                [jnp.where(lower, values, other), jnp.where(lower, other, values)]
            )
            bit *= 2
    return values


def scatter_axis(grid, values, axis, dim):
    bit = grid.sizes[axis]
    while bit > 1:
        bit //= 2
        upper = grid.coords[axis] // bit % 2
        kept = lax.dynamic_slice_in_dim(values, upper * bit, bit, dim)
        sent = lax.dynamic_slice_in_dim(values, (1 - upper) * bit, bit, dim)
        values = kept + grid.flip(sent, axis, bit)
    return lax.squeeze(values, (dim,))


def scatter_small(grid, values):
    for axis in (CORE, X_AXIS, Y_AXIS, Z_AXIS):
        values = scatter_axis(grid, values, axis, axis)
    return values


def gather_and_scatter(grid, values, table, ready):
    turned = jnp.swapaxes(table, Y_AXIS, X_AXIS)
    table = jnp.where(grid.coords[CORE] == 0, table, turned)
    for axis in (Z_AXIS, MIX_Q, MIX_P, CORE):
        values = values[None]
        bit = 1
        while bit < grid.sizes[axis]:
            lower = grid.coords[axis] // bit % 2 == 0
            halves = table.reshape((table.shape[0] // 2, 2) + table.shape[1:])
            even, odd = halves[:, 0], halves[:, 1]
            kept = jnp.where(lower, even, odd)
            sent = jnp.where(lower, odd, even).astype(values.dtype)
            count = values.size // 128
            packed = jnp.concatenate([values.reshape(-1, 128), sent.reshape(-1, 128)])
            packed = grid.flip(packed, axis, bit)
            other = packed[:count].reshape(values.shape)
            values = jnp.concatenate(
                [jnp.where(lower, values, other), jnp.where(lower, other, values)]
            )
            table = kept + packed[count:].reshape(kept.shape).astype(jnp.float32)
            bit *= 2
        table = table[0]
        values = meet(values, *ready.get(axis, ()))
    return values, table


class Flow:
    def __init__(self, steps):
        self.steps = steps
        self.out = next(steps)


def meet(values, *flows):
    given = [values] + [array for flow in flows for array in flow.out]
    given = list(lax.optimization_barrier(tuple(given)))
    values = given.pop(0)
    for flow in flows:
        count = len(flow.out)
        flow.out = flow.steps.send(given[:count])
        given = given[count:]
    return values


def last(flow):
    while isinstance(flow.out, list):
        flow.out = flow.steps.send(flow.out)
    return flow.out


def sum_small(grid, values):
    for axis in (3, 2, 1, 0):
        bit = 1
        while bit < grid.sizes[axis]:
            values = values + grid.flip(values, axis, bit)
            bit *= 2
    return values


def relative_places(grid, order, crossed=False):
    dims = (CORE,) + tuple(reversed(order))
    number = jnp.arange(grid.count, dtype=jnp.int32)
    shifts = {}
    for axis in reversed(dims):
        shifts[axis] = number % grid.sizes[axis]
        number = number // grid.sizes[axis]
    core = (grid.coords[CORE] + shifts[CORE]) % grid.sizes[CORE]
    first = core == 0

    def place(axis, own):
        if axis == Z_AXIS and crossed:
            return own ^ shifts[axis]
        return (own + shifts[axis]) % grid.sizes[axis]

    x_own, y_own = grid.coords[X_AXIS], grid.coords[Y_AXIS]
    p_place = place(MIX_P, jnp.where(first, x_own, y_own))
    q_place = place(MIX_Q, jnp.where(first, y_own, x_own))
    return grid.join(
        (
            place(Z_AXIS, grid.coords[Z_AXIS]),
            jnp.where(first, q_place, p_place),
            jnp.where(first, p_place, q_place),
            core,
        )
    ).astype(jnp.int32)


def place_kernel(layout, places, *refs):
    parts, tables, sems = refs[: -1 - len(layout)], refs[-1 - len(layout) : -1], refs[-1]
    copies = []
    entries, rows = parts[0].shape[0], parts[0].shape[1]
    for number, part in enumerate(parts):
        for entry in range(entries):
            place = places[number * entries + entry]
            at = 0
            for table, groups in zip(tables, layout):
                for group in range(groups):
                    copies.append(
                        pltpu.make_async_copy(
                            part.at[entry, :, pl.ds(at, table.shape[2])],
                            table.at[place, pl.ds(group * rows, rows)],
                            sems.at[len(copies)],
                        )
                    )
                    at += table.shape[2]
    for copy in copies:
        copy.start()
    for copy in copies:
        copy.wait()


def gather_bulk(grid, shards, order):
    rows = min(shard.shape[0] for shard in shards)
    layout = [shard.shape[0] // rows for shard in shards]
    pieces = [
        shard[group * rows : (group + 1) * rows]
        for shard, groups in zip(shards, layout)
        for group in range(groups)
    ]
    parts = [jnp.concatenate(pieces, axis=1)]
    columns = parts[0].shape[1]
    for axis in order:
        sent = jnp.stack(parts).reshape((-1, rows, columns))
        parts = [sent]
        for _ in range(1, grid.sizes[axis]):
            parts = parts + (yield [grid.ahead(parts[-1], axis, 1)])
    received = yield [grid.ahead(part, CORE, 1) for part in parts]
    parts = parts + received
    places = relative_places(grid, order)
    shapes = [
        (grid.count, groups * rows, shard.shape[1]) for shard, groups in zip(shards, layout)
    ]
    if rows % 16 == 0:
        tables = pl.pallas_call(
            partial(place_kernel, layout),
            out_shape=[jax.ShapeDtypeStruct(shape, parts[0].dtype) for shape in shapes],
            in_specs=[pl.BlockSpec(memory_space=pltpu.SMEM)]
            + [pl.BlockSpec(memory_space=pl.ANY)] * len(parts),
            out_specs=[pl.BlockSpec(memory_space=pltpu.VMEM)] * len(shapes),
            scratch_shapes=[pltpu.SemaphoreType.DMA((grid.count * sum(layout),))],
            compiler_params=pltpu.CompilerParams(vmem_limit_bytes=32 * 2**20),
            cost_estimate=pl.CostEstimate(
                flops=0, bytes_accessed=4 * grid.count * rows * columns, transcendentals=0
            ),
        )(places, *parts)
    else:
        stacked = jnp.stack(parts).reshape((grid.count, rows, columns))
        stacked = jnp.zeros_like(stacked).at[places].set(stacked)
        tables = []
        for shape, groups in zip(shapes, layout):
            width = groups * shape[2]
            table = stacked[:, :, :width].reshape((grid.count, rows, groups, shape[2]))
            tables.append(table.transpose((0, 2, 1, 3)).reshape(shape))
            stacked = stacked[:, :, width:]
    yield tuple(table.reshape((-1, table.shape[2])) for table in tables)


def pick_kernel(places, *refs):
    tables, picked, sems = refs[:-3], refs[-3:-1], refs[-1]
    copies = []
    for number in range(sum(half.shape[0] for half in picked)):
        half, entry = picked[0], number
        if number >= half.shape[0]:
            half, entry = picked[1], number - half.shape[0]
        at = 0
        for table in tables:
            width = table.shape[2]
            copies.append(
                pltpu.make_async_copy(
                    table.at[places[number]],
                    half.at[entry, :, pl.ds(at, width)],
                    sems.at[len(copies)],
                )
            )
            at += width
    for copy in copies:
        copy.start()
    for copy in copies:
        copy.wait()


def pick_rows(tables, places):
    count, rows = tables[0].shape[:2]
    columns = sum(table.shape[2] for table in tables)
    half = (count // 2, rows, columns)
    if rows % 16:
        picked = jnp.concatenate([table[places] for table in tables], axis=2)
        return picked[: count // 2], picked[count // 2 :]
    return pl.pallas_call(
        pick_kernel,
        out_shape=[jax.ShapeDtypeStruct(half, jnp.bfloat16)] * 2,
        in_specs=[pl.BlockSpec(memory_space=pltpu.SMEM)]
        + [pl.BlockSpec(memory_space=pl.ANY)] * len(tables),
        out_specs=[pl.BlockSpec(memory_space=pltpu.VMEM)] * 2,
        scratch_shapes=[pltpu.SemaphoreType.DMA((count * len(tables),))],
        compiler_params=pltpu.CompilerParams(vmem_limit_bytes=32 * 2**20),
        cost_estimate=pl.CostEstimate(
            flops=0, bytes_accessed=4 * count * rows * columns, transcendentals=0
        ),
    )(places, *tables)


def scatter_bulk(grid, tables, order):
    rows = tables[0].shape[0] // grid.count
    columns = sum(table.shape[1] for table in tables)
    places = relative_places(grid, order, True)
    tables = [table.reshape(grid.count, rows, table.shape[1]) for table in tables]
    axes = tuple(reversed(order))
    dims = tuple(grid.sizes[axis] for axis in axes) + (rows, columns)
    kept, sent = pick_rows(tables, places)
    received = yield [grid.ahead(sent, CORE, 1)]
    terms = [kept.reshape(dims), received[0].reshape(dims)]

    def entry(place):
        return sum(term[place].astype(jnp.float32) for term in terms)

    for axis in axes:
        if axis == Z_AXIS:
            bit = 1
            while bit < grid.sizes[axis]:
                terms = [term.reshape((-1, 2) + term.shape[1:]) for term in terms]
                sent = sum(term[:, 1].astype(jnp.float32) for term in terms)
                received = yield [grid.flip(sent.astype(jnp.bfloat16), axis, bit)]
                terms = [term[:, 0] for term in terms] + received
                bit *= 2
            terms = [term[0] for term in terms]
            continue
        total = None
        for place in range(1, grid.sizes[axis]):
            here = entry(place)
            total = here if total is None else here + total.astype(jnp.float32)
            total = (yield [grid.ahead(total.astype(jnp.bfloat16), axis, 1)])[0]
        terms = [term[0] for term in terms] + [total]
    yield sum(term.astype(jnp.float32) for term in terms)


HEAD_COLS = 4 * HEAD_DIM


def head_probs(query, key):
    scores = dot_tail(query, key) * HEAD_DIM ** (-0.5)
    weights = jnp.exp(scores - jnp.max(scores, axis=-1, keepdims=True))
    return weights * (1.0 / jnp.sum(weights, axis=-1, keepdims=True))


def head_masks():
    lanes = lax.broadcasted_iota(jnp.int32, (1, 2 * HEAD_DIM), 1)
    first = lanes < HEAD_DIM
    return first, (first.astype(jnp.bfloat16), (~first).astype(jnp.bfloat16))


def attend_kernel(query_ref, key_ref, value_ref, mixed_ref):
    first, masks = head_masks()
    for at in range(0, HEAD_COLS, 2 * HEAD_DIM):
        pair = slice(at, at + 2 * HEAD_DIM)
        query, key, value = query_ref[:, pair], key_ref[:, pair], value_ref[:, pair]
        mixed = [
            matmul(head_probs(query * mask, key).astype(jnp.bfloat16), value) for mask in masks
        ]
        mixed_ref[:, pair] = jnp.where(first, mixed[0], mixed[1]).astype(jnp.bfloat16)


def attend_back_kernel(query_ref, key_ref, value_ref, grad_ref, out_ref, bias_ref):
    first, masks = head_masks()

    @pl.when(pl.program_id(1) == 0)
    def _():
        bias_ref[...] = jnp.zeros_like(bias_ref)

    for at in range(0, HEAD_COLS, 2 * HEAD_DIM):
        pair = slice(at, at + 2 * HEAD_DIM)
        query, key, value = query_ref[:, pair], key_ref[:, pair], value_ref[:, pair]
        grad = grad_ref[:, pair]
        parts = []
        for mask in masks:
            probs = head_probs(query * mask, key)
            grad_probs = dot_tail(grad * mask, value)
            inner = jnp.sum(probs * grad_probs, axis=-1, keepdims=True)
            grad_scores = (probs * (grad_probs - inner)).astype(jnp.bfloat16)
            parts.append(
                (
                    matmul(grad_scores, key) * HEAD_DIM ** (-0.5),
                    dot_head(grad_scores, query) * HEAD_DIM ** (-0.5),
                    dot_head(probs.astype(jnp.bfloat16), grad),
                )
            )
        whole = [jnp.where(first, one, two) for one, two in zip(*parts)]
        for index in range(3):
            out_ref[index, :, pair] = whole[index].astype(jnp.bfloat16)
        bias_ref[0:1, pair] += jnp.sum(whole[0], axis=0, keepdims=True)
        bias_ref[1:2, pair] += jnp.sum(whole[2], axis=0, keepdims=True)


def head_specs():
    groups = D // HEAD_COLS
    return [
        pl.BlockSpec((TOK, HEAD_COLS), lambda group, image, part=part: (image, part * groups + group))
        for part in range(3)
    ]


def attend(proj):
    count = proj.shape[0] // TOK
    flops = 4 * count * HEADS * TOK * TOK * HEAD_DIM
    return pl.pallas_call(
        attend_kernel,
        grid=(D // HEAD_COLS, count),
        out_shape=jax.ShapeDtypeStruct((proj.shape[0], D), jnp.bfloat16),
        in_specs=head_specs(),
        out_specs=pl.BlockSpec((TOK, HEAD_COLS), lambda group, image: (image, group)),
        compiler_params=pltpu.CompilerParams(vmem_limit_bytes=24 * 2**20),
        cost_estimate=pl.CostEstimate(
            flops=4 * flops, bytes_accessed=8 * proj.size, transcendentals=flops // 256
        ),
    )(proj, proj, proj)


def attend_back(proj, grad_mixed):
    count = proj.shape[0] // TOK
    flops = 12 * count * HEADS * TOK * TOK * HEAD_DIM
    block = pl.BlockSpec((TOK, HEAD_COLS), lambda group, image: (image, group))
    return pl.pallas_call(
        attend_back_kernel,
        grid=(D // HEAD_COLS, count),
        out_shape=[
            jax.ShapeDtypeStruct((3, proj.shape[0], D), jnp.bfloat16),
            jax.ShapeDtypeStruct((8, D), jnp.float32),
        ],
        in_specs=head_specs() + [block],
        out_specs=[
            pl.BlockSpec((3, TOK, HEAD_COLS), lambda group, image: (0, image, group)),
            pl.BlockSpec((8, HEAD_COLS), lambda group, image: (0, group)),
        ],
        compiler_params=pltpu.CompilerParams(vmem_limit_bytes=24 * 2**20),
        cost_estimate=pl.CostEstimate(
            flops=3 * flops, bytes_accessed=16 * proj.size, transcendentals=flops // 512
        ),
    )(proj, proj, proj, grad_mixed)


ORDER = (Z_AXIS, MIX_P, MIX_Q)


def per_device(
    latents,
    noise_draw,
    timesteps,
    labels,
    weights_in,
    weights_down,
    weights_side,
    biases,
    first_in,
    first_down,
    first_side,
    first_bias,
    second_in,
    second_down,
    second_side,
    second_bias,
):
    bf16 = jnp.bfloat16
    count_all = lax.axis_size(AXIS)
    grid = Grid(count_all)
    sizes = grid.shape
    count = latents.shape[0]
    rows_all = count * TOK
    image_total = count * count_all
    rows = weights_in.shape[0]
    bias_rows = biases.shape[0]
    my_rows = lax.axis_index(AXIS) * rows
    masters = (weights_in, weights_down, weights_side, biases)
    in_bf = weights_in.astype(bf16)
    down_bf = weights_down.astype(bf16)
    side_bf = weights_side.astype(bf16)
    t_first = side_bf[:, :TFREQ]
    patch_at = TFREQ
    class_at = TFREQ + PATCH_FEAT
    head_at = class_at + CLASSES
    w_class = side_bf[:, class_at:head_at]
    w_mods = in_bf[:, 4 * D + FF : 12 * D + FF]
    w_time = in_bf[:, 12 * D + FF :]

    numbers = jnp.concatenate([timesteps, labels])
    packed = jnp.concatenate(
        [
            biases.astype(bf16),
            side_bf[:, patch_at:class_at].reshape(-1),
            side_bf[:, head_at:].reshape(-1),
            (numbers // 32).astype(bf16),
            (numbers % 32).astype(bf16),
        ]
    )
    width = packed.shape[0]
    tall = -(-width // (SMALL_ROWS * 128)) * SMALL_ROWS
    packed = jnp.pad(packed, (0, tall * 128 - width)).reshape(tall, 128)
    head_in = weights_in[:, : 4 * D].astype(bf16)
    table_qkvo = lax.all_gather(head_in, AXIS, axis=0, tiled=True)
    up_bf = weights_in[:, 4 * D : 4 * D + FF].astype(bf16)
    table_up = lax.all_gather(up_bf, AXIS, axis=0, tiled=True)
    get = Flow(gather_bulk(grid, [down_bf], ORDER))
    spread_all = gather_small(grid, packed, (CORE, X_AXIS, Y_AXIS, Z_AXIS))
    spread_all = spread_all.reshape(count_all, tall * 128)
    bias_full = spread_all[:, :bias_rows].reshape(-1).astype(jnp.float32)
    at = bias_rows
    w_patch = spread_all[:, at : at + rows * PATCH_FEAT].reshape(D, PATCH_FEAT)
    at += rows * PATCH_FEAT
    w_head = spread_all[:, at : at + rows * PATCH_FEAT].reshape(D, PATCH_FEAT)
    at += rows * PATCH_FEAT
    numbers = spread_all[:, at : at + 4 * count].astype(jnp.float32)
    numbers = numbers[:, : 2 * count] * 32.0 + numbers[:, 2 * count :]
    numbers = numbers.reshape(sizes + (2 * count,))
    numbers = jnp.stack(
        [numbers[:, :, :, core].transpose((1, 2, 0, 3) if core else (2, 1, 0, 3)) for core in range(sizes[CORE])]
    ).reshape(count_all, 2 * count)
    steps_all = numbers[:, :count].reshape(image_total)
    labels_all = numbers[:, count:].reshape(image_total).astype(jnp.int32)

    b_qkv = jnp.concatenate([bias_full[:D], jnp.zeros((D,), jnp.float32), bias_full[D : 2 * D]])
    b_out = bias_full[2 * D : 3 * D]
    b_up = bias_full[3 * D : 3 * D + FF]
    b_down = bias_full[3 * D + FF : 4 * D + FF]
    b_mods = bias_full[4 * D + FF : 12 * D + FF]
    b_tfirst = lax.dynamic_slice_in_dim(bias_full[12 * D + FF : 13 * D + FF], my_rows, rows)
    b_time = lax.dynamic_slice_in_dim(bias_full[13 * D + FF : 14 * D + FF], my_rows, rows)
    b_patch = bias_full[14 * D + FF :]

    feats = time_features(steps_all).astype(bf16)
    time_pre = dot_tail(t_first, feats) + b_tfirst[:, None]
    time_act = jax.nn.silu(time_pre).astype(bf16)
    onehot = labels_all[:, None] == jnp.arange(CLASSES, dtype=jnp.int32)[None, :]
    cond_part = lax.dot_general(
        w_time, time_act, (((0,), (0,)), ((), ())), preferred_element_type=jnp.float32
    )
    cond = cond_part.reshape(sizes + (rows, image_total))
    cond = scatter_small(grid, cond)
    cond = cond + b_time[:, None] + dot_tail(w_class, onehot.astype(bf16))
    cond_act = jax.nn.silu(cond).astype(bf16)

    def own_columns(part):
        wide = jnp.zeros((image_total, D), jnp.float32)
        return lax.dynamic_update_slice(wide, part.T, (0, my_rows))

    mods = jnp.concatenate(
        [dot_head(cond_act, w_mods), own_columns(cond), own_columns(time_pre)], axis=1
    )
    mods = mods.reshape(sizes[CORE], sizes[X_AXIS], sizes[Y_AXIS], sizes[Z_AXIS] * count, 10 * D)
    mods = scatter_axis(grid, mods, CORE, 0)
    mods = meet(scatter_axis(grid, mods, MIX_P, 0), get)
    mods = meet(scatter_axis(grid, mods, MIX_Q, 0), get)
    mods = mods.reshape(sizes[Z_AXIS], count * 10 * D // 128, 128)
    total = lax.dynamic_index_in_dim(mods, grid.coords[Z_AXIS], 0, keepdims=False)
    for shift in range(1, sizes[Z_AXIS]):
        part = lax.dynamic_index_in_dim(mods, grid.place(Z_AXIS, -shift), 0, keepdims=False)
        total = total + grid.ahead(part, Z_AXIS, shift)
    mods = meet(total.reshape(count, 10 * D), get)
    cond_own, time_own = mods[:, 8 * D : 9 * D], mods[:, 9 * D :]
    mods = mods[:, : 8 * D] + b_mods
    shift_a, scale_a, gate_a, shift_b, scale_b, gate_b, shift_f, scale_f = jnp.split(
        mods, 8, axis=1
    )

    w_qkv, w_out = table_qkvo[:, : 3 * D], table_qkvo[:, 3 * D :]

    signal, spread = noise_scales(timesteps)
    noise_rows = noise_draw.astype(jnp.float32)
    noisy = signal[:, None, None] * latents.astype(jnp.float32) + spread[:, None, None] * noise_rows
    noisy = noisy.astype(bf16).reshape(rows_all, PATCH_FEAT)
    hidden = dot_tail(noisy, w_patch) + b_patch + jnp.tile(positions(), (count, 1))
    resid_in = hidden.reshape(count, TOK, D)
    normed_a = modulate(resid_in, shift_a, scale_a).astype(bf16).reshape(rows_all, D)
    proj = (matmul(normed_a, w_qkv) + b_qkv).astype(bf16)
    mixed = meet(attend(meet(proj, get)), get)
    tail_bf = after(in_bf[:, 4 * D + FF :], mixed)
    table_cond = lax.all_gather(tail_bf, AXIS, axis=0, tiled=True)
    attended = (matmul(mixed, w_out) + b_out).reshape(count, TOK, D)
    resid_mid = resid_in + gate_a[:, None, :] * attended
    normed_b = modulate(resid_mid, shift_b, scale_b).astype(bf16).reshape(rows_all, D)
    normed_b = meet(normed_b, get)
    (table_down,) = last(get)
    upper = matmul(normed_b, table_up) + b_up
    active = jax.nn.gelu(upper, approximate=True).astype(bf16)
    lowered = matmul(active, table_down) + b_down
    lowered = lowered.reshape(count, TOK, D)
    resid_out = resid_mid + gate_b[:, None, :] * lowered
    normed_c = modulate(resid_out, shift_f, scale_f).astype(bf16).reshape(rows_all, D)
    predicted = matmul(normed_c, w_head)
    error = predicted - noise_rows.reshape(rows_all, PATCH_FEAT)
    loss_local = jnp.sum(error * error)
    grad_pred = (2.0 / image_total * error).astype(bf16)

    grad_head = dot_head(normed_c, grad_pred)
    grad_normed_c = dot_tail(grad_pred, w_head).reshape(count, TOK, D)
    _, pull_final = jax.vjp(modulate, resid_out, shift_f, scale_f)
    grad_out, grad_shift_f, grad_scale_f = pull_final(grad_normed_c)
    grad_gate_b = jnp.sum(grad_out * lowered, axis=1)
    grad_lowered = (grad_out * gate_b[:, None, :]).reshape(rows_all, D)
    grad_b_down = jnp.sum(grad_lowered, axis=0)
    lowered_bf = grad_lowered.astype(bf16)
    grad_w_down = dot_head(active, lowered_bf).astype(bf16)
    put_down = Flow(scatter_bulk(grid, [grad_w_down], ORDER))
    lowered_bf = after(lowered_bf, grad_w_down)
    grad_active = dot_tail(lowered_bf, table_down)
    gelu = partial(jax.nn.gelu, approximate=True)
    grad_upper = jax.vjp(gelu, upper)[1](grad_active)[0]
    grad_b_up = jnp.sum(grad_upper, axis=0)
    upper_bf = grad_upper.astype(bf16)
    upper_bf = meet(upper_bf, put_down)
    grad_w_up = dot_head(normed_b, upper_bf).astype(bf16)
    put_up = Flow(scatter_bulk(grid, [grad_w_up], ORDER))
    upper_bf = after(upper_bf, grad_w_up)
    grad_normed_b = dot_tail(upper_bf, table_up).reshape(count, TOK, D)
    _, pull_mid = jax.vjp(modulate, resid_mid, shift_b, scale_b)
    grad_mid_norm, grad_shift_b, grad_scale_b = pull_mid(grad_normed_b)
    grad_mid = grad_out + grad_mid_norm
    grad_gate_a = jnp.sum(grad_mid * attended, axis=1)
    grad_attended = (grad_mid * gate_a[:, None, :]).reshape(rows_all, D)
    grad_b_out = jnp.sum(grad_attended, axis=0)
    attended_bf = grad_attended.astype(bf16)
    grad_w_out = dot_head(mixed, attended_bf).astype(bf16)
    grad_mixed = dot_tail(attended_bf, w_out).astype(bf16)
    grad_mixed = meet(grad_mixed, put_down, put_up)
    proj_bf, proj_sums = attend_back(proj, grad_mixed)
    grad_b_query, grad_b_value = proj_sums[0], proj_sums[1]
    proj_bf = meet(proj_bf, put_down, put_up)
    grad_qkv = [dot_head(normed_a, proj_bf[part]).astype(bf16) for part in range(3)]
    grad_qkv[0] = meet(grad_qkv[0], put_down, put_up)
    put_rest = Flow(scatter_bulk(grid, grad_qkv + [grad_w_out], ORDER))
    proj_bf = meet(after(proj_bf, *grad_qkv), put_down)
    grad_normed_a = sum(
        dot_tail(proj_bf[part], w_qkv[:, part * D : (part + 1) * D]) for part in range(3)
    ).reshape(count, TOK, D)
    grad_normed_a = meet(grad_normed_a, put_up, put_rest)
    _, pull_first = jax.vjp(modulate, resid_in, shift_a, scale_a)
    grad_in_norm, grad_shift_a, grad_scale_a = pull_first(grad_normed_a)
    grad_hidden = (grad_mid + grad_in_norm).reshape(rows_all, D)
    grad_b_patch = jnp.sum(grad_hidden, axis=0)
    grad_w_patch = dot_head(grad_hidden.astype(bf16), noisy)

    grad_mods = jnp.concatenate(
        [
            grad_shift_a,
            grad_scale_a,
            grad_gate_a,
            grad_shift_b,
            grad_scale_b,
            grad_gate_b,
            grad_shift_f,
            grad_scale_f,
        ],
        axis=1,
    )
    grad_mods = meet(grad_mods, put_up)
    mods_bf = grad_mods.astype(bf16)
    grad_cond = jax.vjp(jax.nn.silu, cond_own)[1](dot_tail(mods_bf, table_cond[:, : 8 * D]))[0]
    cond_bf = grad_cond.astype(bf16)
    grad_time_act = dot_tail(cond_bf, table_cond[:, 8 * D :])
    grad_time_pre = jax.vjp(jax.nn.silu, time_own)[1](grad_time_act)[0]
    image_grads = jnp.concatenate([mods_bf, cond_bf, grad_time_pre.astype(bf16)], axis=1)
    image_grads = meet(image_grads, put_rest).reshape(-1, 128)
    grad_bias = jnp.concatenate(
        [
            grad_b_query,
            grad_b_value,
            grad_b_out,
            grad_b_up,
            grad_b_down,
            jnp.zeros((10 * D,), jnp.float32),
            grad_b_patch,
        ]
    )
    small = jnp.concatenate(
        [
            grad_bias.reshape(count_all, bias_rows),
            grad_w_patch.reshape(count_all, rows * PATCH_FEAT),
            grad_head.reshape(count_all, rows * PATCH_FEAT),
        ],
        axis=1,
    )
    tall = -(-small.shape[1] // 2048) * SMALL_ROWS
    small = jnp.pad(small, ((0, 0), (0, tall * 128 - small.shape[1])))
    small = small.reshape(sizes + (tall, 128))
    ready = {axis: (put_rest,) for axis in (Z_AXIS, MIX_P, CORE)}
    image_grads, small = gather_and_scatter(grid, image_grads, small, ready)
    small = small.reshape(-1)
    image_grads = image_grads.reshape(image_total, 10 * D)
    mods_bf, cond_bf = image_grads[:, : 8 * D], image_grads[:, 8 * D : 9 * D]
    grad_w_mods = matmul(cond_act, mods_bf)
    grad_w_time = matmul(time_act, cond_bf)
    grad_w_class = lax.dot_general(
        lax.dynamic_slice_in_dim(cond_bf, my_rows, rows, 1).astype(jnp.float32),
        onehot.astype(jnp.float32),
        (((0,), (0,)), ((), ())),
        precision=lax.Precision.HIGHEST,
        preferred_element_type=jnp.float32,
    )
    own_pre = lax.dynamic_slice_in_dim(image_grads, 9 * D + my_rows, rows, 1)
    grad_t_first = dot_head(own_pre, feats)
    sums = jnp.sum(image_grads.astype(jnp.float32), axis=0)
    known = jnp.concatenate(
        [
            jnp.zeros((4 * D + FF,), jnp.float32),
            sums[: 8 * D],
            sums[9 * D :],
            sums[8 * D : 9 * D],
            jnp.zeros((D,), jnp.float32),
        ]
    )
    known = lax.dynamic_slice_in_dim(known, lax.axis_index(AXIS) * bias_rows, bias_rows)
    at = bias_rows
    sum_patch = small[at : at + rows * PATCH_FEAT].reshape(rows, PATCH_FEAT)
    at += rows * PATCH_FEAT
    sum_head = small[at : at + rows * PATCH_FEAT].reshape(rows, PATCH_FEAT)

    sum_rest, sum_up, sum_down = last(put_rest), last(put_up), last(put_down)
    grads_in = (sum_rest, sum_up, grad_w_mods, grad_w_time)
    grads_other = (
        sum_down,
        jnp.concatenate([grad_t_first, sum_patch, grad_w_class, sum_head], axis=1),
        (small[:bias_rows] + known)[None],
    )
    masters = (weights_in, weights_down, weights_side, biases[None])
    firsts = (first_in, first_down, first_side, first_bias[None])
    seconds = (second_in, second_down, second_side, second_bias[None])
    shapes = [master.shape for master in masters]
    results = directions(masters, firsts, seconds, grads_in, grads_other)
    loss_spot = jnp.arange(8, dtype=jnp.int32)[:, None] == 3
    sums = sum_small(grid, results[12] + jnp.where(loss_spot, loss_local, 0.0))
    updated = updates(sums, masters, results[8:12])
    norms = updated[4]
    return (
        sums[3, 0],
        updated[0],
        updated[1],
        updated[2],
        updated[3][0],
        results[0],
        results[1],
        results[2],
        results[3][0],
        results[4],
        results[5],
        results[6],
        results[7][0],
        norms[2, :12],
        norms[0, :12],
        norms[1, :12],
    )


def solution(mesh):
    placed = (
        P("fsdp", None, None),
        P("fsdp", None, None),
        P("fsdp"),
        P("fsdp"),
        P("fsdp", None),
        P("fsdp", None),
        P("fsdp", None),
        P("fsdp"),
        P("fsdp", None),
        P("fsdp", None),
        P("fsdp", None),
        P("fsdp"),
        P("fsdp", None),
        P("fsdp", None),
        P("fsdp", None),
        P("fsdp"),
    )
    return jax.shard_map(
        per_device,
        mesh=mesh,
        in_specs=placed,
        out_specs=(
            P(),
            P("fsdp", None),
            P("fsdp", None),
            P("fsdp", None),
            P("fsdp"),
            P("fsdp", None),
            P("fsdp", None),
            P("fsdp", None),
            P("fsdp"),
            P("fsdp", None),
            P("fsdp", None),
            P("fsdp", None),
            P("fsdp"),
            P(),
            P(),
            P(),
        ),
        check_vma=False,
    )
```

```python
from functools import partial
import math

import jax
import jax.numpy as jnp
from jax import lax
from jax.experimental import pallas as pl
from jax.experimental.pallas import tpu as pltpu
from jax.sharding import PartitionSpec as P

D = 1024
HEADS = 16
HEAD_DIM = 64
FF = 4096
CLASSES = 1000
PATCH_FEAT = 16
TFREQ = 256
GRID = 16
TOK = 256
MICRO = 2
STEP = 10
IMG_DEV = 1
SIDE = 1288


BETA_ONE = 0.5
BETA_TWO = 0.5
EPSILON = 1e-06
DECAY = 0.01
RATE = 0.25
NORM_EPS = 1e-06
SMALL_ROWS = 16
AXIS = "fsdp"


def matmul(left, right):
    return jnp.dot(left, right, preferred_element_type=jnp.float32)


def dot_tail(left, right):
    return lax.dot_general(
        left, right, (((1,), (1,)), ((), ())), preferred_element_type=jnp.float32
    )


def dot_head(left, right):
    return lax.dot_general(
        left, right, (((0,), (0,)), ((), ())), preferred_element_type=jnp.float32
    )


def layer_norm(values):
    center = values - jnp.mean(values, axis=-1, keepdims=True)
    return center * lax.rsqrt(jnp.mean(center * center, axis=-1, keepdims=True) + NORM_EPS)


def modulate(values, shift, scale):
    return layer_norm(values) * (1.0 + scale[:, None, :]) + shift[:, None, :]


def noise_scales(steps_part):
    phase = (steps_part.astype(jnp.float32) / 1000.0 + 0.008) / 1.008 * (math.pi / 2.0)
    signal = jnp.cos(phase) * jnp.cos(phase)
    return (jnp.sqrt(signal), jnp.sqrt(1.0 - signal))


def time_features(steps_part):
    half_width = TFREQ // 2
    freqs = jnp.exp(-math.log(10000.0) * jnp.arange(half_width, dtype=jnp.float32) / half_width)
    angles = steps_part.astype(jnp.float32)[:, None] * freqs[None, :]
    return jnp.concatenate([jnp.cos(angles), jnp.sin(angles)], axis=1)


def positions():
    quarter = D // 4
    omega = 1.0 / 10000.0 ** (jnp.arange(quarter, dtype=jnp.float32) / quarter)
    cells = jnp.arange(TOK, dtype=jnp.int32)
    row_pos = (cells // GRID).astype(jnp.float32)[:, None] * omega[None, :]
    col_pos = (cells % GRID).astype(jnp.float32)[:, None] * omega[None, :]
    return jnp.concatenate(
        [jnp.sin(row_pos), jnp.cos(row_pos), jnp.sin(col_pos), jnp.cos(col_pos)], axis=1
    )


def column_blocks():
    return [
        (0, 0, 3 * D),
        (0, 3 * D, 4 * D),
        (0, 4 * D, 4 * D + FF),
        (0, 4 * D + FF, 10 * D + FF),
        (0, 10 * D + FF, 12 * D + FF),
        (0, 12 * D + FF, 13 * D + FF),
        (1, 0, 0),
        (2, 0, TFREQ),
        (2, TFREQ, TFREQ + PATCH_FEAT),
        (2, TFREQ + PATCH_FEAT, TFREQ + PATCH_FEAT + CLASSES),
        (2, TFREQ + PATCH_FEAT + CLASSES, SIDE),
        (3, 0, 0),
    ]


def adam_direction(weight, grad, first, second):
    first_new = BETA_ONE * first + (1.0 - BETA_ONE) * grad
    second_new = BETA_TWO * second + (1.0 - BETA_TWO) * grad * grad
    direction = (
        first_new
        / (1.0 - BETA_ONE**STEP)
        / (jnp.sqrt(second_new / (1.0 - BETA_TWO**STEP)) + EPSILON)
        + DECAY * weight
    )
    return (first_new, second_new, direction)


def column_chunks(edges, shapes):
    blocks = column_blocks()
    chunks = []
    for kind in (1, 2, 3):
        parts = [
            (block, start, stop or shapes[kind][1])
            for block, (other, start, stop) in enumerate(blocks)
            if other == kind
        ]
        chunks.append((kind, len(edges) - 2 + kind, 0, 0, shapes[kind][1], parts))
    for number in range(len(edges) - 1):
        for low in range(edges[number], edges[number + 1], 4 * D):
            high = min(low + 4 * D, edges[number + 1])
            parts = [
                (block, max(start, low), min(stop, high))
                for block, (kind, start, stop) in enumerate(blocks)
                if kind == 0 and max(start, low) < min(stop, high)
            ]
            chunks.append((0, number, low - edges[number], low, high, parts))
    return chunks


def span(ref, low, high):
    return ref if (low, high) == (0, ref.shape[1]) else ref.at[:, pl.ds(low, high - low)]


def direction_kernel(edges, shapes, *refs):
    weights, firsts, seconds = refs[0:4], refs[4:8], refs[8:12]
    count = len(edges) - 1 + 3
    grads, outs = refs[12 : 12 + count], refs[12 + count : 25 + count]
    scratch, in_sems, out_sems = refs[25 + count : -2], refs[-2], refs[-1]
    lanes = lax.broadcasted_iota(jnp.int32, (8, 128), 1)
    lines = lax.broadcasted_iota(jnp.int32, (8, 128), 0)
    sums = jnp.zeros((8, 128), jnp.float32)
    chunks = column_chunks(edges, shapes)
    loads, stores = [], []
    for index, (kind, number, at, low, high, _) in enumerate(chunks):
        sources = [span(group[kind], low, high) for group in (weights, firsts, seconds)]
        sources.append(span(grads[number], at, at + high - low))
        held = scratch[7 * kind : 7 * kind + 4]
        loads.append(
            [
                pltpu.make_async_copy(
                    source, span(held[slot], low, high), in_sems.at[index, slot]
                )
                for slot, source in enumerate(sources)
            ]
        )
        for copy in loads[-1]:
            copy.start()
    for index, (kind, _, _, low, high, parts) in enumerate(chunks):
        held, made = scratch[7 * kind : 7 * kind + 4], scratch[7 * kind + 4 : 7 * kind + 7]
        for copy in loads[index]:
            copy.wait()
        for block, start, stop in parts:
            columns = slice(start, stop)
            weight = held[0][:, columns]
            results = adam_direction(
                weight, held[3][:, columns], held[1][:, columns], held[2][:, columns]
            )
            for target, result in zip(made, results):
                target[:, columns] = result
            here = lanes == block
            sums = sums + jnp.where(here & (lines == 0), jnp.sum(weight * weight), 0.0)
            sums = sums + jnp.where(here & (lines == 1), jnp.sum(results[2] * results[2]), 0.0)
        for slot in range(3):
            stores.append(
                pltpu.make_async_copy(
                    span(made[slot], low, high),
                    span(outs[4 * slot + kind], low, high),
                    out_sems.at[index, slot],
                )
            )
            stores[-1].start()
    outs[12][...] = sums
    for copy in stores:
        copy.wait()


def lamb_call(kernel, args, first_specs, shapes, held, slots):
    any_space = pl.BlockSpec(memory_space=pl.ANY)
    size = sum(arg.size for arg in args) + sum(math.prod(shape) for shape in shapes)
    return pl.pallas_call(
        kernel,
        out_shape=[jax.ShapeDtypeStruct(shape, jnp.float32) for shape in shapes],
        in_specs=first_specs + [any_space] * (len(args) - len(first_specs)),
        out_specs=[any_space] * (len(shapes) - 1) + [pl.BlockSpec(memory_space=pltpu.VMEM)],
        scratch_shapes=[pltpu.VMEM(shape, jnp.float32) for shape in held]
        + [pltpu.SemaphoreType.DMA(slot) for slot in slots],
        compiler_params=pltpu.CompilerParams(vmem_limit_bytes=60 * 2**20),
        cost_estimate=pl.CostEstimate(
            flops=10 * size, bytes_accessed=4 * size, transcendentals=size // 8
        ),
    )(*args)


def directions(masters, firsts, seconds, grads_in, grads_other):
    edges = [0]
    for grad in grads_in:
        edges.append(edges[-1] + grad.shape[1])
    shapes = [master.shape for master in masters]
    return lamb_call(
        partial(direction_kernel, edges, shapes),
        masters + firsts + seconds + grads_in + grads_other,
        [],
        shapes * 3 + [(8, 128)],
        [shape for shape in shapes for _ in range(7)],
        [(len(column_chunks(edges, shapes)), slot) for slot in (4, 3)],
    )


def update_kernel(edges, shapes, sums_ref, *refs):
    weights, steps, outs = refs[0:4], refs[4:8], refs[8:13]
    scratch, in_sems, out_sems = refs[13:-2], refs[-2], refs[-1]
    norms = jnp.sqrt(sums_ref[...])
    trust = norms[0:1] / norms[1:2]
    line = lax.broadcasted_iota(jnp.int32, (8, 128), 0)
    outs[4][...] = jnp.where(line == 2, trust, norms)
    chunks = column_chunks(edges, shapes)
    loads, stores = [], []
    for index, (kind, _, _, low, high, _) in enumerate(chunks):
        loads.append(
            [
                pltpu.make_async_copy(
                    span(source[kind], low, high),
                    span(scratch[3 * kind + slot], low, high),
                    in_sems.at[index, slot],
                )
                for slot, source in enumerate((weights, steps))
            ]
        )
        for copy in loads[-1]:
            copy.start()
    for index, (kind, _, _, low, high, parts) in enumerate(chunks):
        held, made = scratch[3 * kind : 3 * kind + 2], scratch[3 * kind + 2]
        for copy in loads[index]:
            copy.wait()
        for block, start, stop in parts:
            columns = slice(start, stop)
            factor = RATE * trust[0:1, block : block + 1]
            made[:, columns] = held[0][:, columns] - factor * held[1][:, columns]
        stores.append(
            pltpu.make_async_copy(
                span(made, low, high), span(outs[kind], low, high), out_sems.at[index]
            )
        )
        stores[-1].start()
    for copy in stores:
        copy.wait()


def updates(sums, masters, steps):
    edges = [0, masters[0].shape[1]]
    shapes = [master.shape for master in masters]
    chunks = len(column_chunks(edges, shapes))
    return lamb_call(
        partial(update_kernel, edges, shapes),
        (sums,) + masters + tuple(steps),
        [pl.BlockSpec(memory_space=pltpu.VMEM)],
        shapes + [(8, 128)],
        [shape for shape in shapes for _ in range(3)],
        [(chunks, 2), (chunks,)],
    )


Z_AXIS, Y_AXIS, X_AXIS, CORE, MIX_P, MIX_Q = range(6)


class Grid:
    def __init__(self, count):
        if count == 32:
            sizes = (4, 2, 2, 2)
        elif count == 256:
            sizes = (8, 4, 4, 2)
        else:
            sizes = (count // 2, 1, 1, 2)
        self.count = count
        self.shape = sizes
        self.sizes = sizes + (sizes[X_AXIS], sizes[Y_AXIS])
        index = lax.axis_index(AXIS)
        self.coords = self.split(index)
        mixed = [
            jnp.where(self.coords[CORE] == 0, self.coords[X_AXIS], self.coords[Y_AXIS]),
            jnp.where(self.coords[CORE] == 0, self.coords[Y_AXIS], self.coords[X_AXIS]),
        ]
        self.coords = self.coords + tuple(mixed)

    def split(self, index):
        coords = []
        for size in reversed(self.shape):
            coords.append(index % size)
            index = index // size
        return tuple(reversed(coords))

    def join(self, coords):
        index = 0
        for size, place in zip(self.shape, coords):
            index = index * size + place
        return index

    def move(self, values, axis, change):
        pairs = []
        for source in range(self.count):
            coords = list(self.split(source))
            real = axis
            if axis == MIX_P:
                real = X_AXIS if coords[CORE] == 0 else Y_AXIS
            if axis == MIX_Q:
                real = Y_AXIS if coords[CORE] == 0 else X_AXIS
            coords[real] = change(coords[real])
            pairs.append((source, self.join(coords)))
        return lax.ppermute(values, AXIS, pairs)

    def ahead(self, values, axis, shift):
        size = self.sizes[axis]
        return self.move(values, axis, lambda place: (place - shift) % size)

    def flip(self, values, axis, bit):
        return self.move(values, axis, lambda place: place ^ bit)

    def place(self, axis, shift):
        return (self.coords[axis] + shift) % self.sizes[axis]


def after(values, *others):
    return lax.optimization_barrier((values,) + others)[0] if others else values


def gather_small(grid, values, order):
    for axis in order:
        values = values[None]
        bit = 1
        while bit < grid.sizes[axis]:
            other = grid.flip(values, axis, bit)
            lower = grid.coords[axis] // bit % 2 == 0
            values = jnp.concatenate(
                [jnp.where(lower, values, other), jnp.where(lower, other, values)]
            )
            bit *= 2
    return values


def scatter_axis(grid, values, axis, dim):
    bit = grid.sizes[axis]
    while bit > 1:
        bit //= 2
        upper = grid.coords[axis] // bit % 2
        kept = lax.dynamic_slice_in_dim(values, upper * bit, bit, dim)
        sent = lax.dynamic_slice_in_dim(values, (1 - upper) * bit, bit, dim)
        values = kept + grid.flip(sent, axis, bit)
    return lax.squeeze(values, (dim,))


def scatter_small(grid, values):
    for axis in (CORE, X_AXIS, Y_AXIS, Z_AXIS):
        values = scatter_axis(grid, values, axis, axis)
    return values


def gather_and_scatter(grid, values, table, ready):
    turned = jnp.swapaxes(table, Y_AXIS, X_AXIS)
    table = jnp.where(grid.coords[CORE] == 0, table, turned)
    for axis in (Z_AXIS, MIX_Q, MIX_P, CORE):
        values = values[None]
        bit = 1
        while bit < grid.sizes[axis]:
            lower = grid.coords[axis] // bit % 2 == 0
            halves = table.reshape((table.shape[0] // 2, 2) + table.shape[1:])
            even, odd = halves[:, 0], halves[:, 1]
            kept = jnp.where(lower, even, odd)
            sent = jnp.where(lower, odd, even).astype(values.dtype)
            count = values.size // 128
            packed = jnp.concatenate([values.reshape(-1, 128), sent.reshape(-1, 128)])
            packed = grid.flip(packed, axis, bit)
            other = packed[:count].reshape(values.shape)
            values = jnp.concatenate(
                [jnp.where(lower, values, other), jnp.where(lower, other, values)]
            )
            table = kept + packed[count:].reshape(kept.shape).astype(jnp.float32)
            bit *= 2
        table = table[0]
        values = meet(values, *ready.get(axis, ()))
    return values, table


class Flow:
    def __init__(self, steps):
        self.steps = steps
        self.out = next(steps)


def meet(values, *flows):
    given = [values] + [array for flow in flows for array in flow.out]
    given = list(lax.optimization_barrier(tuple(given)))
    values = given.pop(0)
    for flow in flows:
        count = len(flow.out)
        flow.out = flow.steps.send(given[:count])
        given = given[count:]
    return values


def last(flow):
    while isinstance(flow.out, list):
        flow.out = flow.steps.send(flow.out)
    return flow.out


def sum_small(grid, values):
    for axis in (3, 2, 1, 0):
        bit = 1
        while bit < grid.sizes[axis]:
            values = values + grid.flip(values, axis, bit)
            bit *= 2
    return values


def relative_places(grid, order, crossed=False):
    dims = (CORE,) + tuple(reversed(order))
    number = jnp.arange(grid.count, dtype=jnp.int32)
    shifts = {}
    for axis in reversed(dims):
        shifts[axis] = number % grid.sizes[axis]
        number = number // grid.sizes[axis]
    core = (grid.coords[CORE] + shifts[CORE]) % grid.sizes[CORE]
    first = core == 0

    def place(axis, own):
        if axis == Z_AXIS and crossed:
            return own ^ shifts[axis]
        return (own + shifts[axis]) % grid.sizes[axis]

    x_own, y_own = grid.coords[X_AXIS], grid.coords[Y_AXIS]
    p_place = place(MIX_P, jnp.where(first, x_own, y_own))
    q_place = place(MIX_Q, jnp.where(first, y_own, x_own))
    return grid.join(
        (
            place(Z_AXIS, grid.coords[Z_AXIS]),
            jnp.where(first, q_place, p_place),
            jnp.where(first, p_place, q_place),
            core,
        )
    ).astype(jnp.int32)


def place_kernel(layout, places, *refs):
    parts, tables, sems = refs[: -1 - len(layout)], refs[-1 - len(layout) : -1], refs[-1]
    copies = []
    entries, rows = parts[0].shape[0], parts[0].shape[1]
    for number, part in enumerate(parts):
        for entry in range(entries):
            place = places[number * entries + entry]
            at = 0
            for table, groups in zip(tables, layout):
                for group in range(groups):
                    copies.append(
                        pltpu.make_async_copy(
                            part.at[entry, :, pl.ds(at, table.shape[2])],
                            table.at[place, pl.ds(group * rows, rows)],
                            sems.at[len(copies)],
                        )
                    )
                    at += table.shape[2]
    for copy in copies:
        copy.start()
    for copy in copies:
        copy.wait()


def gather_bulk(grid, shards, order):
    rows = min(shard.shape[0] for shard in shards)
    layout = [shard.shape[0] // rows for shard in shards]
    pieces = [
        shard[group * rows : (group + 1) * rows]
        for shard, groups in zip(shards, layout)
        for group in range(groups)
    ]
    parts = [jnp.concatenate(pieces, axis=1)]
    columns = parts[0].shape[1]
    for axis in order:
        sent = jnp.stack(parts).reshape((-1, rows, columns))
        parts = [sent]
        for _ in range(1, grid.sizes[axis]):
            parts = parts + (yield [grid.ahead(parts[-1], axis, 1)])
    received = yield [grid.ahead(part, CORE, 1) for part in parts]
    parts = parts + received
    places = relative_places(grid, order)
    shapes = [
        (grid.count, groups * rows, shard.shape[1]) for shard, groups in zip(shards, layout)
    ]
    if rows % 16 == 0:
        tables = pl.pallas_call(
            partial(place_kernel, layout),
            out_shape=[jax.ShapeDtypeStruct(shape, parts[0].dtype) for shape in shapes],
            in_specs=[pl.BlockSpec(memory_space=pltpu.SMEM)]
            + [pl.BlockSpec(memory_space=pl.ANY)] * len(parts),
            out_specs=[pl.BlockSpec(memory_space=pltpu.VMEM)] * len(shapes),
            scratch_shapes=[pltpu.SemaphoreType.DMA((grid.count * sum(layout),))],
            compiler_params=pltpu.CompilerParams(vmem_limit_bytes=32 * 2**20),
            cost_estimate=pl.CostEstimate(
                flops=0, bytes_accessed=4 * grid.count * rows * columns, transcendentals=0
            ),
        )(places, *parts)
    else:
        stacked = jnp.stack(parts).reshape((grid.count, rows, columns))
        stacked = jnp.zeros_like(stacked).at[places].set(stacked)
        tables = []
        for shape, groups in zip(shapes, layout):
            width = groups * shape[2]
            table = stacked[:, :, :width].reshape((grid.count, rows, groups, shape[2]))
            tables.append(table.transpose((0, 2, 1, 3)).reshape(shape))
            stacked = stacked[:, :, width:]
    yield tuple(table.reshape((-1, table.shape[2])) for table in tables)


def pick_kernel(places, *refs):
    tables, picked, sems = refs[:-3], refs[-3:-1], refs[-1]
    copies = []
    for number in range(sum(half.shape[0] for half in picked)):
        half, entry = picked[0], number
        if number >= half.shape[0]:
            half, entry = picked[1], number - half.shape[0]
        at = 0
        for table in tables:
            width = table.shape[2]
            copies.append(
                pltpu.make_async_copy(
                    table.at[places[number]],
                    half.at[entry, :, pl.ds(at, width)],
                    sems.at[len(copies)],
                )
            )
            at += width
    for copy in copies:
        copy.start()
    for copy in copies:
        copy.wait()


def pick_rows(tables, places):
    count, rows = tables[0].shape[:2]
    columns = sum(table.shape[2] for table in tables)
    half = (count // 2, rows, columns)
    if rows % 16:
        picked = jnp.concatenate([table[places] for table in tables], axis=2)
        return picked[: count // 2], picked[count // 2 :]
    return pl.pallas_call(
        pick_kernel,
        out_shape=[jax.ShapeDtypeStruct(half, jnp.bfloat16)] * 2,
        in_specs=[pl.BlockSpec(memory_space=pltpu.SMEM)]
        + [pl.BlockSpec(memory_space=pl.ANY)] * len(tables),
        out_specs=[pl.BlockSpec(memory_space=pltpu.VMEM)] * 2,
        scratch_shapes=[pltpu.SemaphoreType.DMA((count * len(tables),))],
        compiler_params=pltpu.CompilerParams(vmem_limit_bytes=32 * 2**20),
        cost_estimate=pl.CostEstimate(
            flops=0, bytes_accessed=4 * count * rows * columns, transcendentals=0
        ),
    )(places, *tables)


def scatter_bulk(grid, tables, order):
    rows = tables[0].shape[0] // grid.count
    columns = sum(table.shape[1] for table in tables)
    places = relative_places(grid, order, True)
    tables = [table.reshape(grid.count, rows, table.shape[1]) for table in tables]
    axes = tuple(reversed(order))
    dims = tuple(grid.sizes[axis] for axis in axes) + (rows, columns)
    kept, sent = pick_rows(tables, places)
    received = yield [grid.ahead(sent, CORE, 1)]
    terms = [kept.reshape(dims), received[0].reshape(dims)]

    def entry(place):
        return sum(term[place].astype(jnp.float32) for term in terms)

    for axis in axes:
        if axis == Z_AXIS:
            bit = 1
            while bit < grid.sizes[axis]:
                terms = [term.reshape((-1, 2) + term.shape[1:]) for term in terms]
                sent = sum(term[:, 1].astype(jnp.float32) for term in terms)
                received = yield [grid.flip(sent.astype(jnp.bfloat16), axis, bit)]
                terms = [term[:, 0] for term in terms] + received
                bit *= 2
            terms = [term[0] for term in terms]
            continue
        total = None
        for place in range(1, grid.sizes[axis]):
            here = entry(place)
            total = here if total is None else here + total.astype(jnp.float32)
            total = (yield [grid.ahead(total.astype(jnp.bfloat16), axis, 1)])[0]
        terms = [term[0] for term in terms] + [total]
    yield sum(term.astype(jnp.float32) for term in terms)


HEAD_COLS = 4 * HEAD_DIM


def head_probs(query, key):
    scores = dot_tail(query, key) * HEAD_DIM ** (-0.5)
    weights = jnp.exp(scores - jnp.max(scores, axis=-1, keepdims=True))
    return weights * (1.0 / jnp.sum(weights, axis=-1, keepdims=True))


def head_masks():
    lanes = lax.broadcasted_iota(jnp.int32, (1, 2 * HEAD_DIM), 1)
    first = lanes < HEAD_DIM
    return first, (first.astype(jnp.bfloat16), (~first).astype(jnp.bfloat16))


def attend_kernel(query_ref, key_ref, value_ref, mixed_ref):
    first, masks = head_masks()
    for at in range(0, HEAD_COLS, 2 * HEAD_DIM):
        pair = slice(at, at + 2 * HEAD_DIM)
        query, key, value = query_ref[:, pair], key_ref[:, pair], value_ref[:, pair]
        mixed = [
            matmul(head_probs(query * mask, key).astype(jnp.bfloat16), value) for mask in masks
        ]
        mixed_ref[:, pair] = jnp.where(first, mixed[0], mixed[1]).astype(jnp.bfloat16)


def attend_back_kernel(query_ref, key_ref, value_ref, grad_ref, out_ref, bias_ref):
    first, masks = head_masks()

    @pl.when(pl.program_id(1) == 0)
    def _():
        bias_ref[...] = jnp.zeros_like(bias_ref)

    for at in range(0, HEAD_COLS, 2 * HEAD_DIM):
        pair = slice(at, at + 2 * HEAD_DIM)
        query, key, value = query_ref[:, pair], key_ref[:, pair], value_ref[:, pair]
        grad = grad_ref[:, pair]
        parts = []
        for mask in masks:
            probs = head_probs(query * mask, key)
            grad_probs = dot_tail(grad * mask, value)
            inner = jnp.sum(probs * grad_probs, axis=-1, keepdims=True)
            grad_scores = (probs * (grad_probs - inner)).astype(jnp.bfloat16)
            parts.append(
                (
                    matmul(grad_scores, key) * HEAD_DIM ** (-0.5),
                    dot_head(grad_scores, query) * HEAD_DIM ** (-0.5),
                    dot_head(probs.astype(jnp.bfloat16), grad),
                )
            )
        whole = [jnp.where(first, one, two) for one, two in zip(*parts)]
        for index in range(3):
            out_ref[index, :, pair] = whole[index].astype(jnp.bfloat16)
        bias_ref[0:1, pair] += jnp.sum(whole[0], axis=0, keepdims=True)
        bias_ref[1:2, pair] += jnp.sum(whole[2], axis=0, keepdims=True)


def head_specs():
    groups = D // HEAD_COLS
    return [
        pl.BlockSpec((TOK, HEAD_COLS), lambda group, image, part=part: (image, part * groups + group))
        for part in range(3)
    ]


def attend(proj):
    count = proj.shape[0] // TOK
    flops = 4 * count * HEADS * TOK * TOK * HEAD_DIM
    return pl.pallas_call(
        attend_kernel,
        grid=(D // HEAD_COLS, count),
        out_shape=jax.ShapeDtypeStruct((proj.shape[0], D), jnp.bfloat16),
        in_specs=head_specs(),
        out_specs=pl.BlockSpec((TOK, HEAD_COLS), lambda group, image: (image, group)),
        compiler_params=pltpu.CompilerParams(vmem_limit_bytes=24 * 2**20),
        cost_estimate=pl.CostEstimate(
            flops=4 * flops, bytes_accessed=8 * proj.size, transcendentals=flops // 256
        ),
    )(proj, proj, proj)


def attend_back(proj, grad_mixed):
    count = proj.shape[0] // TOK
    flops = 12 * count * HEADS * TOK * TOK * HEAD_DIM
    block = pl.BlockSpec((TOK, HEAD_COLS), lambda group, image: (image, group))
    return pl.pallas_call(
        attend_back_kernel,
        grid=(D // HEAD_COLS, count),
        out_shape=[
            jax.ShapeDtypeStruct((3, proj.shape[0], D), jnp.bfloat16),
            jax.ShapeDtypeStruct((8, D), jnp.float32),
        ],
        in_specs=head_specs() + [block],
        out_specs=[
            pl.BlockSpec((3, TOK, HEAD_COLS), lambda group, image: (0, image, group)),
            pl.BlockSpec((8, HEAD_COLS), lambda group, image: (0, group)),
        ],
        compiler_params=pltpu.CompilerParams(vmem_limit_bytes=24 * 2**20),
        cost_estimate=pl.CostEstimate(
            flops=3 * flops, bytes_accessed=16 * proj.size, transcendentals=flops // 512
        ),
    )(proj, proj, proj, grad_mixed)


ORDER = (Z_AXIS, MIX_P, MIX_Q)


def per_device(
    latents,
    noise_draw,
    timesteps,
    labels,
    weights_in,
    weights_down,
    weights_side,
    biases,
    first_in,
    first_down,
    first_side,
    first_bias,
    second_in,
    second_down,
    second_side,
    second_bias,
):
    bf16 = jnp.bfloat16
    count_all = lax.axis_size(AXIS)
    grid = Grid(count_all)
    sizes = grid.shape
    count = latents.shape[0]
    rows_all = count * TOK
    image_total = count * count_all
    rows = weights_in.shape[0]
    bias_rows = biases.shape[0]
    my_rows = lax.axis_index(AXIS) * rows
    masters = (weights_in, weights_down, weights_side, biases)
    in_bf = weights_in.astype(bf16)
    down_bf = weights_down.astype(bf16)
    side_bf = weights_side.astype(bf16)
    t_first = side_bf[:, :TFREQ]
    patch_at = TFREQ
    class_at = TFREQ + PATCH_FEAT
    head_at = class_at + CLASSES
    w_class = side_bf[:, class_at:head_at]
    w_mods = in_bf[:, 4 * D + FF : 12 * D + FF]
    w_time = in_bf[:, 12 * D + FF :]

    numbers = jnp.concatenate([timesteps, labels])
    packed = jnp.concatenate(
        [
            biases.astype(bf16),
            side_bf[:, patch_at:class_at].reshape(-1),
            side_bf[:, head_at:].reshape(-1),
            (numbers // 32).astype(bf16),
            (numbers % 32).astype(bf16),
        ]
    )
    width = packed.shape[0]
    tall = -(-width // (SMALL_ROWS * 128)) * SMALL_ROWS
    packed = jnp.pad(packed, (0, tall * 128 - width)).reshape(tall, 128)
    main_bf = weights_in[:, : 4 * D + FF].astype(bf16)
    table_main = lax.all_gather(main_bf, AXIS, axis=0, tiled=True)
    get = Flow(gather_bulk(grid, [down_bf], ORDER))
    spread_all = gather_small(grid, packed, (CORE, X_AXIS, Y_AXIS))
    spread_all = gather_small(grid, meet(spread_all, get), (Z_AXIS,))
    spread_all = spread_all.reshape(count_all, tall * 128)
    bias_full = spread_all[:, :bias_rows].reshape(-1).astype(jnp.float32)
    at = bias_rows
    w_patch = spread_all[:, at : at + rows * PATCH_FEAT].reshape(D, PATCH_FEAT)
    at += rows * PATCH_FEAT
    w_head = spread_all[:, at : at + rows * PATCH_FEAT].reshape(D, PATCH_FEAT)
    at += rows * PATCH_FEAT
    numbers = spread_all[:, at : at + 4 * count].astype(jnp.float32)
    numbers = numbers[:, : 2 * count] * 32.0 + numbers[:, 2 * count :]
    numbers = numbers.reshape(sizes + (2 * count,))
    numbers = jnp.stack(
        [numbers[:, :, :, core].transpose((1, 2, 0, 3) if core else (2, 1, 0, 3)) for core in range(sizes[CORE])]
    ).reshape(count_all, 2 * count)
    steps_all = numbers[:, :count].reshape(image_total)
    labels_all = numbers[:, count:].reshape(image_total).astype(jnp.int32)

    b_qkv = jnp.concatenate([bias_full[:D], jnp.zeros((D,), jnp.float32), bias_full[D : 2 * D]])
    b_out = bias_full[2 * D : 3 * D]
    b_up = bias_full[3 * D : 3 * D + FF]
    b_down = bias_full[3 * D + FF : 4 * D + FF]
    b_mods = bias_full[4 * D + FF : 12 * D + FF]
    b_tfirst = lax.dynamic_slice_in_dim(bias_full[12 * D + FF : 13 * D + FF], my_rows, rows)
    b_time = lax.dynamic_slice_in_dim(bias_full[13 * D + FF : 14 * D + FF], my_rows, rows)
    b_patch = bias_full[14 * D + FF :]

    feats = time_features(steps_all).astype(bf16)
    time_pre = dot_tail(t_first, feats) + b_tfirst[:, None]
    time_act = jax.nn.silu(time_pre).astype(bf16)
    onehot = labels_all[:, None] == jnp.arange(CLASSES, dtype=jnp.int32)[None, :]
    cond_part = lax.dot_general(
        w_time, time_act, (((0,), (0,)), ((), ())), preferred_element_type=jnp.float32
    )
    cond = cond_part.reshape(sizes + (rows, image_total))
    cond = scatter_axis(grid, scatter_axis(grid, cond, CORE, CORE), X_AXIS, X_AXIS)
    cond = scatter_axis(grid, meet(cond, get), Y_AXIS, Y_AXIS)
    cond = scatter_axis(grid, cond, Z_AXIS, Z_AXIS)
    cond = cond + b_time[:, None] + dot_tail(w_class, onehot.astype(bf16))
    cond_act = jax.nn.silu(cond).astype(bf16)

    def own_columns(part):
        wide = jnp.zeros((image_total, D), jnp.float32)
        return lax.dynamic_update_slice(wide, part.T, (0, my_rows))

    mods = jnp.concatenate(
        [dot_head(cond_act, w_mods), own_columns(cond), own_columns(time_pre)], axis=1
    )
    mods = mods.reshape(sizes[CORE], sizes[X_AXIS], sizes[Y_AXIS], sizes[Z_AXIS] * count, 10 * D)
    mods = meet(scatter_axis(grid, mods, CORE, 0), get)
    mods = scatter_axis(grid, mods, MIX_P, 0)
    mods = scatter_axis(grid, mods, MIX_Q, 0)
    mods = mods.reshape(sizes[Z_AXIS], count * 10 * D // 128, 128)
    total = lax.dynamic_index_in_dim(mods, grid.coords[Z_AXIS], 0, keepdims=False)
    for shift in range(1, sizes[Z_AXIS]):
        part = lax.dynamic_index_in_dim(mods, grid.place(Z_AXIS, -shift), 0, keepdims=False)
        total = total + grid.ahead(part, Z_AXIS, shift)
    mods = meet(total.reshape(count, 10 * D), get)
    cond_own, time_own = mods[:, 8 * D : 9 * D], mods[:, 9 * D :]
    mods = mods[:, : 8 * D] + b_mods
    shift_a, scale_a, gate_a, shift_b, scale_b, gate_b, shift_f, scale_f = jnp.split(
        mods, 8, axis=1
    )

    w_qkv, w_out = table_main[:, : 3 * D], table_main[:, 3 * D : 4 * D]
    table_up = table_main[:, 4 * D :]

    signal, spread = noise_scales(timesteps)
    noise_rows = noise_draw.astype(jnp.float32)
    noisy = signal[:, None, None] * latents.astype(jnp.float32) + spread[:, None, None] * noise_rows
    noisy = noisy.astype(bf16).reshape(rows_all, PATCH_FEAT)
    hidden = dot_tail(noisy, w_patch) + b_patch + jnp.tile(positions(), (count, 1))
    resid_in = hidden.reshape(count, TOK, D)
    normed_a = modulate(resid_in, shift_a, scale_a).astype(bf16).reshape(rows_all, D)
    proj = (matmul(normed_a, w_qkv) + b_qkv).astype(bf16)
    mixed = meet(attend(proj), get)
    tail_bf = after(in_bf[:, 4 * D + FF :], mixed)
    table_cond = lax.all_gather(tail_bf, AXIS, axis=0, tiled=True)
    attended = (matmul(mixed, w_out) + b_out).reshape(count, TOK, D)
    resid_mid = resid_in + gate_a[:, None, :] * attended
    normed_b = modulate(resid_mid, shift_b, scale_b).astype(bf16).reshape(rows_all, D)
    normed_b = meet(normed_b, get)
    (table_down,) = last(get)
    upper = matmul(normed_b, table_up) + b_up
    active = jax.nn.gelu(upper, approximate=True).astype(bf16)
    lowered = matmul(active, table_down) + b_down
    lowered = lowered.reshape(count, TOK, D)
    resid_out = resid_mid + gate_b[:, None, :] * lowered
    normed_c = modulate(resid_out, shift_f, scale_f).astype(bf16).reshape(rows_all, D)
    predicted = matmul(normed_c, w_head)
    error = predicted - noise_rows.reshape(rows_all, PATCH_FEAT)
    loss_local = jnp.sum(error * error)
    grad_pred = (2.0 / image_total * error).astype(bf16)

    grad_head = dot_head(normed_c, grad_pred)
    grad_normed_c = dot_tail(grad_pred, w_head).reshape(count, TOK, D)
    _, pull_final = jax.vjp(modulate, resid_out, shift_f, scale_f)
    grad_out, grad_shift_f, grad_scale_f = pull_final(grad_normed_c)
    grad_gate_b = jnp.sum(grad_out * lowered, axis=1)
    grad_lowered = (grad_out * gate_b[:, None, :]).reshape(rows_all, D)
    grad_b_down = jnp.sum(grad_lowered, axis=0)
    lowered_bf = grad_lowered.astype(bf16)
    grad_w_down = dot_head(active, lowered_bf).astype(bf16)
    put_down = Flow(scatter_bulk(grid, [grad_w_down], ORDER))
    lowered_bf = after(lowered_bf, grad_w_down)
    grad_active = dot_tail(lowered_bf, table_down)
    gelu = partial(jax.nn.gelu, approximate=True)
    grad_upper = jax.vjp(gelu, upper)[1](grad_active)[0]
    grad_b_up = jnp.sum(grad_upper, axis=0)
    upper_bf = grad_upper.astype(bf16)
    upper_bf = meet(upper_bf, put_down)
    grad_w_up = dot_head(normed_b, upper_bf).astype(bf16)
    put_up = Flow(scatter_bulk(grid, [grad_w_up], ORDER))
    upper_bf = after(upper_bf, grad_w_up)
    grad_normed_b = dot_tail(upper_bf, table_up).reshape(count, TOK, D)
    grad_normed_b = meet(grad_normed_b, put_down)
    _, pull_mid = jax.vjp(modulate, resid_mid, shift_b, scale_b)
    grad_mid_norm, grad_shift_b, grad_scale_b = pull_mid(grad_normed_b)
    grad_mid = grad_out + grad_mid_norm
    grad_gate_a = jnp.sum(grad_mid * attended, axis=1)
    grad_attended = (grad_mid * gate_a[:, None, :]).reshape(rows_all, D)
    grad_b_out = jnp.sum(grad_attended, axis=0)
    attended_bf = grad_attended.astype(bf16)
    grad_w_out = dot_head(mixed, attended_bf).astype(bf16)
    grad_mixed = dot_tail(attended_bf, w_out).astype(bf16)
    grad_mixed = meet(grad_mixed, put_down, put_up)
    proj_bf, proj_sums = attend_back(proj, grad_mixed)
    grad_b_query, grad_b_value = proj_sums[0], proj_sums[1]
    proj_bf = meet(proj_bf, put_down, put_up)
    grad_qkv = [dot_head(normed_a, proj_bf[part]).astype(bf16) for part in range(3)]
    grad_qkv[0] = meet(grad_qkv[0], put_down, put_up)
    put_rest = Flow(scatter_bulk(grid, grad_qkv + [grad_w_out], ORDER))
    proj_bf = after(proj_bf, *grad_qkv)
    grad_normed_a = sum(
        dot_tail(proj_bf[part], w_qkv[:, part * D : (part + 1) * D]) for part in range(3)
    ).reshape(count, TOK, D)
    grad_normed_a = meet(grad_normed_a, put_up, put_rest)
    _, pull_first = jax.vjp(modulate, resid_in, shift_a, scale_a)
    grad_in_norm, grad_shift_a, grad_scale_a = pull_first(grad_normed_a)
    grad_hidden = (grad_mid + grad_in_norm).reshape(rows_all, D)
    grad_b_patch = jnp.sum(grad_hidden, axis=0)
    grad_w_patch = dot_head(grad_hidden.astype(bf16), noisy)

    grad_mods = jnp.concatenate(
        [
            grad_shift_a,
            grad_scale_a,
            grad_gate_a,
            grad_shift_b,
            grad_scale_b,
            grad_gate_b,
            grad_shift_f,
            grad_scale_f,
        ],
        axis=1,
    )
    grad_mods = meet(grad_mods, put_up)
    mods_bf = grad_mods.astype(bf16)
    grad_cond = jax.vjp(jax.nn.silu, cond_own)[1](dot_tail(mods_bf, table_cond[:, : 8 * D]))[0]
    cond_bf = grad_cond.astype(bf16)
    grad_time_act = dot_tail(cond_bf, table_cond[:, 8 * D :])
    grad_time_pre = jax.vjp(jax.nn.silu, time_own)[1](grad_time_act)[0]
    image_grads = jnp.concatenate([mods_bf, grad_time_pre.astype(bf16), cond_bf], axis=1)
    image_grads = meet(image_grads, put_rest).reshape(-1, 128)
    grad_bias = jnp.concatenate(
        [
            grad_b_query,
            grad_b_value,
            grad_b_out,
            grad_b_up,
            grad_b_down,
            jnp.zeros((10 * D,), jnp.float32),
            grad_b_patch,
        ]
    )
    small = jnp.concatenate(
        [
            grad_bias.reshape(count_all, bias_rows),
            grad_w_patch.reshape(count_all, rows * PATCH_FEAT),
            grad_head.reshape(count_all, rows * PATCH_FEAT),
        ],
        axis=1,
    )
    tall = -(-small.shape[1] // 2048) * SMALL_ROWS
    small = jnp.pad(small, ((0, 0), (0, tall * 128 - small.shape[1])))
    small = small.reshape(sizes + (tall, 128))
    ready = {axis: (put_rest,) for axis in (Z_AXIS, MIX_P, CORE)}
    image_grads, small = gather_and_scatter(grid, image_grads, small, ready)
    small = small.reshape(-1)
    image_grads = image_grads.reshape(image_total, 10 * D)
    mods_bf, cond_bf = image_grads[:, : 8 * D], image_grads[:, 9 * D :]
    grad_w_mods = matmul(cond_act, mods_bf)
    grad_w_time = matmul(time_act, cond_bf)
    grad_w_class = lax.dot_general(
        lax.dynamic_slice_in_dim(cond_bf, my_rows, rows, 1).astype(jnp.float32),
        onehot.astype(jnp.float32),
        (((0,), (0,)), ((), ())),
        precision=lax.Precision.HIGHEST,
        preferred_element_type=jnp.float32,
    )
    own_pre = lax.dynamic_slice_in_dim(image_grads, 8 * D + my_rows, rows, 1)
    grad_t_first = dot_head(own_pre, feats)
    sums = jnp.sum(image_grads.astype(jnp.float32), axis=0)
    known = jnp.pad(sums, (4 * D + FF, D))
    known = lax.dynamic_slice_in_dim(known, lax.axis_index(AXIS) * bias_rows, bias_rows)
    at = bias_rows
    sum_patch = small[at : at + rows * PATCH_FEAT].reshape(rows, PATCH_FEAT)
    at += rows * PATCH_FEAT
    sum_head = small[at : at + rows * PATCH_FEAT].reshape(rows, PATCH_FEAT)

    sum_rest, sum_up, sum_down = last(put_rest), last(put_up), last(put_down)
    grads_in = (sum_rest, sum_up, grad_w_mods, grad_w_time)
    grads_other = (
        sum_down,
        jnp.concatenate([grad_t_first, sum_patch, grad_w_class, sum_head], axis=1),
        (small[:bias_rows] + known)[None],
    )
    masters = (weights_in, weights_down, weights_side, biases[None])
    firsts = (first_in, first_down, first_side, first_bias[None])
    seconds = (second_in, second_down, second_side, second_bias[None])
    shapes = [master.shape for master in masters]
    results = directions(masters, firsts, seconds, grads_in, grads_other)
    loss_spot = jnp.arange(8, dtype=jnp.int32)[:, None] == 3
    sums = sum_small(grid, results[12] + jnp.where(loss_spot, loss_local, 0.0))
    updated = updates(sums, masters, results[8:12])
    norms = updated[4]
    return (
        sums[3, 0],
        updated[0],
        updated[1],
        updated[2],
        updated[3][0],
        results[0],
        results[1],
        results[2],
        results[3][0],
        results[4],
        results[5],
        results[6],
        results[7][0],
        norms[2, :12],
        norms[0, :12],
        norms[1, :12],
    )


def solution(mesh):
    placed = (
        P("fsdp", None, None),
        P("fsdp", None, None),
        P("fsdp"),
        P("fsdp"),
        P("fsdp", None),
        P("fsdp", None),
        P("fsdp", None),
        P("fsdp"),
        P("fsdp", None),
        P("fsdp", None),
        P("fsdp", None),
        P("fsdp"),
        P("fsdp", None),
        P("fsdp", None),
        P("fsdp", None),
        P("fsdp"),
    )
    return jax.shard_map(
        per_device,
        mesh=mesh,
        in_specs=placed,
        out_specs=(
            P(),
            P("fsdp", None),
            P("fsdp", None),
            P("fsdp", None),
            P("fsdp"),
            P("fsdp", None),
            P("fsdp", None),
            P("fsdp", None),
            P("fsdp"),
            P("fsdp", None),
            P("fsdp", None),
            P("fsdp", None),
            P("fsdp"),
            P(),
            P(),
            P(),
        ),
        check_vma=False,
    )
```

```python
from functools import partial
import math

import jax
import jax.numpy as jnp
from jax import lax
from jax.experimental import pallas as pl
from jax.experimental.pallas import tpu as pltpu
from jax.sharding import PartitionSpec as P

D = 1024
HEADS = 16
HEAD_DIM = 64
FF = 4096
CLASSES = 1000
PATCH_FEAT = 16
TFREQ = 256
GRID = 16
TOK = 256
MICRO = 2
STEP = 10
IMG_DEV = 1
SIDE = 1288


BETA_ONE = 0.5
BETA_TWO = 0.5
EPSILON = 1e-06
DECAY = 0.01
RATE = 0.25
NORM_EPS = 1e-06
SMALL_ROWS = 16
AXIS = "fsdp"


def matmul(left, right):
    return jnp.dot(left, right, preferred_element_type=jnp.float32)


def dot_tail(left, right):
    return lax.dot_general(
        left, right, (((1,), (1,)), ((), ())), preferred_element_type=jnp.float32
    )


def dot_head(left, right):
    return lax.dot_general(
        left, right, (((0,), (0,)), ((), ())), preferred_element_type=jnp.float32
    )


def layer_norm(values):
    center = values - jnp.mean(values, axis=-1, keepdims=True)
    return center * lax.rsqrt(jnp.mean(center * center, axis=-1, keepdims=True) + NORM_EPS)


def modulate(values, shift, scale):
    return layer_norm(values) * (1.0 + scale[:, None, :]) + shift[:, None, :]


def noise_scales(steps_part):
    phase = (steps_part.astype(jnp.float32) / 1000.0 + 0.008) / 1.008 * (math.pi / 2.0)
    signal = jnp.cos(phase) * jnp.cos(phase)
    return (jnp.sqrt(signal), jnp.sqrt(1.0 - signal))


def time_features(steps_part):
    half_width = TFREQ // 2
    freqs = jnp.exp(-math.log(10000.0) * jnp.arange(half_width, dtype=jnp.float32) / half_width)
    angles = steps_part.astype(jnp.float32)[:, None] * freqs[None, :]
    return jnp.concatenate([jnp.cos(angles), jnp.sin(angles)], axis=1)


def positions():
    quarter = D // 4
    omega = 1.0 / 10000.0 ** (jnp.arange(quarter, dtype=jnp.float32) / quarter)
    cells = jnp.arange(TOK, dtype=jnp.int32)
    row_pos = (cells // GRID).astype(jnp.float32)[:, None] * omega[None, :]
    col_pos = (cells % GRID).astype(jnp.float32)[:, None] * omega[None, :]
    return jnp.concatenate(
        [jnp.sin(row_pos), jnp.cos(row_pos), jnp.sin(col_pos), jnp.cos(col_pos)], axis=1
    )


def column_blocks():
    return [
        (0, 0, 3 * D),
        (0, 3 * D, 4 * D),
        (0, 4 * D, 4 * D + FF),
        (0, 4 * D + FF, 10 * D + FF),
        (0, 10 * D + FF, 12 * D + FF),
        (0, 12 * D + FF, 13 * D + FF),
        (1, 0, 0),
        (2, 0, TFREQ),
        (2, TFREQ, TFREQ + PATCH_FEAT),
        (2, TFREQ + PATCH_FEAT, TFREQ + PATCH_FEAT + CLASSES),
        (2, TFREQ + PATCH_FEAT + CLASSES, SIDE),
        (3, 0, 0),
    ]


def adam_direction(weight, grad, first, second):
    first_new = BETA_ONE * first + (1.0 - BETA_ONE) * grad
    second_new = BETA_TWO * second + (1.0 - BETA_TWO) * grad * grad
    direction = (
        first_new
        / (1.0 - BETA_ONE**STEP)
        / (jnp.sqrt(second_new / (1.0 - BETA_TWO**STEP)) + EPSILON)
        + DECAY * weight
    )
    return (first_new, second_new, direction)


def column_chunks(edges, shapes):
    blocks = column_blocks()
    chunks = []
    for kind in (1, 2, 3):
        parts = [
            (block, start, stop or shapes[kind][1])
            for block, (other, start, stop) in enumerate(blocks)
            if other == kind
        ]
        chunks.append((kind, len(edges) - 2 + kind, 0, 0, shapes[kind][1], parts))
    for number in range(len(edges) - 1):
        for low in range(edges[number], edges[number + 1], 4 * D):
            high = min(low + 4 * D, edges[number + 1])
            parts = [
                (block, max(start, low), min(stop, high))
                for block, (kind, start, stop) in enumerate(blocks)
                if kind == 0 and max(start, low) < min(stop, high)
            ]
            chunks.append((0, number, low - edges[number], low, high, parts))
    return chunks


def span(ref, low, high):
    return ref if (low, high) == (0, ref.shape[1]) else ref.at[:, pl.ds(low, high - low)]


def direction_kernel(edges, shapes, *refs):
    weights, firsts, seconds = refs[0:4], refs[4:8], refs[8:12]
    count = len(edges) - 1 + 3
    grads, outs = refs[12 : 12 + count], refs[12 + count : 25 + count]
    scratch, in_sems, out_sems = refs[25 + count : -2], refs[-2], refs[-1]
    lanes = lax.broadcasted_iota(jnp.int32, (8, 128), 1)
    lines = lax.broadcasted_iota(jnp.int32, (8, 128), 0)
    sums = jnp.zeros((8, 128), jnp.float32)
    chunks = column_chunks(edges, shapes)
    loads, stores = [], []
    for index, (kind, number, at, low, high, _) in enumerate(chunks):
        sources = [span(group[kind], low, high) for group in (weights, firsts, seconds)]
        sources.append(span(grads[number], at, at + high - low))
        held = scratch[7 * kind : 7 * kind + 4]
        loads.append(
            [
                pltpu.make_async_copy(
                    source, span(held[slot], low, high), in_sems.at[index, slot]
                )
                for slot, source in enumerate(sources)
            ]
        )
        for copy in loads[-1]:
            copy.start()
    for index, (kind, _, _, low, high, parts) in enumerate(chunks):
        held, made = scratch[7 * kind : 7 * kind + 4], scratch[7 * kind + 4 : 7 * kind + 7]
        for copy in loads[index]:
            copy.wait()
        for block, start, stop in parts:
            columns = slice(start, stop)
            weight = held[0][:, columns]
            results = adam_direction(
                weight, held[3][:, columns], held[1][:, columns], held[2][:, columns]
            )
            for target, result in zip(made, results):
                target[:, columns] = result
            here = lanes == block
            sums = sums + jnp.where(here & (lines == 0), jnp.sum(weight * weight), 0.0)
            sums = sums + jnp.where(here & (lines == 1), jnp.sum(results[2] * results[2]), 0.0)
        for slot in range(3):
            stores.append(
                pltpu.make_async_copy(
                    span(made[slot], low, high),
                    span(outs[4 * slot + kind], low, high),
                    out_sems.at[index, slot],
                )
            )
            stores[-1].start()
    outs[12][...] = sums
    for copy in stores:
        copy.wait()


def lamb_call(kernel, args, first_specs, shapes, held, slots):
    any_space = pl.BlockSpec(memory_space=pl.ANY)
    size = sum(arg.size for arg in args) + sum(math.prod(shape) for shape in shapes)
    return pl.pallas_call(
        kernel,
        out_shape=[jax.ShapeDtypeStruct(shape, jnp.float32) for shape in shapes],
        in_specs=first_specs + [any_space] * (len(args) - len(first_specs)),
        out_specs=[any_space] * (len(shapes) - 1) + [pl.BlockSpec(memory_space=pltpu.VMEM)],
        scratch_shapes=[pltpu.VMEM(shape, jnp.float32) for shape in held]
        + [pltpu.SemaphoreType.DMA(slot) for slot in slots],
        compiler_params=pltpu.CompilerParams(vmem_limit_bytes=60 * 2**20),
        cost_estimate=pl.CostEstimate(
            flops=10 * size, bytes_accessed=4 * size, transcendentals=size // 8
        ),
    )(*args)


def directions(masters, firsts, seconds, grads_in, grads_other):
    edges = [0]
    for grad in grads_in:
        edges.append(edges[-1] + grad.shape[1])
    shapes = [master.shape for master in masters]
    return lamb_call(
        partial(direction_kernel, edges, shapes),
        masters + firsts + seconds + grads_in + grads_other,
        [],
        shapes * 3 + [(8, 128)],
        [shape for shape in shapes for _ in range(7)],
        [(len(column_chunks(edges, shapes)), slot) for slot in (4, 3)],
    )


def update_kernel(edges, shapes, sums_ref, *refs):
    weights, steps, outs = refs[0:4], refs[4:8], refs[8:13]
    scratch, in_sems, out_sems = refs[13:-2], refs[-2], refs[-1]
    norms = jnp.sqrt(sums_ref[...])
    trust = norms[0:1] / norms[1:2]
    line = lax.broadcasted_iota(jnp.int32, (8, 128), 0)
    outs[4][...] = jnp.where(line == 2, trust, norms)
    chunks = column_chunks(edges, shapes)
    loads, stores = [], []
    for index, (kind, _, _, low, high, _) in enumerate(chunks):
        loads.append(
            [
                pltpu.make_async_copy(
                    span(source[kind], low, high),
                    span(scratch[3 * kind + slot], low, high),
                    in_sems.at[index, slot],
                )
                for slot, source in enumerate((weights, steps))
            ]
        )
        for copy in loads[-1]:
            copy.start()
    for index, (kind, _, _, low, high, parts) in enumerate(chunks):
        held, made = scratch[3 * kind : 3 * kind + 2], scratch[3 * kind + 2]
        for copy in loads[index]:
            copy.wait()
        for block, start, stop in parts:
            columns = slice(start, stop)
            factor = RATE * trust[0:1, block : block + 1]
            made[:, columns] = held[0][:, columns] - factor * held[1][:, columns]
        stores.append(
            pltpu.make_async_copy(
                span(made, low, high), span(outs[kind], low, high), out_sems.at[index]
            )
        )
        stores[-1].start()
    for copy in stores:
        copy.wait()


def updates(sums, masters, steps):
    edges = [0, masters[0].shape[1]]
    shapes = [master.shape for master in masters]
    chunks = len(column_chunks(edges, shapes))
    return lamb_call(
        partial(update_kernel, edges, shapes),
        (sums,) + masters + tuple(steps),
        [pl.BlockSpec(memory_space=pltpu.VMEM)],
        shapes + [(8, 128)],
        [shape for shape in shapes for _ in range(3)],
        [(chunks, 2), (chunks,)],
    )


Z_AXIS, Y_AXIS, X_AXIS, CORE, MIX_P, MIX_Q = range(6)


class Grid:
    def __init__(self, count):
        if count == 32:
            sizes = (4, 2, 2, 2)
        elif count == 256:
            sizes = (8, 4, 4, 2)
        else:
            sizes = (count // 2, 1, 1, 2)
        self.count = count
        self.shape = sizes
        self.sizes = sizes + (sizes[X_AXIS], sizes[Y_AXIS])
        index = lax.axis_index(AXIS)
        self.coords = self.split(index)
        mixed = [
            jnp.where(self.coords[CORE] == 0, self.coords[X_AXIS], self.coords[Y_AXIS]),
            jnp.where(self.coords[CORE] == 0, self.coords[Y_AXIS], self.coords[X_AXIS]),
        ]
        self.coords = self.coords + tuple(mixed)

    def split(self, index):
        coords = []
        for size in reversed(self.shape):
            coords.append(index % size)
            index = index // size
        return tuple(reversed(coords))

    def join(self, coords):
        index = 0
        for size, place in zip(self.shape, coords):
            index = index * size + place
        return index

    def move(self, values, axis, change):
        pairs = []
        for source in range(self.count):
            coords = list(self.split(source))
            real = axis
            if axis == MIX_P:
                real = X_AXIS if coords[CORE] == 0 else Y_AXIS
            if axis == MIX_Q:
                real = Y_AXIS if coords[CORE] == 0 else X_AXIS
            coords[real] = change(coords[real])
            pairs.append((source, self.join(coords)))
        return lax.ppermute(values, AXIS, pairs)

    def ahead(self, values, axis, shift):
        size = self.sizes[axis]
        return self.move(values, axis, lambda place: (place - shift) % size)

    def flip(self, values, axis, bit):
        return self.move(values, axis, lambda place: place ^ bit)

    def place(self, axis, shift):
        return (self.coords[axis] + shift) % self.sizes[axis]


def after(values, *others):
    return lax.optimization_barrier((values,) + others)[0] if others else values


def gather_small(grid, values, order):
    for axis in order:
        values = values[None]
        bit = 1
        while bit < grid.sizes[axis]:
            other = grid.flip(values, axis, bit)
            lower = grid.coords[axis] // bit % 2 == 0
            values = jnp.concatenate(
                [jnp.where(lower, values, other), jnp.where(lower, other, values)]
            )
            bit *= 2
    return values


def scatter_axis(grid, values, axis, dim):
    bit = grid.sizes[axis]
    while bit > 1:
        bit //= 2
        upper = grid.coords[axis] // bit % 2
        kept = lax.dynamic_slice_in_dim(values, upper * bit, bit, dim)
        sent = lax.dynamic_slice_in_dim(values, (1 - upper) * bit, bit, dim)
        values = kept + grid.flip(sent, axis, bit)
    return lax.squeeze(values, (dim,))


def scatter_small(grid, values):
    for axis in (CORE, X_AXIS, Y_AXIS, Z_AXIS):
        values = scatter_axis(grid, values, axis, axis)
    return values


def beside_kernel(*refs):
    parts, out = refs[:-1], refs[-1]
    at = 0
    for part in parts:
        out[:, at : at + part.shape[1]] = part[...].astype(out.dtype)
        at += part.shape[1]


def beside(parts):
    vmem = pl.BlockSpec(memory_space=pltpu.VMEM)
    shape = (parts[0].shape[0], sum(part.shape[1] for part in parts))
    return pl.pallas_call(
        beside_kernel,
        out_shape=jax.ShapeDtypeStruct(shape, jnp.bfloat16),
        in_specs=[vmem] * len(parts),
        out_specs=vmem,
    )(*parts)


def gather_and_scatter(grid, values, table, ready):
    turned = jnp.swapaxes(table, Y_AXIS, X_AXIS)
    table = jnp.where(grid.coords[CORE] == 0, table, turned)
    for axis in (Z_AXIS, MIX_Q, MIX_P, CORE):
        values = values[None]
        bit = 1
        while bit < grid.sizes[axis]:
            lower = grid.coords[axis] // bit % 2 == 0
            halves = table.reshape((table.shape[0] // 2, 2) + table.shape[1:])
            even, odd = halves[:, 0], halves[:, 1]
            kept = jnp.where(lower, even, odd)
            sent = jnp.where(lower, odd, even).astype(values.dtype)
            count = values.size // 128
            packed = jnp.concatenate([values.reshape(-1, 128), sent.reshape(-1, 128)])
            packed = grid.flip(packed, axis, bit)
            other = packed[:count].reshape(values.shape)
            values = jnp.concatenate(
                [jnp.where(lower, values, other), jnp.where(lower, other, values)]
            )
            table = kept + packed[count:].reshape(kept.shape).astype(jnp.float32)
            bit *= 2
        table = table[0]
        values = meet(values, *ready.get(axis, ()))
    return values, table


class Flow:
    def __init__(self, steps):
        self.steps = steps
        self.out = next(steps)


def meet(values, *flows):
    given = [values] + [array for flow in flows for array in flow.out]
    given = list(lax.optimization_barrier(tuple(given)))
    values = given.pop(0)
    for flow in flows:
        count = len(flow.out)
        flow.out = flow.steps.send(given[:count])
        given = given[count:]
    return values


def last(flow):
    while isinstance(flow.out, list):
        flow.out = flow.steps.send(flow.out)
    return flow.out


def sum_small(grid, values):
    for axis in (3, 2, 1, 0):
        bit = 1
        while bit < grid.sizes[axis]:
            values = values + grid.flip(values, axis, bit)
            bit *= 2
    return values


def relative_places(grid, order, crossed=False):
    dims = (CORE,) + tuple(reversed(order))
    number = jnp.arange(grid.count, dtype=jnp.int32)
    shifts = {}
    for axis in reversed(dims):
        shifts[axis] = number % grid.sizes[axis]
        number = number // grid.sizes[axis]
    core = (grid.coords[CORE] + shifts[CORE]) % grid.sizes[CORE]
    first = core == 0

    def place(axis, own):
        if axis == Z_AXIS and crossed:
            return own ^ shifts[axis]
        return (own + shifts[axis]) % grid.sizes[axis]

    x_own, y_own = grid.coords[X_AXIS], grid.coords[Y_AXIS]
    p_place = place(MIX_P, jnp.where(first, x_own, y_own))
    q_place = place(MIX_Q, jnp.where(first, y_own, x_own))
    return grid.join(
        (
            place(Z_AXIS, grid.coords[Z_AXIS]),
            jnp.where(first, q_place, p_place),
            jnp.where(first, p_place, q_place),
            core,
        )
    ).astype(jnp.int32)


def place_kernel(layout, places, *refs):
    parts, tables, sems = refs[: -1 - len(layout)], refs[-1 - len(layout) : -1], refs[-1]
    copies = []
    entries, rows = parts[0].shape[0], parts[0].shape[1]
    for number, part in enumerate(parts):
        for entry in range(entries):
            place = places[number * entries + entry]
            at = 0
            for table, groups in zip(tables, layout):
                for group in range(groups):
                    copies.append(
                        pltpu.make_async_copy(
                            part.at[entry, :, pl.ds(at, table.shape[2])],
                            table.at[place, pl.ds(group * rows, rows)],
                            sems.at[len(copies)],
                        )
                    )
                    at += table.shape[2]
    for copy in copies:
        copy.start()
    for copy in copies:
        copy.wait()


def gather_bulk(grid, shards, order):
    rows = min(shard.shape[0] for shard in shards)
    layout = [shard.shape[0] // rows for shard in shards]
    pieces = [
        shard[group * rows : (group + 1) * rows]
        for shard, groups in zip(shards, layout)
        for group in range(groups)
    ]
    parts = [jnp.concatenate(pieces, axis=1)]
    columns = parts[0].shape[1]
    for axis in order:
        sent = jnp.stack(parts).reshape((-1, rows, columns))
        parts = [sent]
        for _ in range(1, grid.sizes[axis]):
            parts = parts + (yield [grid.ahead(parts[-1], axis, 1)])
    received = yield [grid.ahead(part, CORE, 1) for part in parts]
    parts = parts + received
    places = relative_places(grid, order)
    shapes = [
        (grid.count, groups * rows, shard.shape[1]) for shard, groups in zip(shards, layout)
    ]
    if rows % 16 == 0:
        tables = pl.pallas_call(
            partial(place_kernel, layout),
            out_shape=[jax.ShapeDtypeStruct(shape, parts[0].dtype) for shape in shapes],
            in_specs=[pl.BlockSpec(memory_space=pltpu.SMEM)]
            + [pl.BlockSpec(memory_space=pl.ANY)] * len(parts),
            out_specs=[pl.BlockSpec(memory_space=pltpu.VMEM)] * len(shapes),
            scratch_shapes=[pltpu.SemaphoreType.DMA((grid.count * sum(layout),))],
            compiler_params=pltpu.CompilerParams(vmem_limit_bytes=32 * 2**20),
            cost_estimate=pl.CostEstimate(
                flops=0, bytes_accessed=4 * grid.count * rows * columns, transcendentals=0
            ),
        )(places, *parts)
    else:
        stacked = jnp.stack(parts).reshape((grid.count, rows, columns))
        stacked = jnp.zeros_like(stacked).at[places].set(stacked)
        tables = []
        for shape, groups in zip(shapes, layout):
            width = groups * shape[2]
            table = stacked[:, :, :width].reshape((grid.count, rows, groups, shape[2]))
            tables.append(table.transpose((0, 2, 1, 3)).reshape(shape))
            stacked = stacked[:, :, width:]
    yield tuple(table.reshape((-1, table.shape[2])) for table in tables)


def pick_kernel(places, *refs):
    tables, picked, sems = refs[:-3], refs[-3:-1], refs[-1]
    copies = []
    for number in range(sum(half.shape[0] for half in picked)):
        half, entry = picked[0], number
        if number >= half.shape[0]:
            half, entry = picked[1], number - half.shape[0]
        at = 0
        for table in tables:
            width = table.shape[2]
            copies.append(
                pltpu.make_async_copy(
                    table.at[places[number]],
                    half.at[entry, :, pl.ds(at, width)],
                    sems.at[len(copies)],
                )
            )
            at += width
    for copy in copies:
        copy.start()
    for copy in copies:
        copy.wait()


def pick_rows(tables, places):
    count, rows = tables[0].shape[:2]
    columns = sum(table.shape[2] for table in tables)
    half = (count // 2, rows, columns)
    if rows % 16:
        picked = jnp.concatenate([table[places] for table in tables], axis=2)
        return picked[: count // 2], picked[count // 2 :]
    return pl.pallas_call(
        pick_kernel,
        out_shape=[jax.ShapeDtypeStruct(half, jnp.bfloat16)] * 2,
        in_specs=[pl.BlockSpec(memory_space=pltpu.SMEM)]
        + [pl.BlockSpec(memory_space=pl.ANY)] * len(tables),
        out_specs=[pl.BlockSpec(memory_space=pltpu.VMEM)] * 2,
        scratch_shapes=[pltpu.SemaphoreType.DMA((count * len(tables),))],
        compiler_params=pltpu.CompilerParams(vmem_limit_bytes=32 * 2**20),
        cost_estimate=pl.CostEstimate(
            flops=0, bytes_accessed=4 * count * rows * columns, transcendentals=0
        ),
    )(places, *tables)


def scatter_bulk(grid, tables, order):
    rows = tables[0].shape[0] // grid.count
    columns = sum(table.shape[1] for table in tables)
    places = relative_places(grid, order, True)
    tables = [table.reshape(grid.count, rows, table.shape[1]) for table in tables]
    axes = tuple(reversed(order))
    dims = tuple(grid.sizes[axis] for axis in axes) + (rows, columns)
    kept, sent = pick_rows(tables, places)
    received = yield [grid.ahead(sent, CORE, 1)]
    terms = [(kept.reshape(dims), (), 1), (received[0].reshape(dims), (), 1)]

    def total(*index):
        return sum(array[prefix + index].astype(jnp.float32) for array, prefix, _ in terms)

    for axis in axes:
        if axis == Z_AXIS:
            bit = 1
            while bit < grid.sizes[axis]:
                sent = sum(
                    array[prefix + (slice(stride, None, 2 * stride),)].astype(jnp.float32)
                    for array, prefix, stride in terms
                )
                received = yield [grid.flip(sent.astype(jnp.bfloat16), axis, bit)]
                terms = [(array, prefix, 2 * stride) for array, prefix, stride in terms]
                terms.append((received[0], (), 1))
                bit *= 2
        else:
            passing = None
            for place in range(1, grid.sizes[axis]):
                here = total(place)
                if passing is not None:
                    here = here + passing.astype(jnp.float32)
                passing = (yield [grid.ahead(here.astype(jnp.bfloat16), axis, 1)])[0]
            terms = [(array, prefix + (0,), 1) for array, prefix, _ in terms]
            terms.append((passing, (), 1))
            continue
        terms = [(array, prefix + (0,), 1) for array, prefix, _ in terms]
    yield total()


HEAD_COLS = 4 * HEAD_DIM


def head_probs(query, key):
    scores = dot_tail(query, key) * HEAD_DIM ** (-0.5)
    weights = jnp.exp(scores - jnp.max(scores, axis=-1, keepdims=True))
    return weights * (1.0 / jnp.sum(weights, axis=-1, keepdims=True))


def head_masks():
    lanes = lax.broadcasted_iota(jnp.int32, (1, 2 * HEAD_DIM), 1)
    first = lanes < HEAD_DIM
    return first, (first.astype(jnp.bfloat16), (~first).astype(jnp.bfloat16))


def attend_kernel(query_ref, key_ref, value_ref, mixed_ref):
    first, masks = head_masks()
    for at in range(0, HEAD_COLS, 2 * HEAD_DIM):
        pair = slice(at, at + 2 * HEAD_DIM)
        query, key, value = query_ref[:, pair], key_ref[:, pair], value_ref[:, pair]
        mixed = [
            matmul(head_probs(query * mask, key).astype(jnp.bfloat16), value) for mask in masks
        ]
        mixed_ref[:, pair] = jnp.where(first, mixed[0], mixed[1]).astype(jnp.bfloat16)


def attend_back_kernel(query_ref, key_ref, value_ref, grad_ref, out_ref, bias_ref):
    first, masks = head_masks()

    @pl.when(pl.program_id(1) == 0)
    def _():
        bias_ref[...] = jnp.zeros_like(bias_ref)

    for at in range(0, HEAD_COLS, 2 * HEAD_DIM):
        pair = slice(at, at + 2 * HEAD_DIM)
        query, key, value = query_ref[:, pair], key_ref[:, pair], value_ref[:, pair]
        grad = grad_ref[:, pair]
        parts = []
        for mask in masks:
            probs = head_probs(query * mask, key)
            grad_probs = dot_tail(grad * mask, value)
            inner = jnp.sum(probs * grad_probs, axis=-1, keepdims=True)
            grad_scores = (probs * (grad_probs - inner)).astype(jnp.bfloat16)
            parts.append(
                (
                    matmul(grad_scores, key) * HEAD_DIM ** (-0.5),
                    dot_head(grad_scores, query) * HEAD_DIM ** (-0.5),
                    dot_head(probs.astype(jnp.bfloat16), grad),
                )
            )
        whole = [jnp.where(first, one, two) for one, two in zip(*parts)]
        for index in range(3):
            out_ref[index, :, pair] = whole[index].astype(jnp.bfloat16)
        bias_ref[0:1, pair] += jnp.sum(whole[0], axis=0, keepdims=True)
        bias_ref[1:2, pair] += jnp.sum(whole[2], axis=0, keepdims=True)


def head_specs():
    groups = D // HEAD_COLS
    return [
        pl.BlockSpec((TOK, HEAD_COLS), lambda group, image, part=part: (image, part * groups + group))
        for part in range(3)
    ]


def attend(proj):
    count = proj.shape[0] // TOK
    flops = 4 * count * HEADS * TOK * TOK * HEAD_DIM
    return pl.pallas_call(
        attend_kernel,
        grid=(D // HEAD_COLS, count),
        out_shape=jax.ShapeDtypeStruct((proj.shape[0], D), jnp.bfloat16),
        in_specs=head_specs(),
        out_specs=pl.BlockSpec((TOK, HEAD_COLS), lambda group, image: (image, group)),
        compiler_params=pltpu.CompilerParams(vmem_limit_bytes=24 * 2**20),
        cost_estimate=pl.CostEstimate(
            flops=4 * flops, bytes_accessed=8 * proj.size, transcendentals=flops // 256
        ),
    )(proj, proj, proj)


def attend_back(proj, grad_mixed):
    count = proj.shape[0] // TOK
    flops = 12 * count * HEADS * TOK * TOK * HEAD_DIM
    block = pl.BlockSpec((TOK, HEAD_COLS), lambda group, image: (image, group))
    return pl.pallas_call(
        attend_back_kernel,
        grid=(D // HEAD_COLS, count),
        out_shape=[
            jax.ShapeDtypeStruct((3, proj.shape[0], D), jnp.bfloat16),
            jax.ShapeDtypeStruct((8, D), jnp.float32),
        ],
        in_specs=head_specs() + [block],
        out_specs=[
            pl.BlockSpec((3, TOK, HEAD_COLS), lambda group, image: (0, image, group)),
            pl.BlockSpec((8, HEAD_COLS), lambda group, image: (0, group)),
        ],
        compiler_params=pltpu.CompilerParams(vmem_limit_bytes=24 * 2**20),
        cost_estimate=pl.CostEstimate(
            flops=3 * flops, bytes_accessed=16 * proj.size, transcendentals=flops // 512
        ),
    )(proj, proj, proj, grad_mixed)


ORDER = (Z_AXIS, MIX_P, MIX_Q)


def per_device(
    latents,
    noise_draw,
    timesteps,
    labels,
    weights_in,
    weights_down,
    weights_side,
    biases,
    first_in,
    first_down,
    first_side,
    first_bias,
    second_in,
    second_down,
    second_side,
    second_bias,
):
    bf16 = jnp.bfloat16
    count_all = lax.axis_size(AXIS)
    grid = Grid(count_all)
    sizes = grid.shape
    count = latents.shape[0]
    rows_all = count * TOK
    image_total = count * count_all
    rows = weights_in.shape[0]
    bias_rows = biases.shape[0]
    my_rows = lax.axis_index(AXIS) * rows
    masters = (weights_in, weights_down, weights_side, biases)
    in_bf = weights_in.astype(bf16)
    down_bf = weights_down.astype(bf16)
    side_bf = weights_side.astype(bf16)
    t_first = side_bf[:, :TFREQ]
    patch_at = TFREQ
    class_at = TFREQ + PATCH_FEAT
    head_at = class_at + CLASSES
    w_class = side_bf[:, class_at:head_at]
    w_mods = in_bf[:, 4 * D + FF : 12 * D + FF]
    w_time = in_bf[:, 12 * D + FF :]

    numbers = jnp.concatenate([timesteps, labels])
    packed = jnp.concatenate(
        [
            biases.astype(bf16),
            side_bf[:, patch_at:class_at].reshape(-1),
            side_bf[:, head_at:].reshape(-1),
            (numbers // 32).astype(bf16),
            (numbers % 32).astype(bf16),
        ]
    )
    width = packed.shape[0]
    tall = -(-width // (SMALL_ROWS * 128)) * SMALL_ROWS
    packed = jnp.pad(packed, (0, tall * 128 - width)).reshape(tall, 128)
    main_bf = weights_in[:, : 4 * D + FF].astype(bf16)
    table_main = lax.all_gather(main_bf, AXIS, axis=0, tiled=True)
    get = Flow(gather_bulk(grid, [down_bf], ORDER))
    spread_all = gather_small(grid, packed, (CORE, X_AXIS, Y_AXIS))
    spread_all = gather_small(grid, meet(spread_all, get), (Z_AXIS,))
    spread_all = spread_all.reshape(count_all, tall * 128)
    bias_full = spread_all[:, :bias_rows].reshape(-1).astype(jnp.float32)
    at = bias_rows
    w_patch = spread_all[:, at : at + rows * PATCH_FEAT].reshape(D, PATCH_FEAT)
    at += rows * PATCH_FEAT
    w_head = spread_all[:, at : at + rows * PATCH_FEAT].reshape(D, PATCH_FEAT)
    at += rows * PATCH_FEAT
    numbers = spread_all[:, at : at + 4 * count].astype(jnp.float32)
    numbers = numbers[:, : 2 * count] * 32.0 + numbers[:, 2 * count :]
    numbers = numbers.reshape(sizes + (2 * count,))
    numbers = jnp.stack(
        [numbers[:, :, :, core].transpose((1, 2, 0, 3) if core else (2, 1, 0, 3)) for core in range(sizes[CORE])]
    ).reshape(count_all, 2 * count)
    steps_all = numbers[:, :count].reshape(image_total)
    labels_all = numbers[:, count:].reshape(image_total).astype(jnp.int32)

    b_qkv = jnp.concatenate([bias_full[:D], jnp.zeros((D,), jnp.float32), bias_full[D : 2 * D]])
    b_out = bias_full[2 * D : 3 * D]
    b_up = bias_full[3 * D : 3 * D + FF]
    b_down = bias_full[3 * D + FF : 4 * D + FF]
    b_mods = bias_full[4 * D + FF : 12 * D + FF]
    b_tfirst = lax.dynamic_slice_in_dim(bias_full[12 * D + FF : 13 * D + FF], my_rows, rows)
    b_time = lax.dynamic_slice_in_dim(bias_full[13 * D + FF : 14 * D + FF], my_rows, rows)
    b_patch = bias_full[14 * D + FF :]

    feats = time_features(steps_all).astype(bf16)
    time_pre = dot_tail(t_first, feats) + b_tfirst[:, None]
    time_act = jax.nn.silu(time_pre).astype(bf16)
    onehot = labels_all[:, None] == jnp.arange(CLASSES, dtype=jnp.int32)[None, :]
    cond_part = lax.dot_general(
        w_time, time_act, (((0,), (0,)), ((), ())), preferred_element_type=jnp.float32
    )
    cond = cond_part.reshape(sizes + (rows, image_total))
    cond = scatter_axis(grid, scatter_axis(grid, cond, CORE, CORE), X_AXIS, X_AXIS)
    cond = scatter_axis(grid, meet(cond, get), Y_AXIS, Y_AXIS)
    cond = scatter_axis(grid, cond, Z_AXIS, Z_AXIS)
    cond = cond + b_time[:, None] + dot_tail(w_class, onehot.astype(bf16))
    cond_act = jax.nn.silu(cond).astype(bf16)

    def own_columns(part):
        wide = jnp.zeros((image_total, D), jnp.float32)
        return lax.dynamic_update_slice(wide, part.T, (0, my_rows))

    mods = jnp.concatenate(
        [dot_head(cond_act, w_mods), own_columns(cond), own_columns(time_pre)], axis=1
    )
    mods = mods.reshape(sizes[CORE], sizes[X_AXIS], sizes[Y_AXIS], sizes[Z_AXIS] * count, 10 * D)
    mods = meet(scatter_axis(grid, mods, CORE, 0), get)
    mods = scatter_axis(grid, mods, MIX_P, 0)
    mods = scatter_axis(grid, mods, MIX_Q, 0)
    mods = mods.reshape(sizes[Z_AXIS], count * 10 * D // 128, 128)
    total = lax.dynamic_index_in_dim(mods, grid.coords[Z_AXIS], 0, keepdims=False)
    for shift in range(1, sizes[Z_AXIS]):
        part = lax.dynamic_index_in_dim(mods, grid.place(Z_AXIS, -shift), 0, keepdims=False)
        total = total + grid.ahead(part, Z_AXIS, shift)
    mods = meet(total.reshape(count, 10 * D), get)
    cond_own, time_own = mods[:, 8 * D : 9 * D], mods[:, 9 * D :]
    mods = mods[:, : 8 * D] + b_mods
    shift_a, scale_a, gate_a, shift_b, scale_b, gate_b, shift_f, scale_f = jnp.split(
        mods, 8, axis=1
    )

    w_qkv, w_out = table_main[:, : 3 * D], table_main[:, 3 * D : 4 * D]
    table_up = table_main[:, 4 * D :]

    signal, spread = noise_scales(timesteps)
    noise_rows = noise_draw.astype(jnp.float32)
    noisy = signal[:, None, None] * latents.astype(jnp.float32) + spread[:, None, None] * noise_rows
    noisy = noisy.astype(bf16).reshape(rows_all, PATCH_FEAT)
    hidden = dot_tail(noisy, w_patch) + b_patch + jnp.tile(positions(), (count, 1))
    resid_in = hidden.reshape(count, TOK, D)
    normed_a = modulate(resid_in, shift_a, scale_a).astype(bf16).reshape(rows_all, D)
    proj = (matmul(normed_a, w_qkv) + b_qkv).astype(bf16)
    mixed = meet(attend(proj), get)
    tail_bf = after(in_bf[:, 4 * D + FF :], mods)
    table_cond = lax.all_gather(tail_bf, AXIS, axis=0, tiled=True)
    attended = (matmul(mixed, w_out) + b_out).reshape(count, TOK, D)
    resid_mid = resid_in + gate_a[:, None, :] * attended
    normed_b = modulate(resid_mid, shift_b, scale_b).astype(bf16).reshape(rows_all, D)
    normed_b = meet(normed_b, get)
    (table_down,) = last(get)
    upper = matmul(normed_b, table_up) + b_up
    active, pull_gelu = jax.vjp(partial(jax.nn.gelu, approximate=True), upper)
    slope = pull_gelu(jnp.ones_like(upper))[0]
    active, slope = lax.optimization_barrier((active.astype(bf16), slope))
    lowered = matmul(active, table_down) + b_down
    lowered = lowered.reshape(count, TOK, D)
    resid_out = resid_mid + gate_b[:, None, :] * lowered
    normed_c = modulate(resid_out, shift_f, scale_f).astype(bf16).reshape(rows_all, D)
    predicted = matmul(normed_c, w_head)
    error = predicted - noise_rows.reshape(rows_all, PATCH_FEAT)
    loss_local = jnp.sum(error * error)
    grad_pred = (2.0 / image_total * error).astype(bf16)

    grad_head = dot_head(normed_c, grad_pred)
    grad_normed_c = dot_tail(grad_pred, w_head).reshape(count, TOK, D)
    _, pull_final = jax.vjp(modulate, resid_out, shift_f, scale_f)
    grad_out, grad_shift_f, grad_scale_f = pull_final(grad_normed_c)
    grad_gate_b = jnp.sum(grad_out * lowered, axis=1)
    grad_lowered = (grad_out * gate_b[:, None, :]).reshape(rows_all, D)
    grad_b_down = jnp.sum(grad_lowered, axis=0)
    lowered_bf = grad_lowered.astype(bf16)
    grad_w_down = dot_head(active, lowered_bf).astype(bf16)
    put_down = Flow(scatter_bulk(grid, [grad_w_down], ORDER))
    lowered_bf = after(lowered_bf, grad_w_down)
    grad_active = dot_tail(lowered_bf, table_down)
    grad_upper = grad_active * slope
    grad_b_up = jnp.sum(grad_upper, axis=0)
    upper_bf = grad_upper.astype(bf16)
    upper_bf = meet(upper_bf, put_down)
    grad_w_up = dot_head(normed_b, upper_bf).astype(bf16)
    put_up = Flow(scatter_bulk(grid, [grad_w_up], ORDER))
    upper_bf = after(upper_bf, grad_w_up)
    grad_normed_b = dot_tail(upper_bf, table_up).reshape(count, TOK, D)
    grad_normed_b = meet(grad_normed_b, put_down)
    _, pull_mid = jax.vjp(modulate, resid_mid, shift_b, scale_b)
    grad_mid_norm, grad_shift_b, grad_scale_b = pull_mid(grad_normed_b)
    grad_mid = grad_out + grad_mid_norm
    grad_gate_a = jnp.sum(grad_mid * attended, axis=1)
    grad_attended = (grad_mid * gate_a[:, None, :]).reshape(rows_all, D)
    grad_b_out = jnp.sum(grad_attended, axis=0)
    attended_bf = grad_attended.astype(bf16)
    grad_w_out = dot_head(mixed, attended_bf).astype(bf16)
    grad_mixed = dot_tail(attended_bf, w_out).astype(bf16)
    grad_mixed = meet(grad_mixed, put_down, put_up)
    proj_bf, proj_sums = attend_back(proj, grad_mixed)
    grad_b_query, grad_b_value = proj_sums[0], proj_sums[1]
    proj_bf = meet(proj_bf, put_down, put_up)
    grad_qkv = [dot_head(normed_a, proj_bf[part]).astype(bf16) for part in range(3)]
    grad_qkv[0] = meet(grad_qkv[0], put_down, put_up)
    put_rest = Flow(scatter_bulk(grid, grad_qkv + [grad_w_out], ORDER))
    proj_bf = after(proj_bf, *grad_qkv)
    grad_normed_a = sum(
        dot_tail(proj_bf[part], w_qkv[:, part * D : (part + 1) * D]) for part in range(3)
    ).reshape(count, TOK, D)
    grad_normed_a = meet(grad_normed_a, put_up, put_rest)
    _, pull_first = jax.vjp(modulate, resid_in, shift_a, scale_a)
    grad_in_norm, grad_shift_a, grad_scale_a = pull_first(grad_normed_a)
    grad_hidden = (grad_mid + grad_in_norm).reshape(rows_all, D)
    grad_b_patch = jnp.sum(grad_hidden, axis=0)
    grad_w_patch = dot_head(grad_hidden.astype(bf16), noisy)

    mods_bf = beside(
        [
            grad_shift_a,
            grad_scale_a,
            grad_gate_a,
            grad_shift_b,
            grad_scale_b,
            grad_gate_b,
            grad_shift_f,
            grad_scale_f,
        ]
    )
    grad_cond = jax.vjp(jax.nn.silu, cond_own)[1](dot_tail(mods_bf, table_cond[:, : 8 * D]))[0]
    cond_bf = grad_cond.astype(bf16)
    grad_time_act = dot_tail(cond_bf, table_cond[:, 8 * D :])
    grad_time_pre = jax.vjp(jax.nn.silu, time_own)[1](grad_time_act)[0]
    image_grads = beside([mods_bf, grad_time_pre, grad_cond])
    image_grads = meet(image_grads, put_up, put_rest).reshape(-1, 128)
    grad_bias = jnp.concatenate(
        [
            grad_b_query,
            grad_b_value,
            grad_b_out,
            grad_b_up,
            grad_b_down,
            jnp.zeros((10 * D,), jnp.float32),
            grad_b_patch,
        ]
    )
    small = jnp.concatenate(
        [
            grad_bias.reshape(count_all, bias_rows),
            grad_w_patch.reshape(count_all, rows * PATCH_FEAT),
            grad_head.reshape(count_all, rows * PATCH_FEAT),
        ],
        axis=1,
    )
    tall = -(-small.shape[1] // 2048) * SMALL_ROWS
    small = jnp.pad(small, ((0, 0), (0, tall * 128 - small.shape[1])))
    small = small.reshape(sizes + (tall, 128))
    ready = {axis: (put_rest,) for axis in (Z_AXIS, MIX_P, CORE)}
    image_grads, small = gather_and_scatter(grid, image_grads, small, ready)
    small = small.reshape(-1)
    image_grads = image_grads.reshape(image_total, 10 * D)
    mods_bf, cond_bf = image_grads[:, : 8 * D], image_grads[:, 9 * D :]
    grad_w_mods = matmul(cond_act, mods_bf)
    grad_w_time = matmul(time_act, cond_bf)
    grad_w_class = lax.dot_general(
        lax.dynamic_slice_in_dim(cond_bf, my_rows, rows, 1).astype(jnp.float32),
        onehot.astype(jnp.float32),
        (((0,), (0,)), ((), ())),
        precision=lax.Precision.HIGHEST,
        preferred_element_type=jnp.float32,
    )
    own_pre = lax.dynamic_slice_in_dim(image_grads, 8 * D + my_rows, rows, 1)
    grad_t_first = dot_head(own_pre, feats)
    sums = jnp.sum(image_grads.astype(jnp.float32), axis=0)
    known = jnp.pad(sums, (4 * D + FF, D))
    known = lax.dynamic_slice_in_dim(known, lax.axis_index(AXIS) * bias_rows, bias_rows)
    at = bias_rows
    sum_patch = small[at : at + rows * PATCH_FEAT].reshape(rows, PATCH_FEAT)
    at += rows * PATCH_FEAT
    sum_head = small[at : at + rows * PATCH_FEAT].reshape(rows, PATCH_FEAT)

    sum_rest, sum_up, sum_down = last(put_rest), last(put_up), last(put_down)
    grads_in = (sum_rest, sum_up, grad_w_mods, grad_w_time)
    grads_other = (
        sum_down,
        jnp.concatenate([grad_t_first, sum_patch, grad_w_class, sum_head], axis=1),
        (small[:bias_rows] + known)[None],
    )
    masters = (weights_in, weights_down, weights_side, biases[None])
    firsts = (first_in, first_down, first_side, first_bias[None])
    seconds = (second_in, second_down, second_side, second_bias[None])
    shapes = [master.shape for master in masters]
    results = directions(masters, firsts, seconds, grads_in, grads_other)
    loss_spot = jnp.arange(8, dtype=jnp.int32)[:, None] == 3
    sums = sum_small(grid, results[12] + jnp.where(loss_spot, loss_local, 0.0))
    updated = updates(sums, masters, results[8:12])
    norms = updated[4]
    return (
        sums[3, 0],
        updated[0],
        updated[1],
        updated[2],
        updated[3][0],
        results[0],
        results[1],
        results[2],
        results[3][0],
        results[4],
        results[5],
        results[6],
        results[7][0],
        norms[2, :12],
        norms[0, :12],
        norms[1, :12],
    )


def solution(mesh):
    placed = (
        P("fsdp", None, None),
        P("fsdp", None, None),
        P("fsdp"),
        P("fsdp"),
        P("fsdp", None),
        P("fsdp", None),
        P("fsdp", None),
        P("fsdp"),
        P("fsdp", None),
        P("fsdp", None),
        P("fsdp", None),
        P("fsdp"),
        P("fsdp", None),
        P("fsdp", None),
        P("fsdp", None),
        P("fsdp"),
    )
    return jax.shard_map(
        per_device,
        mesh=mesh,
        in_specs=placed,
        out_specs=(
            P(),
            P("fsdp", None),
            P("fsdp", None),
            P("fsdp", None),
            P("fsdp"),
            P("fsdp", None),
            P("fsdp", None),
            P("fsdp", None),
            P("fsdp"),
            P("fsdp", None),
            P("fsdp", None),
            P("fsdp", None),
            P("fsdp"),
            P(),
            P(),
            P(),
        ),
        check_vma=False,
    )
```

```python
from functools import partial
import math

import jax
import jax.numpy as jnp
from jax import lax
from jax.experimental import pallas as pl
from jax.experimental.pallas import tpu as pltpu
from jax.sharding import PartitionSpec as P

D = 1024
HEADS = 16
HEAD_DIM = 64
FF = 4096
CLASSES = 1000
PATCH_FEAT = 16
TFREQ = 256
GRID = 16
TOK = 256
MICRO = 2
STEP = 10
IMG_DEV = 1
SIDE = 1288


BETA_ONE = 0.5
BETA_TWO = 0.5
EPSILON = 1e-06
DECAY = 0.01
RATE = 0.25
NORM_EPS = 1e-06
SMALL_ROWS = 16
AXIS = "fsdp"


def matmul(left, right):
    return jnp.dot(left, right, preferred_element_type=jnp.float32)


def dot_tail(left, right):
    return lax.dot_general(
        left, right, (((1,), (1,)), ((), ())), preferred_element_type=jnp.float32
    )


def dot_head(left, right):
    return lax.dot_general(
        left, right, (((0,), (0,)), ((), ())), preferred_element_type=jnp.float32
    )


def layer_norm(values):
    center = values - jnp.mean(values, axis=-1, keepdims=True)
    return center * lax.rsqrt(jnp.mean(center * center, axis=-1, keepdims=True) + NORM_EPS)


def modulate(values, shift, scale):
    return layer_norm(values) * (1.0 + scale[:, None, :]) + shift[:, None, :]


def noise_scales(steps_part):
    phase = (steps_part.astype(jnp.float32) / 1000.0 + 0.008) / 1.008 * (math.pi / 2.0)
    signal = jnp.cos(phase) * jnp.cos(phase)
    return (jnp.sqrt(signal), jnp.sqrt(1.0 - signal))


def time_features(steps_part):
    half_width = TFREQ // 2
    freqs = jnp.exp(-math.log(10000.0) * jnp.arange(half_width, dtype=jnp.float32) / half_width)
    angles = steps_part.astype(jnp.float32)[:, None] * freqs[None, :]
    return jnp.concatenate([jnp.cos(angles), jnp.sin(angles)], axis=1)


def positions():
    quarter = D // 4
    omega = 1.0 / 10000.0 ** (jnp.arange(quarter, dtype=jnp.float32) / quarter)
    cells = jnp.arange(TOK, dtype=jnp.int32)
    row_pos = (cells // GRID).astype(jnp.float32)[:, None] * omega[None, :]
    col_pos = (cells % GRID).astype(jnp.float32)[:, None] * omega[None, :]
    return jnp.concatenate(
        [jnp.sin(row_pos), jnp.cos(row_pos), jnp.sin(col_pos), jnp.cos(col_pos)], axis=1
    )


def column_blocks():
    return [
        (0, 0, 3 * D),
        (0, 3 * D, 4 * D),
        (0, 4 * D, 4 * D + FF),
        (0, 4 * D + FF, 10 * D + FF),
        (0, 10 * D + FF, 12 * D + FF),
        (0, 12 * D + FF, 13 * D + FF),
        (1, 0, 0),
        (2, 0, TFREQ),
        (2, TFREQ, TFREQ + PATCH_FEAT),
        (2, TFREQ + PATCH_FEAT, TFREQ + PATCH_FEAT + CLASSES),
        (2, TFREQ + PATCH_FEAT + CLASSES, SIDE),
        (3, 0, 0),
    ]


def adam_direction(weight, grad, first, second):
    first_new = BETA_ONE * first + (1.0 - BETA_ONE) * grad
    second_new = BETA_TWO * second + (1.0 - BETA_TWO) * grad * grad
    direction = (
        first_new
        / (1.0 - BETA_ONE**STEP)
        / (jnp.sqrt(second_new / (1.0 - BETA_TWO**STEP)) + EPSILON)
        + DECAY * weight
    )
    return (first_new, second_new, direction)


def column_chunks(edges, shapes):
    blocks = column_blocks()
    chunks = []
    for kind in (1, 2, 3):
        parts = [
            (block, start, stop or shapes[kind][1])
            for block, (other, start, stop) in enumerate(blocks)
            if other == kind
        ]
        chunks.append((kind, len(edges) - 2 + kind, 0, 0, shapes[kind][1], parts))
    for number in range(len(edges) - 1):
        for low in range(edges[number], edges[number + 1], 4 * D):
            high = min(low + 4 * D, edges[number + 1])
            parts = [
                (block, max(start, low), min(stop, high))
                for block, (kind, start, stop) in enumerate(blocks)
                if kind == 0 and max(start, low) < min(stop, high)
            ]
            chunks.append((0, number, low - edges[number], low, high, parts))
    return chunks


def span(ref, low, high):
    return ref if (low, high) == (0, ref.shape[1]) else ref.at[:, pl.ds(low, high - low)]


def direction_kernel(edges, shapes, *refs):
    weights, firsts, seconds = refs[0:4], refs[4:8], refs[8:12]
    count = len(edges) - 1 + 3
    grads, outs = refs[12 : 12 + count], refs[12 + count : 25 + count]
    scratch, in_sems, out_sems = refs[25 + count : -2], refs[-2], refs[-1]
    lanes = lax.broadcasted_iota(jnp.int32, (8, 128), 1)
    lines = lax.broadcasted_iota(jnp.int32, (8, 128), 0)
    sums = jnp.zeros((8, 128), jnp.float32)
    chunks = column_chunks(edges, shapes)
    loads, stores = [], []
    for index, (kind, number, at, low, high, _) in enumerate(chunks):
        sources = [span(group[kind], low, high) for group in (weights, firsts, seconds)]
        sources.append(span(grads[number], at, at + high - low))
        held = scratch[7 * kind : 7 * kind + 4]
        loads.append(
            [
                pltpu.make_async_copy(
                    source, span(held[slot], low, high), in_sems.at[index, slot]
                )
                for slot, source in enumerate(sources)
            ]
        )
        for copy in loads[-1]:
            copy.start()
    for index, (kind, _, _, low, high, parts) in enumerate(chunks):
        held, made = scratch[7 * kind : 7 * kind + 4], scratch[7 * kind + 4 : 7 * kind + 7]
        for copy in loads[index]:
            copy.wait()
        for block, start, stop in parts:
            columns = slice(start, stop)
            weight = held[0][:, columns]
            results = adam_direction(
                weight, held[3][:, columns], held[1][:, columns], held[2][:, columns]
            )
            for target, result in zip(made, results):
                target[:, columns] = result
            here = lanes == block
            sums = sums + jnp.where(here & (lines == 0), jnp.sum(weight * weight), 0.0)
            sums = sums + jnp.where(here & (lines == 1), jnp.sum(results[2] * results[2]), 0.0)
        for slot in range(3):
            stores.append(
                pltpu.make_async_copy(
                    span(made[slot], low, high),
                    span(outs[4 * slot + kind], low, high),
                    out_sems.at[index, slot],
                )
            )
            stores[-1].start()
    outs[12][...] = sums
    for copy in stores:
        copy.wait()


def lamb_call(kernel, args, first_specs, shapes, held, slots):
    any_space = pl.BlockSpec(memory_space=pl.ANY)
    size = sum(arg.size for arg in args) + sum(math.prod(shape) for shape in shapes)
    return pl.pallas_call(
        kernel,
        out_shape=[jax.ShapeDtypeStruct(shape, jnp.float32) for shape in shapes],
        in_specs=first_specs + [any_space] * (len(args) - len(first_specs)),
        out_specs=[any_space] * (len(shapes) - 1) + [pl.BlockSpec(memory_space=pltpu.VMEM)],
        scratch_shapes=[pltpu.VMEM(shape, jnp.float32) for shape in held]
        + [pltpu.SemaphoreType.DMA(slot) for slot in slots],
        compiler_params=pltpu.CompilerParams(vmem_limit_bytes=60 * 2**20),
        cost_estimate=pl.CostEstimate(
            flops=10 * size, bytes_accessed=4 * size, transcendentals=size // 8
        ),
    )(*args)


def directions(masters, firsts, seconds, grads_in, grads_other):
    edges = [0]
    for grad in grads_in:
        edges.append(edges[-1] + grad.shape[1])
    shapes = [master.shape for master in masters]
    return lamb_call(
        partial(direction_kernel, edges, shapes),
        masters + firsts + seconds + grads_in + grads_other,
        [],
        shapes * 3 + [(8, 128)],
        [shape for shape in shapes for _ in range(7)],
        [(len(column_chunks(edges, shapes)), slot) for slot in (4, 3)],
    )


def update_kernel(edges, shapes, sums_ref, *refs):
    weights, steps, outs = refs[0:4], refs[4:8], refs[8:13]
    scratch, in_sems, out_sems = refs[13:-2], refs[-2], refs[-1]
    norms = jnp.sqrt(sums_ref[...])
    trust = norms[0:1] / norms[1:2]
    line = lax.broadcasted_iota(jnp.int32, (8, 128), 0)
    outs[4][...] = jnp.where(line == 2, trust, norms)
    chunks = column_chunks(edges, shapes)
    loads, stores = [], []
    for index, (kind, _, _, low, high, _) in enumerate(chunks):
        loads.append(
            [
                pltpu.make_async_copy(
                    span(source[kind], low, high),
                    span(scratch[3 * kind + slot], low, high),
                    in_sems.at[index, slot],
                )
                for slot, source in enumerate((weights, steps))
            ]
        )
        for copy in loads[-1]:
            copy.start()
    for index, (kind, _, _, low, high, parts) in enumerate(chunks):
        held, made = scratch[3 * kind : 3 * kind + 2], scratch[3 * kind + 2]
        for copy in loads[index]:
            copy.wait()
        for block, start, stop in parts:
            columns = slice(start, stop)
            factor = RATE * trust[0:1, block : block + 1]
            made[:, columns] = held[0][:, columns] - factor * held[1][:, columns]
        stores.append(
            pltpu.make_async_copy(
                span(made, low, high), span(outs[kind], low, high), out_sems.at[index]
            )
        )
        stores[-1].start()
    for copy in stores:
        copy.wait()


def updates(sums, masters, steps):
    edges = [0, masters[0].shape[1]]
    shapes = [master.shape for master in masters]
    chunks = len(column_chunks(edges, shapes))
    return lamb_call(
        partial(update_kernel, edges, shapes),
        (sums,) + masters + tuple(steps),
        [pl.BlockSpec(memory_space=pltpu.VMEM)],
        shapes + [(8, 128)],
        [shape for shape in shapes for _ in range(3)],
        [(chunks, 2), (chunks,)],
    )


Z_AXIS, Y_AXIS, X_AXIS, CORE, MIX_P, MIX_Q = range(6)


class Grid:
    def __init__(self, count):
        if count == 32:
            sizes = (4, 2, 2, 2)
        elif count == 256:
            sizes = (8, 4, 4, 2)
        else:
            sizes = (count // 2, 1, 1, 2)
        self.count = count
        self.shape = sizes
        self.sizes = sizes + (sizes[X_AXIS], sizes[Y_AXIS])
        index = lax.axis_index(AXIS)
        self.coords = self.split(index)
        mixed = [
            jnp.where(self.coords[CORE] == 0, self.coords[X_AXIS], self.coords[Y_AXIS]),
            jnp.where(self.coords[CORE] == 0, self.coords[Y_AXIS], self.coords[X_AXIS]),
        ]
        self.coords = self.coords + tuple(mixed)

    def split(self, index):
        coords = []
        for size in reversed(self.shape):
            coords.append(index % size)
            index = index // size
        return tuple(reversed(coords))

    def join(self, coords):
        index = 0
        for size, place in zip(self.shape, coords):
            index = index * size + place
        return index

    def move(self, values, axis, change):
        pairs = []
        for source in range(self.count):
            coords = list(self.split(source))
            real = axis
            if axis == MIX_P:
                real = X_AXIS if coords[CORE] == 0 else Y_AXIS
            if axis == MIX_Q:
                real = Y_AXIS if coords[CORE] == 0 else X_AXIS
            coords[real] = change(coords[real])
            pairs.append((source, self.join(coords)))
        return lax.ppermute(values, AXIS, pairs)

    def ahead(self, values, axis, shift):
        size = self.sizes[axis]
        return self.move(values, axis, lambda place: (place - shift) % size)

    def flip(self, values, axis, bit):
        return self.move(values, axis, lambda place: place ^ bit)

    def place(self, axis, shift):
        return (self.coords[axis] + shift) % self.sizes[axis]


def after(values, *others):
    return lax.optimization_barrier((values,) + others)[0] if others else values


def gather_small(grid, values, order):
    for axis in order:
        values = values[None]
        bit = 1
        while bit < grid.sizes[axis]:
            other = grid.flip(values, axis, bit)
            lower = grid.coords[axis] // bit % 2 == 0
            values = jnp.concatenate(
                [jnp.where(lower, values, other), jnp.where(lower, other, values)]
            )
            bit *= 2
    return values


def scatter_axis(grid, values, axis, dim):
    bit = grid.sizes[axis]
    while bit > 1:
        bit //= 2
        upper = grid.coords[axis] // bit % 2
        kept = lax.dynamic_slice_in_dim(values, upper * bit, bit, dim)
        sent = lax.dynamic_slice_in_dim(values, (1 - upper) * bit, bit, dim)
        values = kept + grid.flip(sent, axis, bit)
    return lax.squeeze(values, (dim,))


def scatter_small(grid, values):
    for axis in (CORE, X_AXIS, Y_AXIS, Z_AXIS):
        values = scatter_axis(grid, values, axis, axis)
    return values


def beside_kernel(*refs):
    parts, out = refs[:-1], refs[-1]
    at = 0
    for part in parts:
        out[:, at : at + part.shape[1]] = part[...].astype(out.dtype)
        at += part.shape[1]


def beside(parts):
    vmem = pl.BlockSpec(memory_space=pltpu.VMEM)
    shape = (parts[0].shape[0], sum(part.shape[1] for part in parts))
    return pl.pallas_call(
        beside_kernel,
        out_shape=jax.ShapeDtypeStruct(shape, jnp.bfloat16),
        in_specs=[vmem] * len(parts),
        out_specs=vmem,
    )(*parts)


def gather_and_scatter(grid, values, table, ready):
    turned = jnp.swapaxes(table, Y_AXIS, X_AXIS)
    table = jnp.where(grid.coords[CORE] == 0, table, turned)
    for axis in (Z_AXIS, MIX_Q, MIX_P, CORE):
        values = values[None]
        bit = 1
        while bit < grid.sizes[axis]:
            lower = grid.coords[axis] // bit % 2 == 0
            halves = table.reshape((table.shape[0] // 2, 2) + table.shape[1:])
            even, odd = halves[:, 0], halves[:, 1]
            kept = jnp.where(lower, even, odd)
            sent = jnp.where(lower, odd, even).astype(values.dtype)
            count = values.size // 128
            packed = jnp.concatenate([values.reshape(-1, 128), sent.reshape(-1, 128)])
            packed = grid.flip(packed, axis, bit)
            other = packed[:count].reshape(values.shape)
            values = jnp.concatenate(
                [jnp.where(lower, values, other), jnp.where(lower, other, values)]
            )
            table = kept + packed[count:].reshape(kept.shape).astype(jnp.float32)
            bit *= 2
        table = table[0]
        values = meet(values, *ready.get(axis, ()))
    return values, table


class Flow:
    def __init__(self, steps):
        self.steps = steps
        self.out = next(steps)


def meet(values, *flows):
    given = [values] + [array for flow in flows for array in flow.out]
    given = list(lax.optimization_barrier(tuple(given)))
    values = given.pop(0)
    for flow in flows:
        count = len(flow.out)
        flow.out = flow.steps.send(given[:count])
        given = given[count:]
    return values


def last(flow):
    while isinstance(flow.out, list):
        flow.out = flow.steps.send(flow.out)
    return flow.out


def sum_small(grid, values):
    for axis in (3, 2, 1, 0):
        bit = 1
        while bit < grid.sizes[axis]:
            values = values + grid.flip(values, axis, bit)
            bit *= 2
    return values


def relative_places(grid, order, crossed=False):
    dims = (CORE,) + tuple(reversed(order))
    number = jnp.arange(grid.count, dtype=jnp.int32)
    shifts = {}
    for axis in reversed(dims):
        shifts[axis] = number % grid.sizes[axis]
        number = number // grid.sizes[axis]
    core = (grid.coords[CORE] + shifts[CORE]) % grid.sizes[CORE]
    first = core == 0

    def place(axis, own):
        if axis == Z_AXIS and crossed:
            return own ^ shifts[axis]
        return (own + shifts[axis]) % grid.sizes[axis]

    x_own, y_own = grid.coords[X_AXIS], grid.coords[Y_AXIS]
    p_place = place(MIX_P, jnp.where(first, x_own, y_own))
    q_place = place(MIX_Q, jnp.where(first, y_own, x_own))
    return grid.join(
        (
            place(Z_AXIS, grid.coords[Z_AXIS]),
            jnp.where(first, q_place, p_place),
            jnp.where(first, p_place, q_place),
            core,
        )
    ).astype(jnp.int32)


def place_kernel(layout, places, *refs):
    parts, tables, sems = refs[: -1 - len(layout)], refs[-1 - len(layout) : -1], refs[-1]
    copies = []
    entries, rows = parts[0].shape[0], parts[0].shape[1]
    for number, part in enumerate(parts):
        for entry in range(entries):
            place = places[number * entries + entry]
            at = 0
            for table, groups in zip(tables, layout):
                for group in range(groups):
                    copies.append(
                        pltpu.make_async_copy(
                            part.at[entry, :, pl.ds(at, table.shape[2])],
                            table.at[place, pl.ds(group * rows, rows)],
                            sems.at[len(copies)],
                        )
                    )
                    at += table.shape[2]
    for copy in copies:
        copy.start()
    for copy in copies:
        copy.wait()


def gather_bulk(grid, shards, order):
    rows = min(shard.shape[0] for shard in shards)
    layout = [shard.shape[0] // rows for shard in shards]
    pieces = [
        shard[group * rows : (group + 1) * rows]
        for shard, groups in zip(shards, layout)
        for group in range(groups)
    ]
    parts = [jnp.concatenate(pieces, axis=1)]
    columns = parts[0].shape[1]
    for axis in order:
        sent = jnp.stack(parts).reshape((-1, rows, columns))
        parts = [sent]
        for _ in range(1, grid.sizes[axis]):
            parts = parts + (yield [grid.ahead(parts[-1], axis, 1)])
    received = yield [grid.ahead(part, CORE, 1) for part in parts]
    parts = parts + received
    places = relative_places(grid, order)
    shapes = [
        (grid.count, groups * rows, shard.shape[1]) for shard, groups in zip(shards, layout)
    ]
    if rows % 16 == 0:
        tables = pl.pallas_call(
            partial(place_kernel, layout),
            out_shape=[jax.ShapeDtypeStruct(shape, parts[0].dtype) for shape in shapes],
            in_specs=[pl.BlockSpec(memory_space=pltpu.SMEM)]
            + [pl.BlockSpec(memory_space=pl.ANY)] * len(parts),
            out_specs=[pl.BlockSpec(memory_space=pltpu.VMEM)] * len(shapes),
            scratch_shapes=[pltpu.SemaphoreType.DMA((grid.count * sum(layout),))],
            compiler_params=pltpu.CompilerParams(vmem_limit_bytes=32 * 2**20),
            cost_estimate=pl.CostEstimate(
                flops=0, bytes_accessed=4 * grid.count * rows * columns, transcendentals=0
            ),
        )(places, *parts)
    else:
        stacked = jnp.stack(parts).reshape((grid.count, rows, columns))
        stacked = jnp.zeros_like(stacked).at[places].set(stacked)
        tables = []
        for shape, groups in zip(shapes, layout):
            width = groups * shape[2]
            table = stacked[:, :, :width].reshape((grid.count, rows, groups, shape[2]))
            tables.append(table.transpose((0, 2, 1, 3)).reshape(shape))
            stacked = stacked[:, :, width:]
    yield tuple(table.reshape((-1, table.shape[2])) for table in tables)


def pick_kernel(places, *refs):
    tables, picked, sems = refs[:-3], refs[-3:-1], refs[-1]
    copies = []
    for number in range(sum(half.shape[0] for half in picked)):
        half, entry = picked[0], number
        if number >= half.shape[0]:
            half, entry = picked[1], number - half.shape[0]
        at = 0
        for table in tables:
            width = table.shape[2]
            copies.append(
                pltpu.make_async_copy(
                    table.at[places[number]],
                    half.at[entry, :, pl.ds(at, width)],
                    sems.at[len(copies)],
                )
            )
            at += width
    for copy in copies:
        copy.start()
    for copy in copies:
        copy.wait()


def pick_rows(tables, places):
    count, rows = tables[0].shape[:2]
    columns = sum(table.shape[2] for table in tables)
    half = (count // 2, rows, columns)
    if rows % 16:
        picked = jnp.concatenate([table[places] for table in tables], axis=2)
        return picked[: count // 2], picked[count // 2 :]
    return pl.pallas_call(
        pick_kernel,
        out_shape=[jax.ShapeDtypeStruct(half, jnp.bfloat16)] * 2,
        in_specs=[pl.BlockSpec(memory_space=pltpu.SMEM)]
        + [pl.BlockSpec(memory_space=pl.ANY)] * len(tables),
        out_specs=[pl.BlockSpec(memory_space=pltpu.VMEM)] * 2,
        scratch_shapes=[pltpu.SemaphoreType.DMA((count * len(tables),))],
        compiler_params=pltpu.CompilerParams(vmem_limit_bytes=32 * 2**20),
        cost_estimate=pl.CostEstimate(
            flops=0, bytes_accessed=4 * count * rows * columns, transcendentals=0
        ),
    )(places, *tables)


def scatter_bulk(grid, tables, order):
    rows = tables[0].shape[0] // grid.count
    columns = sum(table.shape[1] for table in tables)
    places = relative_places(grid, order, True)
    tables = [table.reshape(grid.count, rows, table.shape[1]) for table in tables]
    axes = tuple(reversed(order))
    dims = tuple(grid.sizes[axis] for axis in axes) + (rows, columns)
    kept, sent = pick_rows(tables, places)
    received = yield [grid.ahead(sent, CORE, 1)]
    terms = [(kept.reshape(dims), (), 1), (received[0].reshape(dims), (), 1)]

    def total(*index):
        return sum(array[prefix + index].astype(jnp.float32) for array, prefix, _ in terms)

    for axis in axes:
        if axis == Z_AXIS:
            bit = 1
            while bit < grid.sizes[axis]:
                sent = sum(
                    array[prefix + (slice(stride, None, 2 * stride),)].astype(jnp.float32)
                    for array, prefix, stride in terms
                )
                received = yield [grid.flip(sent.astype(jnp.bfloat16), axis, bit)]
                terms = [(array, prefix, 2 * stride) for array, prefix, stride in terms]
                terms.append((received[0], (), 1))
                bit *= 2
        else:
            passing = None
            for place in range(1, grid.sizes[axis]):
                here = total(place)
                if passing is not None:
                    here = here + passing.astype(jnp.float32)
                passing = (yield [grid.ahead(here.astype(jnp.bfloat16), axis, 1)])[0]
            terms = [(array, prefix + (0,), 1) for array, prefix, _ in terms]
            terms.append((passing, (), 1))
            continue
        terms = [(array, prefix + (0,), 1) for array, prefix, _ in terms]
    yield total()


HEAD_COLS = 8 * HEAD_DIM


def head_probs(query, key):
    scores = dot_tail(query, key) * HEAD_DIM ** (-0.5)
    weights = jnp.exp(scores - jnp.max(scores, axis=-1, keepdims=True))
    return weights * (1.0 / jnp.sum(weights, axis=-1, keepdims=True))


def head_masks():
    lanes = lax.broadcasted_iota(jnp.int32, (1, 2 * HEAD_DIM), 1)
    first = lanes < HEAD_DIM
    return first, (first.astype(jnp.bfloat16), (~first).astype(jnp.bfloat16))


def attend_kernel(query_ref, key_ref, value_ref, mixed_ref):
    first, masks = head_masks()
    for at in range(0, HEAD_COLS, 2 * HEAD_DIM):
        pair = slice(at, at + 2 * HEAD_DIM)
        query, key, value = query_ref[:, pair], key_ref[:, pair], value_ref[:, pair]
        mixed = [
            matmul(head_probs(query * mask, key).astype(jnp.bfloat16), value) for mask in masks
        ]
        mixed_ref[:, pair] = jnp.where(first, mixed[0], mixed[1]).astype(jnp.bfloat16)


def attend_back_kernel(query_ref, key_ref, value_ref, grad_ref, out_ref, bias_ref):
    first, masks = head_masks()

    @pl.when(pl.program_id(1) == 0)
    def _():
        bias_ref[...] = jnp.zeros_like(bias_ref)

    for at in range(0, HEAD_COLS, 2 * HEAD_DIM):
        pair = slice(at, at + 2 * HEAD_DIM)
        query, key, value = query_ref[:, pair], key_ref[:, pair], value_ref[:, pair]
        grad = grad_ref[:, pair]
        parts = []
        for mask in masks:
            probs = head_probs(query * mask, key)
            grad_probs = dot_tail(grad * mask, value)
            inner = jnp.sum(probs * grad_probs, axis=-1, keepdims=True)
            grad_scores = (probs * (grad_probs - inner)).astype(jnp.bfloat16)
            parts.append(
                (
                    matmul(grad_scores, key) * HEAD_DIM ** (-0.5),
                    dot_head(grad_scores, query) * HEAD_DIM ** (-0.5),
                    dot_head(probs.astype(jnp.bfloat16), grad),
                )
            )
        whole = [jnp.where(first, one, two) for one, two in zip(*parts)]
        for index in range(3):
            out_ref[index, :, pair] = whole[index].astype(jnp.bfloat16)
        bias_ref[0:1, pair] += jnp.sum(whole[0], axis=0, keepdims=True)
        bias_ref[1:2, pair] += jnp.sum(whole[2], axis=0, keepdims=True)


def head_specs():
    groups = D // HEAD_COLS
    return [
        pl.BlockSpec((TOK, HEAD_COLS), lambda group, image, part=part: (image, part * groups + group))
        for part in range(3)
    ]


def attend(proj):
    count = proj.shape[0] // TOK
    flops = 4 * count * HEADS * TOK * TOK * HEAD_DIM
    return pl.pallas_call(
        attend_kernel,
        grid=(D // HEAD_COLS, count),
        out_shape=jax.ShapeDtypeStruct((proj.shape[0], D), jnp.bfloat16),
        in_specs=head_specs(),
        out_specs=pl.BlockSpec((TOK, HEAD_COLS), lambda group, image: (image, group)),
        compiler_params=pltpu.CompilerParams(vmem_limit_bytes=24 * 2**20),
        cost_estimate=pl.CostEstimate(
            flops=4 * flops, bytes_accessed=8 * proj.size, transcendentals=flops // 256
        ),
    )(proj, proj, proj)


def attend_back(proj, grad_mixed):
    count = proj.shape[0] // TOK
    flops = 12 * count * HEADS * TOK * TOK * HEAD_DIM
    block = pl.BlockSpec((TOK, HEAD_COLS), lambda group, image: (image, group))
    return pl.pallas_call(
        attend_back_kernel,
        grid=(D // HEAD_COLS, count),
        out_shape=[
            jax.ShapeDtypeStruct((3, proj.shape[0], D), jnp.bfloat16),
            jax.ShapeDtypeStruct((8, D), jnp.float32),
        ],
        in_specs=head_specs() + [block],
        out_specs=[
            pl.BlockSpec((3, TOK, HEAD_COLS), lambda group, image: (0, image, group)),
            pl.BlockSpec((8, HEAD_COLS), lambda group, image: (0, group)),
        ],
        compiler_params=pltpu.CompilerParams(vmem_limit_bytes=24 * 2**20),
        cost_estimate=pl.CostEstimate(
            flops=3 * flops, bytes_accessed=16 * proj.size, transcendentals=flops // 512
        ),
    )(proj, proj, proj, grad_mixed)


ORDER = (Z_AXIS, MIX_P, MIX_Q)


def per_device(
    latents,
    noise_draw,
    timesteps,
    labels,
    weights_in,
    weights_down,
    weights_side,
    biases,
    first_in,
    first_down,
    first_side,
    first_bias,
    second_in,
    second_down,
    second_side,
    second_bias,
):
    bf16 = jnp.bfloat16
    count_all = lax.axis_size(AXIS)
    grid = Grid(count_all)
    sizes = grid.shape
    count = latents.shape[0]
    rows_all = count * TOK
    image_total = count * count_all
    rows = weights_in.shape[0]
    bias_rows = biases.shape[0]
    my_rows = lax.axis_index(AXIS) * rows
    masters = (weights_in, weights_down, weights_side, biases)
    in_bf = weights_in.astype(bf16)
    down_bf = weights_down.astype(bf16)
    side_bf = weights_side.astype(bf16)
    t_first = side_bf[:, :TFREQ]
    patch_at = TFREQ
    class_at = TFREQ + PATCH_FEAT
    head_at = class_at + CLASSES
    w_class = side_bf[:, class_at:head_at]
    w_mods = in_bf[:, 4 * D + FF : 12 * D + FF]
    w_time = in_bf[:, 12 * D + FF :]

    numbers = jnp.concatenate([timesteps, labels])
    packed = jnp.concatenate(
        [
            biases.astype(bf16),
            side_bf[:, patch_at:class_at].reshape(-1),
            side_bf[:, head_at:].reshape(-1),
            (numbers // 32).astype(bf16),
            (numbers % 32).astype(bf16),
        ]
    )
    width = packed.shape[0]
    tall = -(-width // (SMALL_ROWS * 128)) * SMALL_ROWS
    packed = jnp.pad(packed, (0, tall * 128 - width)).reshape(tall, 128)
    main_bf = weights_in[:, : 4 * D + FF].astype(bf16)
    table_main = lax.all_gather(main_bf, AXIS, axis=0, tiled=True)
    get = Flow(gather_bulk(grid, [down_bf], ORDER))
    spread_all = gather_small(grid, packed, (CORE, X_AXIS, Y_AXIS))
    spread_all = gather_small(grid, meet(spread_all, get), (Z_AXIS,))
    spread_all = spread_all.reshape(count_all, tall * 128)
    bias_full = spread_all[:, :bias_rows].reshape(-1).astype(jnp.float32)
    at = bias_rows
    w_patch = spread_all[:, at : at + rows * PATCH_FEAT].reshape(D, PATCH_FEAT)
    at += rows * PATCH_FEAT
    w_head = spread_all[:, at : at + rows * PATCH_FEAT].reshape(D, PATCH_FEAT)
    at += rows * PATCH_FEAT
    numbers = spread_all[:, at : at + 4 * count].astype(jnp.float32)
    numbers = numbers[:, : 2 * count] * 32.0 + numbers[:, 2 * count :]
    numbers = numbers.reshape(sizes + (2 * count,))
    numbers = jnp.stack(
        [numbers[:, :, :, core].transpose((1, 2, 0, 3) if core else (2, 1, 0, 3)) for core in range(sizes[CORE])]
    ).reshape(count_all, 2 * count)
    steps_all = numbers[:, :count].reshape(image_total)
    labels_all = numbers[:, count:].reshape(image_total).astype(jnp.int32)

    b_qkv = jnp.concatenate([bias_full[:D], jnp.zeros((D,), jnp.float32), bias_full[D : 2 * D]])
    b_out = bias_full[2 * D : 3 * D]
    b_up = bias_full[3 * D : 3 * D + FF]
    b_down = bias_full[3 * D + FF : 4 * D + FF]
    b_mods = bias_full[4 * D + FF : 12 * D + FF]
    b_tfirst = lax.dynamic_slice_in_dim(bias_full[12 * D + FF : 13 * D + FF], my_rows, rows)
    b_time = lax.dynamic_slice_in_dim(bias_full[13 * D + FF : 14 * D + FF], my_rows, rows)
    b_patch = bias_full[14 * D + FF :]

    feats = time_features(steps_all).astype(bf16)
    time_pre = dot_tail(t_first, feats) + b_tfirst[:, None]
    time_act = jax.nn.silu(time_pre).astype(bf16)
    onehot = labels_all[:, None] == jnp.arange(CLASSES, dtype=jnp.int32)[None, :]
    cond_part = lax.dot_general(
        w_time, time_act, (((0,), (0,)), ((), ())), preferred_element_type=jnp.float32
    )
    cond = cond_part.reshape(sizes + (rows, image_total))
    cond = scatter_axis(grid, scatter_axis(grid, cond, CORE, CORE), X_AXIS, X_AXIS)
    cond = scatter_axis(grid, meet(cond, get), Y_AXIS, Y_AXIS)
    cond = scatter_axis(grid, cond, Z_AXIS, Z_AXIS)
    cond = cond + b_time[:, None] + dot_tail(w_class, onehot.astype(bf16))
    cond_act = jax.nn.silu(cond).astype(bf16)

    def own_columns(part):
        wide = jnp.zeros((image_total, D), jnp.float32)
        return lax.dynamic_update_slice(wide, part.T, (0, my_rows))

    mods = jnp.concatenate(
        [dot_head(cond_act, w_mods), own_columns(cond), own_columns(time_pre)], axis=1
    )
    mods = mods.reshape(sizes[CORE], sizes[X_AXIS], sizes[Y_AXIS], sizes[Z_AXIS] * count, 10 * D)
    mods = meet(scatter_axis(grid, mods, CORE, 0), get)
    mods = scatter_axis(grid, mods, MIX_P, 0)
    mods = scatter_axis(grid, mods, MIX_Q, 0)
    mods = mods.reshape(sizes[Z_AXIS], count * 10 * D // 128, 128)
    total = lax.dynamic_index_in_dim(mods, grid.coords[Z_AXIS], 0, keepdims=False)
    for shift in range(1, sizes[Z_AXIS]):
        part = lax.dynamic_index_in_dim(mods, grid.place(Z_AXIS, -shift), 0, keepdims=False)
        total = total + grid.ahead(part, Z_AXIS, shift)
    mods = meet(total.reshape(count, 10 * D), get)
    cond_own, time_own = mods[:, 8 * D : 9 * D], mods[:, 9 * D :]
    mods = mods[:, : 8 * D] + b_mods
    shift_a, scale_a, gate_a, shift_b, scale_b, gate_b, shift_f, scale_f = jnp.split(
        mods, 8, axis=1
    )

    w_qkv, w_out = table_main[:, : 3 * D], table_main[:, 3 * D : 4 * D]
    table_up = table_main[:, 4 * D :]

    signal, spread = noise_scales(timesteps)
    noise_rows = noise_draw.astype(jnp.float32)
    noisy = signal[:, None, None] * latents.astype(jnp.float32) + spread[:, None, None] * noise_rows
    noisy = noisy.astype(bf16).reshape(rows_all, PATCH_FEAT)
    hidden = dot_tail(noisy, w_patch) + b_patch + jnp.tile(positions(), (count, 1))
    resid_in = hidden.reshape(count, TOK, D)
    normed_a = modulate(resid_in, shift_a, scale_a).astype(bf16).reshape(rows_all, D)
    proj = (matmul(normed_a, w_qkv) + b_qkv).astype(bf16)
    mixed = meet(attend(proj), get)
    tail_bf = after(in_bf[:, 4 * D + FF :], mods)
    table_cond = lax.all_gather(tail_bf, AXIS, axis=0, tiled=True)
    attended = (matmul(mixed, w_out) + b_out).reshape(count, TOK, D)
    resid_mid = resid_in + gate_a[:, None, :] * attended
    normed_b = modulate(resid_mid, shift_b, scale_b).astype(bf16).reshape(rows_all, D)
    normed_b = meet(normed_b, get)
    (table_down,) = last(get)
    upper = matmul(normed_b, table_up) + b_up
    active, pull_gelu = jax.vjp(partial(jax.nn.gelu, approximate=True), upper)
    slope = pull_gelu(jnp.ones_like(upper))[0]
    active, slope = lax.optimization_barrier((active.astype(bf16), slope))
    lowered = matmul(active, table_down) + b_down
    lowered = lowered.reshape(count, TOK, D)
    resid_out = resid_mid + gate_b[:, None, :] * lowered
    normed_c = modulate(resid_out, shift_f, scale_f).astype(bf16).reshape(rows_all, D)
    predicted = matmul(normed_c, w_head)
    error = predicted - noise_rows.reshape(rows_all, PATCH_FEAT)
    loss_local = jnp.sum(error * error)
    grad_pred = (2.0 / image_total * error).astype(bf16)

    grad_head = dot_head(normed_c, grad_pred)
    grad_normed_c = dot_tail(grad_pred, w_head).reshape(count, TOK, D)
    _, pull_final = jax.vjp(modulate, resid_out, shift_f, scale_f)
    grad_out, grad_shift_f, grad_scale_f = pull_final(grad_normed_c)
    grad_gate_b = jnp.sum(grad_out * lowered, axis=1)
    grad_lowered = (grad_out * gate_b[:, None, :]).reshape(rows_all, D)
    grad_b_down = jnp.sum(grad_lowered, axis=0)
    lowered_bf = grad_lowered.astype(bf16)
    grad_w_down = dot_head(active, lowered_bf).astype(bf16)
    put_down = Flow(scatter_bulk(grid, [grad_w_down], ORDER))
    lowered_bf = after(lowered_bf, grad_w_down)
    grad_active = dot_tail(lowered_bf, table_down)
    grad_upper = grad_active * slope
    grad_b_up = jnp.sum(grad_upper, axis=0)
    upper_bf = grad_upper.astype(bf16)
    upper_bf = meet(upper_bf, put_down)
    grad_w_up = dot_head(normed_b, upper_bf).astype(bf16)
    put_up = Flow(scatter_bulk(grid, [grad_w_up], ORDER))
    upper_bf = after(upper_bf, grad_w_up)
    grad_normed_b = dot_tail(upper_bf, table_up).reshape(count, TOK, D)
    grad_normed_b = meet(grad_normed_b, put_down)
    _, pull_mid = jax.vjp(modulate, resid_mid, shift_b, scale_b)
    grad_mid_norm, grad_shift_b, grad_scale_b = pull_mid(grad_normed_b)
    grad_mid = grad_out + grad_mid_norm
    grad_gate_a = jnp.sum(grad_mid * attended, axis=1)
    grad_attended = (grad_mid * gate_a[:, None, :]).reshape(rows_all, D)
    grad_b_out = jnp.sum(grad_attended, axis=0)
    attended_bf = grad_attended.astype(bf16)
    grad_w_out = dot_head(mixed, attended_bf).astype(bf16)
    grad_mixed = dot_tail(attended_bf, w_out).astype(bf16)
    grad_mixed = meet(grad_mixed, put_down, put_up)
    proj_bf, proj_sums = attend_back(proj, grad_mixed)
    grad_b_query, grad_b_value = proj_sums[0], proj_sums[1]
    proj_bf = meet(proj_bf, put_down, put_up)
    grad_qkv = [dot_head(normed_a, proj_bf[part]).astype(bf16) for part in range(3)]
    grad_qkv[0] = meet(grad_qkv[0], put_down, put_up)
    put_rest = Flow(scatter_bulk(grid, grad_qkv + [grad_w_out], ORDER))
    proj_bf = after(proj_bf, *grad_qkv)
    grad_normed_a = sum(
        dot_tail(proj_bf[part], w_qkv[:, part * D : (part + 1) * D]) for part in range(3)
    ).reshape(count, TOK, D)
    grad_normed_a = meet(grad_normed_a, put_up, put_rest)
    _, pull_first = jax.vjp(modulate, resid_in, shift_a, scale_a)
    grad_in_norm, grad_shift_a, grad_scale_a = pull_first(grad_normed_a)
    grad_hidden = (grad_mid + grad_in_norm).reshape(rows_all, D)
    grad_b_patch = jnp.sum(grad_hidden, axis=0)
    grad_w_patch = dot_head(grad_hidden.astype(bf16), noisy)

    mods_bf = beside(
        [
            grad_shift_a,
            grad_scale_a,
            grad_gate_a,
            grad_shift_b,
            grad_scale_b,
            grad_gate_b,
            grad_shift_f,
            grad_scale_f,
        ]
    )
    grad_cond = jax.vjp(jax.nn.silu, cond_own)[1](dot_tail(mods_bf, table_cond[:, : 8 * D]))[0]
    cond_bf = grad_cond.astype(bf16)
    grad_time_act = dot_tail(cond_bf, table_cond[:, 8 * D :])
    grad_time_pre = jax.vjp(jax.nn.silu, time_own)[1](grad_time_act)[0]
    image_grads = beside([mods_bf, grad_time_pre, grad_cond])
    image_grads = meet(image_grads, put_up, put_rest).reshape(-1, 128)
    grad_bias = jnp.concatenate(
        [
            grad_b_query,
            grad_b_value,
            grad_b_out,
            grad_b_up,
            grad_b_down,
            jnp.zeros((10 * D,), jnp.float32),
            grad_b_patch,
        ]
    )
    small = jnp.concatenate(
        [
            grad_bias.reshape(count_all, bias_rows),
            grad_w_patch.reshape(count_all, rows * PATCH_FEAT),
            grad_head.reshape(count_all, rows * PATCH_FEAT),
        ],
        axis=1,
    )
    tall = -(-small.shape[1] // 2048) * SMALL_ROWS
    small = jnp.pad(small, ((0, 0), (0, tall * 128 - small.shape[1])))
    small = small.reshape(sizes + (tall, 128))
    ready = {axis: (put_rest,) for axis in (Z_AXIS, MIX_P, CORE)}
    image_grads, small = gather_and_scatter(grid, image_grads, small, ready)
    small = small.reshape(-1)
    image_grads = image_grads.reshape(image_total, 10 * D)
    mods_bf, cond_bf = image_grads[:, : 8 * D], image_grads[:, 9 * D :]
    grad_w_mods = matmul(cond_act, mods_bf)
    grad_w_time = matmul(time_act, cond_bf)
    grad_w_class = lax.dot_general(
        lax.dynamic_slice_in_dim(cond_bf, my_rows, rows, 1).astype(jnp.float32),
        onehot.astype(jnp.float32),
        (((0,), (0,)), ((), ())),
        precision=lax.Precision.HIGHEST,
        preferred_element_type=jnp.float32,
    )
    own_pre = lax.dynamic_slice_in_dim(image_grads, 8 * D + my_rows, rows, 1)
    grad_t_first = dot_head(own_pre, feats)
    sums = jnp.sum(image_grads.astype(jnp.float32), axis=0)
    known = jnp.pad(sums, (4 * D + FF, D))
    known = lax.dynamic_slice_in_dim(known, lax.axis_index(AXIS) * bias_rows, bias_rows)
    at = bias_rows
    sum_patch = small[at : at + rows * PATCH_FEAT].reshape(rows, PATCH_FEAT)
    at += rows * PATCH_FEAT
    sum_head = small[at : at + rows * PATCH_FEAT].reshape(rows, PATCH_FEAT)

    sum_rest, sum_up, sum_down = last(put_rest), last(put_up), last(put_down)
    grads_in = (sum_rest, sum_up, grad_w_mods, grad_w_time)
    grads_other = (
        sum_down,
        jnp.concatenate([grad_t_first, sum_patch, grad_w_class, sum_head], axis=1),
        (small[:bias_rows] + known)[None],
    )
    masters = (weights_in, weights_down, weights_side, biases[None])
    firsts = (first_in, first_down, first_side, first_bias[None])
    seconds = (second_in, second_down, second_side, second_bias[None])
    shapes = [master.shape for master in masters]
    results = directions(masters, firsts, seconds, grads_in, grads_other)
    loss_spot = jnp.arange(8, dtype=jnp.int32)[:, None] == 3
    sums = sum_small(grid, results[12] + jnp.where(loss_spot, loss_local, 0.0))
    updated = updates(sums, masters, results[8:12])
    norms = updated[4]
    return (
        sums[3, 0],
        updated[0],
        updated[1],
        updated[2],
        updated[3][0],
        results[0],
        results[1],
        results[2],
        results[3][0],
        results[4],
        results[5],
        results[6],
        results[7][0],
        norms[2, :12],
        norms[0, :12],
        norms[1, :12],
    )


def solution(mesh):
    placed = (
        P("fsdp", None, None),
        P("fsdp", None, None),
        P("fsdp"),
        P("fsdp"),
        P("fsdp", None),
        P("fsdp", None),
        P("fsdp", None),
        P("fsdp"),
        P("fsdp", None),
        P("fsdp", None),
        P("fsdp", None),
        P("fsdp"),
        P("fsdp", None),
        P("fsdp", None),
        P("fsdp", None),
        P("fsdp"),
    )
    return jax.shard_map(
        per_device,
        mesh=mesh,
        in_specs=placed,
        out_specs=(
            P(),
            P("fsdp", None),
            P("fsdp", None),
            P("fsdp", None),
            P("fsdp"),
            P("fsdp", None),
            P("fsdp", None),
            P("fsdp", None),
            P("fsdp"),
            P("fsdp", None),
            P("fsdp", None),
            P("fsdp", None),
            P("fsdp"),
            P(),
            P(),
            P(),
        ),
        check_vma=False,
    )
```

```python
from functools import partial
import math

import jax
import jax.numpy as jnp
from jax import lax
from jax.experimental import pallas as pl
from jax.experimental.pallas import tpu as pltpu
from jax.sharding import PartitionSpec as P

D = 1024
HEADS = 16
HEAD_DIM = 64
FF = 4096
CLASSES = 1000
PATCH_FEAT = 16
TFREQ = 256
GRID = 16
TOK = 256
MICRO = 2
STEP = 10
IMG_DEV = 1
SIDE = 1288


BETA_ONE = 0.5
BETA_TWO = 0.5
EPSILON = 1e-06
DECAY = 0.01
RATE = 0.25
NORM_EPS = 1e-06
SMALL_ROWS = 16
AXIS = "fsdp"


def matmul(left, right):
    return jnp.dot(left, right, preferred_element_type=jnp.float32)


def dot_tail(left, right):
    return lax.dot_general(
        left, right, (((1,), (1,)), ((), ())), preferred_element_type=jnp.float32
    )


def dot_head(left, right):
    return lax.dot_general(
        left, right, (((0,), (0,)), ((), ())), preferred_element_type=jnp.float32
    )


def layer_norm(values):
    center = values - jnp.mean(values, axis=-1, keepdims=True)
    return center * lax.rsqrt(jnp.mean(center * center, axis=-1, keepdims=True) + NORM_EPS)


def modulate(values, shift, scale):
    return layer_norm(values) * (1.0 + scale[:, None, :]) + shift[:, None, :]


def noise_scales(steps_part):
    phase = (steps_part.astype(jnp.float32) / 1000.0 + 0.008) / 1.008 * (math.pi / 2.0)
    signal = jnp.cos(phase) * jnp.cos(phase)
    return (jnp.sqrt(signal), jnp.sqrt(1.0 - signal))


def time_features(steps_part):
    half_width = TFREQ // 2
    freqs = jnp.exp(-math.log(10000.0) * jnp.arange(half_width, dtype=jnp.float32) / half_width)
    angles = steps_part.astype(jnp.float32)[:, None] * freqs[None, :]
    return jnp.concatenate([jnp.cos(angles), jnp.sin(angles)], axis=1)


def positions():
    quarter = D // 4
    omega = 1.0 / 10000.0 ** (jnp.arange(quarter, dtype=jnp.float32) / quarter)
    cells = jnp.arange(TOK, dtype=jnp.int32)
    row_pos = (cells // GRID).astype(jnp.float32)[:, None] * omega[None, :]
    col_pos = (cells % GRID).astype(jnp.float32)[:, None] * omega[None, :]
    return jnp.concatenate(
        [jnp.sin(row_pos), jnp.cos(row_pos), jnp.sin(col_pos), jnp.cos(col_pos)], axis=1
    )


def column_blocks():
    return [
        (0, 0, 3 * D),
        (0, 3 * D, 4 * D),
        (0, 4 * D, 4 * D + FF),
        (0, 4 * D + FF, 10 * D + FF),
        (0, 10 * D + FF, 12 * D + FF),
        (0, 12 * D + FF, 13 * D + FF),
        (1, 0, 0),
        (2, 0, TFREQ),
        (2, TFREQ, TFREQ + PATCH_FEAT),
        (2, TFREQ + PATCH_FEAT, TFREQ + PATCH_FEAT + CLASSES),
        (2, TFREQ + PATCH_FEAT + CLASSES, SIDE),
        (3, 0, 0),
    ]


def adam_direction(weight, grad, first, second):
    first_new = BETA_ONE * first + (1.0 - BETA_ONE) * grad
    second_new = BETA_TWO * second + (1.0 - BETA_TWO) * grad * grad
    direction = (
        first_new
        / (1.0 - BETA_ONE**STEP)
        / (jnp.sqrt(second_new / (1.0 - BETA_TWO**STEP)) + EPSILON)
        + DECAY * weight
    )
    return (first_new, second_new, direction)


def column_chunks(edges, shapes):
    blocks = column_blocks()
    chunks = []
    for kind in (1, 2, 3):
        parts = [
            (block, start, stop or shapes[kind][1])
            for block, (other, start, stop) in enumerate(blocks)
            if other == kind
        ]
        chunks.append((kind, len(edges) - 2 + kind, 0, 0, shapes[kind][1], parts))
    for number in range(len(edges) - 1):
        for low in range(edges[number], edges[number + 1], 4 * D):
            high = min(low + 4 * D, edges[number + 1])
            parts = [
                (block, max(start, low), min(stop, high))
                for block, (kind, start, stop) in enumerate(blocks)
                if kind == 0 and max(start, low) < min(stop, high)
            ]
            chunks.append((0, number, low - edges[number], low, high, parts))
    return chunks


def span(ref, low, high):
    return ref if (low, high) == (0, ref.shape[1]) else ref.at[:, pl.ds(low, high - low)]


def direction_kernel(edges, shapes, *refs):
    weights, firsts, seconds = refs[0:4], refs[4:8], refs[8:12]
    count = len(edges) - 1 + 3
    grads, outs = refs[12 : 12 + count], refs[12 + count : 25 + count]
    scratch, in_sems, out_sems = refs[25 + count : -2], refs[-2], refs[-1]
    lanes = lax.broadcasted_iota(jnp.int32, (8, 128), 1)
    lines = lax.broadcasted_iota(jnp.int32, (8, 128), 0)
    sums = jnp.zeros((8, 128), jnp.float32)
    chunks = column_chunks(edges, shapes)
    loads, stores = [], []
    for index, (kind, number, at, low, high, _) in enumerate(chunks):
        sources = [span(group[kind], low, high) for group in (weights, firsts, seconds)]
        sources.append(span(grads[number], at, at + high - low))
        held = scratch[7 * kind : 7 * kind + 4]
        loads.append(
            [
                pltpu.make_async_copy(
                    source, span(held[slot], low, high), in_sems.at[index, slot]
                )
                for slot, source in enumerate(sources)
            ]
        )
        for copy in loads[-1]:
            copy.start()
    for index, (kind, _, _, low, high, parts) in enumerate(chunks):
        held, made = scratch[7 * kind : 7 * kind + 4], scratch[7 * kind + 4 : 7 * kind + 7]
        for copy in loads[index]:
            copy.wait()
        for block, start, stop in parts:
            columns = slice(start, stop)
            weight = held[0][:, columns]
            results = adam_direction(
                weight, held[3][:, columns], held[1][:, columns], held[2][:, columns]
            )
            for target, result in zip(made, results):
                target[:, columns] = result
            here = lanes == block
            sums = sums + jnp.where(here & (lines == 0), jnp.sum(weight * weight), 0.0)
            sums = sums + jnp.where(here & (lines == 1), jnp.sum(results[2] * results[2]), 0.0)
        for slot in range(3):
            stores.append(
                pltpu.make_async_copy(
                    span(made[slot], low, high),
                    span(outs[4 * slot + kind], low, high),
                    out_sems.at[index, slot],
                )
            )
            stores[-1].start()
    outs[12][...] = sums
    for copy in stores:
        copy.wait()


def lamb_call(kernel, args, first_specs, shapes, held, slots):
    any_space = pl.BlockSpec(memory_space=pl.ANY)
    size = sum(arg.size for arg in args) + sum(math.prod(shape) for shape in shapes)
    return pl.pallas_call(
        kernel,
        out_shape=[jax.ShapeDtypeStruct(shape, jnp.float32) for shape in shapes],
        in_specs=first_specs + [any_space] * (len(args) - len(first_specs)),
        out_specs=[any_space] * (len(shapes) - 1) + [pl.BlockSpec(memory_space=pltpu.VMEM)],
        scratch_shapes=[pltpu.VMEM(shape, jnp.float32) for shape in held]
        + [pltpu.SemaphoreType.DMA(slot) for slot in slots],
        compiler_params=pltpu.CompilerParams(vmem_limit_bytes=60 * 2**20),
        cost_estimate=pl.CostEstimate(
            flops=10 * size, bytes_accessed=4 * size, transcendentals=size // 8
        ),
    )(*args)


def directions(masters, firsts, seconds, grads_in, grads_other):
    edges = [0]
    for grad in grads_in:
        edges.append(edges[-1] + grad.shape[1])
    shapes = [master.shape for master in masters]
    return lamb_call(
        partial(direction_kernel, edges, shapes),
        masters + firsts + seconds + grads_in + grads_other,
        [],
        shapes * 3 + [(8, 128)],
        [shape for shape in shapes for _ in range(7)],
        [(len(column_chunks(edges, shapes)), slot) for slot in (4, 3)],
    )


def update_kernel(edges, shapes, sums_ref, *refs):
    weights, steps, outs = refs[0:4], refs[4:8], refs[8:13]
    scratch, in_sems, out_sems = refs[13:-2], refs[-2], refs[-1]
    norms = jnp.sqrt(sums_ref[...])
    trust = norms[0:1] / norms[1:2]
    line = lax.broadcasted_iota(jnp.int32, (8, 128), 0)
    outs[4][...] = jnp.where(line == 2, trust, norms)
    chunks = column_chunks(edges, shapes)
    loads, stores = [], []
    for index, (kind, _, _, low, high, _) in enumerate(chunks):
        loads.append(
            [
                pltpu.make_async_copy(
                    span(source[kind], low, high),
                    span(scratch[3 * kind + slot], low, high),
                    in_sems.at[index, slot],
                )
                for slot, source in enumerate((weights, steps))
            ]
        )
        for copy in loads[-1]:
            copy.start()
    for index, (kind, _, _, low, high, parts) in enumerate(chunks):
        held, made = scratch[3 * kind : 3 * kind + 2], scratch[3 * kind + 2]
        for copy in loads[index]:
            copy.wait()
        for block, start, stop in parts:
            columns = slice(start, stop)
            factor = RATE * trust[0:1, block : block + 1]
            made[:, columns] = held[0][:, columns] - factor * held[1][:, columns]
        stores.append(
            pltpu.make_async_copy(
                span(made, low, high), span(outs[kind], low, high), out_sems.at[index]
            )
        )
        stores[-1].start()
    for copy in stores:
        copy.wait()


def updates(sums, masters, steps):
    edges = [0, masters[0].shape[1]]
    shapes = [master.shape for master in masters]
    chunks = len(column_chunks(edges, shapes))
    return lamb_call(
        partial(update_kernel, edges, shapes),
        (sums,) + masters + tuple(steps),
        [pl.BlockSpec(memory_space=pltpu.VMEM)],
        shapes + [(8, 128)],
        [shape for shape in shapes for _ in range(3)],
        [(chunks, 2), (chunks,)],
    )


Z_AXIS, Y_AXIS, X_AXIS, CORE, MIX_P, MIX_Q = range(6)


class Grid:
    def __init__(self, count):
        if count == 32:
            sizes = (4, 2, 2, 2)
        elif count == 256:
            sizes = (8, 4, 4, 2)
        else:
            sizes = (count // 2, 1, 1, 2)
        self.count = count
        self.shape = sizes
        self.sizes = sizes + (sizes[X_AXIS], sizes[Y_AXIS])
        index = lax.axis_index(AXIS)
        self.coords = self.split(index)
        mixed = [
            jnp.where(self.coords[CORE] == 0, self.coords[X_AXIS], self.coords[Y_AXIS]),
            jnp.where(self.coords[CORE] == 0, self.coords[Y_AXIS], self.coords[X_AXIS]),
        ]
        self.coords = self.coords + tuple(mixed)

    def split(self, index):
        coords = []
        for size in reversed(self.shape):
            coords.append(index % size)
            index = index // size
        return tuple(reversed(coords))

    def join(self, coords):
        index = 0
        for size, place in zip(self.shape, coords):
            index = index * size + place
        return index

    def move(self, values, axis, change):
        pairs = []
        for source in range(self.count):
            coords = list(self.split(source))
            real = axis
            if axis == MIX_P:
                real = X_AXIS if coords[CORE] == 0 else Y_AXIS
            if axis == MIX_Q:
                real = Y_AXIS if coords[CORE] == 0 else X_AXIS
            coords[real] = change(coords[real])
            pairs.append((source, self.join(coords)))
        return lax.ppermute(values, AXIS, pairs)

    def ahead(self, values, axis, shift):
        size = self.sizes[axis]
        return self.move(values, axis, lambda place: (place - shift) % size)

    def flip(self, values, axis, bit):
        return self.move(values, axis, lambda place: place ^ bit)

    def place(self, axis, shift):
        return (self.coords[axis] + shift) % self.sizes[axis]


def after(values, *others):
    return lax.optimization_barrier((values,) + others)[0] if others else values


def gather_small(grid, values, order):
    for axis in order:
        values = values[None]
        bit = 1
        while bit < grid.sizes[axis]:
            other = grid.flip(values, axis, bit)
            lower = grid.coords[axis] // bit % 2 == 0
            values = jnp.concatenate(
                [jnp.where(lower, values, other), jnp.where(lower, other, values)]
            )
            bit *= 2
    return values


def scatter_axis(grid, values, axis, dim, kind=jnp.float32):
    bit = grid.sizes[axis]
    while bit > 1:
        bit //= 2
        upper = grid.coords[axis] // bit % 2
        kept = lax.dynamic_slice_in_dim(values, upper * bit, bit, dim)
        sent = lax.dynamic_slice_in_dim(values, (1 - upper) * bit, bit, dim)
        sent = grid.flip(sent.astype(kind), axis, bit)
        values = kept + sent.astype(jnp.float32)
    return lax.squeeze(values, (dim,))


def scatter_small(grid, values):
    for axis in (CORE, X_AXIS, Y_AXIS, Z_AXIS):
        values = scatter_axis(grid, values, axis, axis)
    return values


def beside_kernel(*refs):
    parts, out = refs[:-1], refs[-1]
    at = 0
    for part in parts:
        out[:, at : at + part.shape[1]] = part[...].astype(out.dtype)
        at += part.shape[1]


def beside(parts):
    vmem = pl.BlockSpec(memory_space=pltpu.VMEM)
    shape = (parts[0].shape[0], sum(part.shape[1] for part in parts))
    return pl.pallas_call(
        beside_kernel,
        out_shape=jax.ShapeDtypeStruct(shape, jnp.bfloat16),
        in_specs=[vmem] * len(parts),
        out_specs=vmem,
    )(*parts)


def gather_and_scatter(grid, values, table, ready):
    turned = jnp.swapaxes(table, Y_AXIS, X_AXIS)
    table = jnp.where(grid.coords[CORE] == 0, table, turned)
    for axis in (Z_AXIS, MIX_Q, MIX_P, CORE):
        values = values[None]
        bit = 1
        while bit < grid.sizes[axis]:
            lower = grid.coords[axis] // bit % 2 == 0
            halves = table.reshape((table.shape[0] // 2, 2) + table.shape[1:])
            even, odd = halves[:, 0], halves[:, 1]
            kept = jnp.where(lower, even, odd)
            sent = jnp.where(lower, odd, even).astype(values.dtype)
            count = values.size // 128
            packed = jnp.concatenate([values.reshape(-1, 128), sent.reshape(-1, 128)])
            packed = grid.flip(packed, axis, bit)
            other = packed[:count].reshape(values.shape)
            values = jnp.concatenate(
                [jnp.where(lower, values, other), jnp.where(lower, other, values)]
            )
            table = kept + packed[count:].reshape(kept.shape).astype(jnp.float32)
            bit *= 2
        table = table[0]
        values = meet(values, *ready.get(axis, ()))
    return values, table


class Flow:
    def __init__(self, steps):
        self.steps = steps
        self.out = next(steps)


def meet(values, *flows):
    given = [values] + [array for flow in flows for array in flow.out]
    given = list(lax.optimization_barrier(tuple(given)))
    values = given.pop(0)
    for flow in flows:
        count = len(flow.out)
        flow.out = flow.steps.send(given[:count])
        given = given[count:]
    return values


def last(flow):
    while isinstance(flow.out, list):
        flow.out = flow.steps.send(flow.out)
    return flow.out


def sum_small(grid, values):
    for axis in (3, 2, 1, 0):
        bit = 1
        while bit < grid.sizes[axis]:
            values = values + grid.flip(values, axis, bit)
            bit *= 2
    return values


def relative_places(grid, order, crossed=False):
    dims = (CORE,) + tuple(reversed(order))
    number = jnp.arange(grid.count, dtype=jnp.int32)
    shifts = {}
    for axis in reversed(dims):
        shifts[axis] = number % grid.sizes[axis]
        number = number // grid.sizes[axis]
    core = (grid.coords[CORE] + shifts[CORE]) % grid.sizes[CORE]
    first = core == 0

    def place(axis, own):
        if axis == Z_AXIS and crossed:
            return own ^ shifts[axis]
        return (own + shifts[axis]) % grid.sizes[axis]

    x_own, y_own = grid.coords[X_AXIS], grid.coords[Y_AXIS]
    p_place = place(MIX_P, jnp.where(first, x_own, y_own))
    q_place = place(MIX_Q, jnp.where(first, y_own, x_own))
    return grid.join(
        (
            place(Z_AXIS, grid.coords[Z_AXIS]),
            jnp.where(first, q_place, p_place),
            jnp.where(first, p_place, q_place),
            core,
        )
    ).astype(jnp.int32)


def place_kernel(layout, places, *refs):
    parts, tables, sems = refs[: -1 - len(layout)], refs[-1 - len(layout) : -1], refs[-1]
    copies = []
    entries, rows = parts[0].shape[0], parts[0].shape[1]
    for number, part in enumerate(parts):
        for entry in range(entries):
            place = places[number * entries + entry]
            at = 0
            for table, groups in zip(tables, layout):
                for group in range(groups):
                    copies.append(
                        pltpu.make_async_copy(
                            part.at[entry, :, pl.ds(at, table.shape[2])],
                            table.at[place, pl.ds(group * rows, rows)],
                            sems.at[len(copies)],
                        )
                    )
                    at += table.shape[2]
    for copy in copies:
        copy.start()
    for copy in copies:
        copy.wait()


def gather_bulk(grid, shards, order):
    rows = min(shard.shape[0] for shard in shards)
    layout = [shard.shape[0] // rows for shard in shards]
    pieces = [
        shard[group * rows : (group + 1) * rows]
        for shard, groups in zip(shards, layout)
        for group in range(groups)
    ]
    parts = [jnp.concatenate(pieces, axis=1)]
    columns = parts[0].shape[1]
    for axis in order:
        sent = jnp.stack(parts).reshape((-1, rows, columns))
        parts = [sent]
        for _ in range(1, grid.sizes[axis]):
            parts = parts + (yield [grid.ahead(parts[-1], axis, 1)])
    received = yield [grid.ahead(part, CORE, 1) for part in parts]
    parts = parts + received
    places = relative_places(grid, order)
    shapes = [
        (grid.count, groups * rows, shard.shape[1]) for shard, groups in zip(shards, layout)
    ]
    if rows % 16 == 0:
        tables = pl.pallas_call(
            partial(place_kernel, layout),
            out_shape=[jax.ShapeDtypeStruct(shape, parts[0].dtype) for shape in shapes],
            in_specs=[pl.BlockSpec(memory_space=pltpu.SMEM)]
            + [pl.BlockSpec(memory_space=pl.ANY)] * len(parts),
            out_specs=[pl.BlockSpec(memory_space=pltpu.VMEM)] * len(shapes),
            scratch_shapes=[pltpu.SemaphoreType.DMA((grid.count * sum(layout),))],
            compiler_params=pltpu.CompilerParams(vmem_limit_bytes=32 * 2**20),
            cost_estimate=pl.CostEstimate(
                flops=0, bytes_accessed=4 * grid.count * rows * columns, transcendentals=0
            ),
        )(places, *parts)
    else:
        stacked = jnp.stack(parts).reshape((grid.count, rows, columns))
        stacked = jnp.zeros_like(stacked).at[places].set(stacked)
        tables = []
        for shape, groups in zip(shapes, layout):
            width = groups * shape[2]
            table = stacked[:, :, :width].reshape((grid.count, rows, groups, shape[2]))
            tables.append(table.transpose((0, 2, 1, 3)).reshape(shape))
            stacked = stacked[:, :, width:]
    yield tuple(table.reshape((-1, table.shape[2])) for table in tables)


def pick_kernel(places, *refs):
    tables, picked, sems = refs[:-3], refs[-3:-1], refs[-1]
    copies = []
    for number in range(sum(half.shape[0] for half in picked)):
        half, entry = picked[0], number
        if number >= half.shape[0]:
            half, entry = picked[1], number - half.shape[0]
        at = 0
        for table in tables:
            width = table.shape[2]
            copies.append(
                pltpu.make_async_copy(
                    table.at[places[number]],
                    half.at[entry, :, pl.ds(at, width)],
                    sems.at[len(copies)],
                )
            )
            at += width
    for copy in copies:
        copy.start()
    for copy in copies:
        copy.wait()


def pick_rows(tables, places):
    count, rows = tables[0].shape[:2]
    columns = sum(table.shape[2] for table in tables)
    half = (count // 2, rows, columns)
    if rows % 16:
        picked = jnp.concatenate([table[places] for table in tables], axis=2)
        return picked[: count // 2], picked[count // 2 :]
    return pl.pallas_call(
        pick_kernel,
        out_shape=[jax.ShapeDtypeStruct(half, jnp.bfloat16)] * 2,
        in_specs=[pl.BlockSpec(memory_space=pltpu.SMEM)]
        + [pl.BlockSpec(memory_space=pl.ANY)] * len(tables),
        out_specs=[pl.BlockSpec(memory_space=pltpu.VMEM)] * 2,
        scratch_shapes=[pltpu.SemaphoreType.DMA((count * len(tables),))],
        compiler_params=pltpu.CompilerParams(vmem_limit_bytes=32 * 2**20),
        cost_estimate=pl.CostEstimate(
            flops=0, bytes_accessed=4 * count * rows * columns, transcendentals=0
        ),
    )(places, *tables)


def scatter_bulk(grid, tables, order):
    rows = tables[0].shape[0] // grid.count
    columns = sum(table.shape[1] for table in tables)
    places = relative_places(grid, order, True)
    tables = [table.reshape(grid.count, rows, table.shape[1]) for table in tables]
    axes = tuple(reversed(order))
    dims = tuple(grid.sizes[axis] for axis in axes) + (rows, columns)
    kept, sent = pick_rows(tables, places)
    received = yield [grid.ahead(sent, CORE, 1)]
    terms = [(kept.reshape(dims), (), 1), (received[0].reshape(dims), (), 1)]

    def total(*index):
        return sum(array[prefix + index].astype(jnp.float32) for array, prefix, _ in terms)

    for axis in axes:
        if axis == Z_AXIS:
            bit = 1
            while bit < grid.sizes[axis]:
                sent = sum(
                    array[prefix + (slice(stride, None, 2 * stride),)].astype(jnp.float32)
                    for array, prefix, stride in terms
                )
                received = yield [grid.flip(sent.astype(jnp.bfloat16), axis, bit)]
                terms = [(array, prefix, 2 * stride) for array, prefix, stride in terms]
                terms.append((received[0], (), 1))
                bit *= 2
        else:
            passing = None
            for place in range(1, grid.sizes[axis]):
                here = total(place)
                if passing is not None:
                    here = here + passing.astype(jnp.float32)
                passing = (yield [grid.ahead(here.astype(jnp.bfloat16), axis, 1)])[0]
            terms = [(array, prefix + (0,), 1) for array, prefix, _ in terms]
            terms.append((passing, (), 1))
            continue
        terms = [(array, prefix + (0,), 1) for array, prefix, _ in terms]
    yield total()


HEAD_COLS = 8 * HEAD_DIM


def head_probs(query, key):
    scores = dot_tail(query, key) * HEAD_DIM ** (-0.5)
    weights = jnp.exp(scores - jnp.max(scores, axis=-1, keepdims=True))
    return weights * (1.0 / jnp.sum(weights, axis=-1, keepdims=True))


def head_masks():
    lanes = lax.broadcasted_iota(jnp.int32, (1, 2 * HEAD_DIM), 1)
    first = lanes < HEAD_DIM
    return first, (first.astype(jnp.bfloat16), (~first).astype(jnp.bfloat16))


def attend_kernel(query_ref, key_ref, value_ref, mixed_ref):
    first, masks = head_masks()
    for at in range(0, HEAD_COLS, 2 * HEAD_DIM):
        pair = slice(at, at + 2 * HEAD_DIM)
        query, key, value = query_ref[:, pair], key_ref[:, pair], value_ref[:, pair]
        mixed = [
            matmul(head_probs(query * mask, key).astype(jnp.bfloat16), value) for mask in masks
        ]
        mixed_ref[:, pair] = jnp.where(first, mixed[0], mixed[1]).astype(jnp.bfloat16)


def attend_back_kernel(query_ref, key_ref, value_ref, grad_ref, out_ref, bias_ref):
    first, masks = head_masks()

    @pl.when(pl.program_id(1) == 0)
    def _():
        bias_ref[...] = jnp.zeros_like(bias_ref)

    for at in range(0, HEAD_COLS, 2 * HEAD_DIM):
        pair = slice(at, at + 2 * HEAD_DIM)
        query, key, value = query_ref[:, pair], key_ref[:, pair], value_ref[:, pair]
        grad = grad_ref[:, pair]
        parts = []
        for mask in masks:
            probs = head_probs(query * mask, key)
            grad_probs = dot_tail(grad * mask, value)
            inner = jnp.sum(probs * grad_probs, axis=-1, keepdims=True)
            grad_scores = (probs * (grad_probs - inner)).astype(jnp.bfloat16)
            parts.append(
                (
                    matmul(grad_scores, key) * HEAD_DIM ** (-0.5),
                    dot_head(grad_scores, query) * HEAD_DIM ** (-0.5),
                    dot_head(probs.astype(jnp.bfloat16), grad),
                )
            )
        whole = [jnp.where(first, one, two) for one, two in zip(*parts)]
        for index in range(3):
            out_ref[index, :, pair] = whole[index].astype(jnp.bfloat16)
        bias_ref[0:1, pair] += jnp.sum(whole[0], axis=0, keepdims=True)
        bias_ref[1:2, pair] += jnp.sum(whole[2], axis=0, keepdims=True)


def head_specs():
    groups = D // HEAD_COLS
    return [
        pl.BlockSpec((TOK, HEAD_COLS), lambda group, image, part=part: (image, part * groups + group))
        for part in range(3)
    ]


def attend(proj):
    count = proj.shape[0] // TOK
    flops = 4 * count * HEADS * TOK * TOK * HEAD_DIM
    return pl.pallas_call(
        attend_kernel,
        grid=(D // HEAD_COLS, count),
        out_shape=jax.ShapeDtypeStruct((proj.shape[0], D), jnp.bfloat16),
        in_specs=head_specs(),
        out_specs=pl.BlockSpec((TOK, HEAD_COLS), lambda group, image: (image, group)),
        compiler_params=pltpu.CompilerParams(vmem_limit_bytes=24 * 2**20),
        cost_estimate=pl.CostEstimate(
            flops=4 * flops, bytes_accessed=8 * proj.size, transcendentals=flops // 256
        ),
    )(proj, proj, proj)


def attend_back(proj, grad_mixed):
    count = proj.shape[0] // TOK
    flops = 12 * count * HEADS * TOK * TOK * HEAD_DIM
    block = pl.BlockSpec((TOK, HEAD_COLS), lambda group, image: (image, group))
    return pl.pallas_call(
        attend_back_kernel,
        grid=(D // HEAD_COLS, count),
        out_shape=[
            jax.ShapeDtypeStruct((3, proj.shape[0], D), jnp.bfloat16),
            jax.ShapeDtypeStruct((8, D), jnp.float32),
        ],
        in_specs=head_specs() + [block],
        out_specs=[
            pl.BlockSpec((3, TOK, HEAD_COLS), lambda group, image: (0, image, group)),
            pl.BlockSpec((8, HEAD_COLS), lambda group, image: (0, group)),
        ],
        compiler_params=pltpu.CompilerParams(vmem_limit_bytes=24 * 2**20),
        cost_estimate=pl.CostEstimate(
            flops=3 * flops, bytes_accessed=16 * proj.size, transcendentals=flops // 512
        ),
    )(proj, proj, proj, grad_mixed)


ORDER = (Z_AXIS, MIX_P, MIX_Q)


def per_device(
    latents,
    noise_draw,
    timesteps,
    labels,
    weights_in,
    weights_down,
    weights_side,
    biases,
    first_in,
    first_down,
    first_side,
    first_bias,
    second_in,
    second_down,
    second_side,
    second_bias,
):
    bf16 = jnp.bfloat16
    count_all = lax.axis_size(AXIS)
    grid = Grid(count_all)
    sizes = grid.shape
    count = latents.shape[0]
    rows_all = count * TOK
    image_total = count * count_all
    rows = weights_in.shape[0]
    bias_rows = biases.shape[0]
    my_rows = lax.axis_index(AXIS) * rows
    masters = (weights_in, weights_down, weights_side, biases)
    in_bf = weights_in.astype(bf16)
    down_bf = weights_down.astype(bf16)
    side_bf = weights_side.astype(bf16)
    t_first = side_bf[:, :TFREQ]
    patch_at = TFREQ
    class_at = TFREQ + PATCH_FEAT
    head_at = class_at + CLASSES
    w_class = side_bf[:, class_at:head_at]
    w_mods = in_bf[:, 4 * D + FF : 12 * D + FF]
    w_time = in_bf[:, 12 * D + FF :]

    numbers = jnp.concatenate([timesteps, labels])
    packed = jnp.concatenate(
        [
            biases.astype(bf16),
            side_bf[:, patch_at:class_at].reshape(-1),
            side_bf[:, head_at:].reshape(-1),
            (numbers // 32).astype(bf16),
            (numbers % 32).astype(bf16),
        ]
    )
    width = packed.shape[0]
    tall = -(-width // (SMALL_ROWS * 128)) * SMALL_ROWS
    packed = jnp.pad(packed, (0, tall * 128 - width)).reshape(tall, 128)
    main_bf = weights_in[:, : 4 * D + FF].astype(bf16)
    table_main = lax.all_gather(main_bf, AXIS, axis=0, tiled=True)
    get = Flow(gather_bulk(grid, [down_bf], ORDER))
    spread_all = gather_small(grid, packed, (CORE, X_AXIS, Y_AXIS))
    spread_all = gather_small(grid, meet(spread_all, get), (Z_AXIS,))
    spread_all = spread_all.reshape(count_all, tall * 128)
    bias_full = spread_all[:, :bias_rows].reshape(-1).astype(jnp.float32)
    at = bias_rows
    w_patch = spread_all[:, at : at + rows * PATCH_FEAT].reshape(D, PATCH_FEAT)
    at += rows * PATCH_FEAT
    w_head = spread_all[:, at : at + rows * PATCH_FEAT].reshape(D, PATCH_FEAT)
    at += rows * PATCH_FEAT
    numbers = spread_all[:, at : at + 4 * count].astype(jnp.float32)
    numbers = numbers[:, : 2 * count] * 32.0 + numbers[:, 2 * count :]
    numbers = numbers.reshape(sizes + (2 * count,))
    numbers = jnp.stack(
        [numbers[:, :, :, core].transpose((1, 2, 0, 3) if core else (2, 1, 0, 3)) for core in range(sizes[CORE])]
    ).reshape(count_all, 2 * count)
    steps_all = numbers[:, :count].reshape(image_total)
    labels_all = numbers[:, count:].reshape(image_total).astype(jnp.int32)

    b_qkv = jnp.concatenate([bias_full[:D], jnp.zeros((D,), jnp.float32), bias_full[D : 2 * D]])
    b_out = bias_full[2 * D : 3 * D]
    b_up = bias_full[3 * D : 3 * D + FF]
    b_down = bias_full[3 * D + FF : 4 * D + FF]
    b_mods = bias_full[4 * D + FF : 12 * D + FF]
    b_tfirst = lax.dynamic_slice_in_dim(bias_full[12 * D + FF : 13 * D + FF], my_rows, rows)
    b_time = lax.dynamic_slice_in_dim(bias_full[13 * D + FF : 14 * D + FF], my_rows, rows)
    b_patch = bias_full[14 * D + FF :]

    feats = time_features(steps_all).astype(bf16)
    time_pre = dot_tail(t_first, feats) + b_tfirst[:, None]
    time_act = jax.nn.silu(time_pre).astype(bf16)
    onehot = labels_all[:, None] == jnp.arange(CLASSES, dtype=jnp.int32)[None, :]
    cond_part = lax.dot_general(
        w_time, time_act, (((0,), (0,)), ((), ())), preferred_element_type=jnp.float32
    )
    cond = cond_part.reshape(sizes + (rows, image_total))
    cond = scatter_axis(grid, scatter_axis(grid, cond, CORE, CORE), X_AXIS, X_AXIS)
    cond = scatter_axis(grid, meet(cond, get), Y_AXIS, Y_AXIS)
    cond = scatter_axis(grid, cond, Z_AXIS, Z_AXIS)
    cond = cond + b_time[:, None] + dot_tail(w_class, onehot.astype(bf16))
    cond_act = jax.nn.silu(cond).astype(bf16)

    def own_columns(part):
        wide = jnp.zeros((image_total, D), jnp.float32)
        return lax.dynamic_update_slice(wide, part.T, (0, my_rows))

    mods = jnp.concatenate(
        [dot_head(cond_act, w_mods), own_columns(cond), own_columns(time_pre)], axis=1
    )
    mods = mods.reshape(sizes[CORE], sizes[X_AXIS], sizes[Y_AXIS], sizes[Z_AXIS] * count, 10 * D)
    mods = meet(scatter_axis(grid, mods, CORE, 0), get)
    mods = scatter_axis(grid, mods, MIX_P, 0, bf16)
    mods = scatter_axis(grid, mods, MIX_Q, 0)
    mods = mods.reshape(sizes[Z_AXIS], count * 10 * D // 128, 128)
    total = lax.dynamic_index_in_dim(mods, grid.coords[Z_AXIS], 0, keepdims=False)
    for shift in range(1, sizes[Z_AXIS]):
        part = lax.dynamic_index_in_dim(mods, grid.place(Z_AXIS, -shift), 0, keepdims=False)
        total = total + grid.ahead(part, Z_AXIS, shift)
    mods = meet(total.reshape(count, 10 * D), get)
    cond_own, time_own = mods[:, 8 * D : 9 * D], mods[:, 9 * D :]
    mods = mods[:, : 8 * D] + b_mods
    shift_a, scale_a, gate_a, shift_b, scale_b, gate_b, shift_f, scale_f = jnp.split(
        mods, 8, axis=1
    )

    w_qkv, w_out = table_main[:, : 3 * D], table_main[:, 3 * D : 4 * D]
    table_up = table_main[:, 4 * D :]

    signal, spread = noise_scales(timesteps)
    noise_rows = noise_draw.astype(jnp.float32)
    noisy = signal[:, None, None] * latents.astype(jnp.float32) + spread[:, None, None] * noise_rows
    noisy = noisy.astype(bf16).reshape(rows_all, PATCH_FEAT)
    hidden = dot_tail(noisy, w_patch) + b_patch + jnp.tile(positions(), (count, 1))
    resid_in = hidden.reshape(count, TOK, D)
    normed_a = modulate(resid_in, shift_a, scale_a).astype(bf16).reshape(rows_all, D)
    proj = (matmul(normed_a, w_qkv) + b_qkv).astype(bf16)
    mixed = meet(attend(proj), get)
    tail_bf = after(in_bf[:, 4 * D + FF :], mods)
    table_cond = lax.all_gather(tail_bf, AXIS, axis=0, tiled=True)
    attended = (matmul(mixed, w_out) + b_out).reshape(count, TOK, D)
    resid_mid = resid_in + gate_a[:, None, :] * attended
    normed_b = modulate(resid_mid, shift_b, scale_b).astype(bf16).reshape(rows_all, D)
    normed_b = meet(normed_b, get)
    (table_down,) = last(get)
    upper = matmul(normed_b, table_up) + b_up
    active, pull_gelu = jax.vjp(partial(jax.nn.gelu, approximate=True), upper)
    slope = pull_gelu(jnp.ones_like(upper))[0]
    active, slope = lax.optimization_barrier((active.astype(bf16), slope))
    lowered = matmul(active, table_down) + b_down
    lowered = lowered.reshape(count, TOK, D)
    resid_out = resid_mid + gate_b[:, None, :] * lowered
    normed_c = modulate(resid_out, shift_f, scale_f).astype(bf16).reshape(rows_all, D)
    predicted = matmul(normed_c, w_head)
    error = predicted - noise_rows.reshape(rows_all, PATCH_FEAT)
    loss_local = jnp.sum(error * error)
    grad_pred = (2.0 / image_total * error).astype(bf16)

    grad_head = dot_head(normed_c, grad_pred)
    grad_normed_c = dot_tail(grad_pred, w_head).reshape(count, TOK, D)
    _, pull_final = jax.vjp(modulate, resid_out, shift_f, scale_f)
    grad_out, grad_shift_f, grad_scale_f = pull_final(grad_normed_c)
    grad_gate_b = jnp.sum(grad_out * lowered, axis=1)
    grad_lowered = (grad_out * gate_b[:, None, :]).reshape(rows_all, D)
    grad_b_down = jnp.sum(grad_lowered, axis=0)
    lowered_bf = grad_lowered.astype(bf16)
    grad_w_down = dot_head(active, lowered_bf).astype(bf16)
    put_down = Flow(scatter_bulk(grid, [grad_w_down], ORDER))
    lowered_bf = after(lowered_bf, grad_w_down)
    grad_active = dot_tail(lowered_bf, table_down)
    grad_upper = grad_active * slope
    grad_b_up = jnp.sum(grad_upper, axis=0)
    upper_bf = grad_upper.astype(bf16)
    upper_bf = meet(upper_bf, put_down)
    grad_w_up = dot_head(normed_b, upper_bf).astype(bf16)
    put_up = Flow(scatter_bulk(grid, [grad_w_up], ORDER))
    upper_bf = after(upper_bf, grad_w_up)
    grad_normed_b = dot_tail(upper_bf, table_up).reshape(count, TOK, D)
    grad_normed_b = meet(grad_normed_b, put_down)
    _, pull_mid = jax.vjp(modulate, resid_mid, shift_b, scale_b)
    grad_mid_norm, grad_shift_b, grad_scale_b = pull_mid(grad_normed_b)
    grad_mid = grad_out + grad_mid_norm
    grad_gate_a = jnp.sum(grad_mid * attended, axis=1)
    grad_attended = (grad_mid * gate_a[:, None, :]).reshape(rows_all, D)
    grad_b_out = jnp.sum(grad_attended, axis=0)
    attended_bf = grad_attended.astype(bf16)
    grad_w_out = dot_head(mixed, attended_bf).astype(bf16)
    grad_mixed = dot_tail(attended_bf, w_out).astype(bf16)
    grad_mixed = meet(grad_mixed, put_down, put_up)
    proj_bf, proj_sums = attend_back(proj, grad_mixed)
    grad_b_query, grad_b_value = proj_sums[0], proj_sums[1]
    proj_bf = meet(proj_bf, put_down, put_up)
    grad_qkv = [dot_head(normed_a, proj_bf[part]).astype(bf16) for part in range(3)]
    grad_qkv[0] = meet(grad_qkv[0], put_down, put_up)
    put_rest = Flow(scatter_bulk(grid, grad_qkv + [grad_w_out], ORDER))
    proj_bf = after(proj_bf, *grad_qkv)
    grad_normed_a = sum(
        dot_tail(proj_bf[part], w_qkv[:, part * D : (part + 1) * D]) for part in range(3)
    ).reshape(count, TOK, D)
    grad_normed_a = meet(grad_normed_a, put_up, put_rest)
    _, pull_first = jax.vjp(modulate, resid_in, shift_a, scale_a)
    grad_in_norm, grad_shift_a, grad_scale_a = pull_first(grad_normed_a)
    grad_hidden = (grad_mid + grad_in_norm).reshape(rows_all, D)
    grad_b_patch = jnp.sum(grad_hidden, axis=0)
    grad_w_patch = dot_head(grad_hidden.astype(bf16), noisy)

    mods_bf = beside(
        [
            grad_shift_a,
            grad_scale_a,
            grad_gate_a,
            grad_shift_b,
            grad_scale_b,
            grad_gate_b,
            grad_shift_f,
            grad_scale_f,
        ]
    )
    grad_cond = jax.vjp(jax.nn.silu, cond_own)[1](dot_tail(mods_bf, table_cond[:, : 8 * D]))[0]
    cond_bf = grad_cond.astype(bf16)
    grad_time_act = dot_tail(cond_bf, table_cond[:, 8 * D :])
    grad_time_pre = jax.vjp(jax.nn.silu, time_own)[1](grad_time_act)[0]
    image_grads = beside([mods_bf, grad_time_pre, grad_cond])
    image_grads = meet(image_grads, put_up, put_rest).reshape(-1, 128)
    grad_bias = jnp.concatenate(
        [
            grad_b_query,
            grad_b_value,
            grad_b_out,
            grad_b_up,
            grad_b_down,
            jnp.zeros((10 * D,), jnp.float32),
            grad_b_patch,
        ]
    )
    small = jnp.concatenate(
        [
            grad_bias.reshape(count_all, bias_rows),
            grad_w_patch.reshape(count_all, rows * PATCH_FEAT),
            grad_head.reshape(count_all, rows * PATCH_FEAT),
        ],
        axis=1,
    )
    tall = -(-small.shape[1] // 2048) * SMALL_ROWS
    small = jnp.pad(small, ((0, 0), (0, tall * 128 - small.shape[1])))
    small = small.reshape(sizes + (tall, 128))
    ready = {axis: (put_rest,) for axis in (Z_AXIS, MIX_P, CORE)}
    image_grads, small = gather_and_scatter(grid, image_grads, small, ready)
    small = small.reshape(-1)
    image_grads = image_grads.reshape(image_total, 10 * D)
    mods_bf, cond_bf = image_grads[:, : 8 * D], image_grads[:, 9 * D :]
    grad_w_mods = matmul(cond_act, mods_bf)
    grad_w_time = matmul(time_act, cond_bf)
    grad_w_class = lax.dot_general(
        lax.dynamic_slice_in_dim(cond_bf, my_rows, rows, 1).astype(jnp.float32),
        onehot.astype(jnp.float32),
        (((0,), (0,)), ((), ())),
        precision=lax.Precision.HIGHEST,
        preferred_element_type=jnp.float32,
    )
    own_pre = lax.dynamic_slice_in_dim(image_grads, 8 * D + my_rows, rows, 1)
    grad_t_first = dot_head(own_pre, feats)
    sums = jnp.sum(image_grads.astype(jnp.float32), axis=0)
    known = jnp.pad(sums, (4 * D + FF, D))
    known = lax.dynamic_slice_in_dim(known, lax.axis_index(AXIS) * bias_rows, bias_rows)
    at = bias_rows
    sum_patch = small[at : at + rows * PATCH_FEAT].reshape(rows, PATCH_FEAT)
    at += rows * PATCH_FEAT
    sum_head = small[at : at + rows * PATCH_FEAT].reshape(rows, PATCH_FEAT)

    sum_rest, sum_up, sum_down = last(put_rest), last(put_up), last(put_down)
    grads_in = (sum_rest, sum_up, grad_w_mods, grad_w_time)
    grads_other = (
        sum_down,
        jnp.concatenate([grad_t_first, sum_patch, grad_w_class, sum_head], axis=1),
        (small[:bias_rows] + known)[None],
    )
    masters = (weights_in, weights_down, weights_side, biases[None])
    firsts = (first_in, first_down, first_side, first_bias[None])
    seconds = (second_in, second_down, second_side, second_bias[None])
    shapes = [master.shape for master in masters]
    results = directions(masters, firsts, seconds, grads_in, grads_other)
    loss_spot = jnp.arange(8, dtype=jnp.int32)[:, None] == 3
    sums = sum_small(grid, results[12] + jnp.where(loss_spot, loss_local, 0.0))
    updated = updates(sums, masters, results[8:12])
    norms = updated[4]
    return (
        sums[3, 0],
        updated[0],
        updated[1],
        updated[2],
        updated[3][0],
        results[0],
        results[1],
        results[2],
        results[3][0],
        results[4],
        results[5],
        results[6],
        results[7][0],
        norms[2, :12],
        norms[0, :12],
        norms[1, :12],
    )


def solution(mesh):
    placed = (
        P("fsdp", None, None),
        P("fsdp", None, None),
        P("fsdp"),
        P("fsdp"),
        P("fsdp", None),
        P("fsdp", None),
        P("fsdp", None),
        P("fsdp"),
        P("fsdp", None),
        P("fsdp", None),
        P("fsdp", None),
        P("fsdp"),
        P("fsdp", None),
        P("fsdp", None),
        P("fsdp", None),
        P("fsdp"),
    )
    return jax.shard_map(
        per_device,
        mesh=mesh,
        in_specs=placed,
        out_specs=(
            P(),
            P("fsdp", None),
            P("fsdp", None),
            P("fsdp", None),
            P("fsdp"),
            P("fsdp", None),
            P("fsdp", None),
            P("fsdp", None),
            P("fsdp"),
            P("fsdp", None),
            P("fsdp", None),
            P("fsdp", None),
            P("fsdp"),
            P(),
            P(),
            P(),
        ),
        check_vma=False,
    )
```
